32 devices in a mesh: pairs: 2 (over y), gx: 4 (over z), gy: 2 (over x), gz: 2 (over core).
Axes of the slice: x: 2, y: 2, z: 4, core: 2. Of those that a mesh axis runs over, the one named last changes fastest.
Arguments:
- sections: bfloat16 [2, 2048, 2048], P('gz', ('pairs', 'gy'), 'gx'), parts along dimension 1, may hold values from -16 to 16
- fine_offsets: int32 [4], P('pairs'), parts along dimension 0, may hold values from 0 to 31
- coarse_offset: int32 [2], P('pairs'), parts along dimension 0, may hold values from 0 to 63
- tissue_mask: int32 [64, 64], P(('pairs', 'gy'), 'gx'), parts along dimension 0, may hold values 0 or 1
Outputs:
- flow: float32 [2, 2, 64, 32], P(None, 'gz', ('pairs', 'gy'), 'gx'), parts along dimension 2
The draws below stay inside these ranges and needn't reach their ends.
There are 2 independent parts, one for each index of `pairs`. The reference program is written for one: setup_inputs(seed, part) draws one part's arguments, and reference() takes and returns one part's arrays. A program takes and returns all parts, laid end to end along the dimension named above; each array names one. Nothing has to cross between parts.
All inputs are finite; a program needn't handle non-finite values. No bound on the sum of `tissue_mask` on one device may be relied on, other than what follows from the above.
Results may differ from the reference program's by a relative error of at most 0.00075.
Values may be sent and summed in bfloat16 or wider, within the bound.
No kernel may reach another device: no remote copies, remote signals or barrier semaphores. Data moves between devices by JAX's collectives and lax.ppermute only.
A program may use at most 64 MiB of HBM per device.

```python
import jax
import jax.numpy as jnp
from jax import lax

P_SIZE = 64
STRIDE = 32
DOWN = 8
TY = 512
TX = 512
NY = 1024
NX = 2048
FR = 16
FC = 16
NCR = 1
NCC = 4
N_GX = 4
N_GY = 2


def roll_rows(column_block, amount):
    return jnp.roll(column_block, amount, axis=0)


def roll_columns(row_block, amount):
    return jnp.roll(row_block, amount, axis=1)


def draw_sections(key, part):
    random_seedlings = jax.random.split(jax.random.fold_in(key, 7), 6)
    texture = jax.random.normal(random_seedlings[0], (NY, NX), jnp.float32)
    down_moves = jax.random.randint(random_seedlings[3], (NX // TX,), -(3 * P_SIZE // 2), 3 * P_SIZE // 2 + 1)
    side_moves = jax.random.randint(random_seedlings[4], (NY // TY,), -(3 * P_SIZE // 2), 3 * P_SIZE // 2 + 1)
    shifted = jax.vmap(roll_rows, in_axes=(1, 0), out_axes=1)(texture.reshape(NY, NX // TX, TX), down_moves).reshape(NY, NX)
    shifted = jax.vmap(roll_columns, in_axes=(0, 0), out_axes=0)(shifted.reshape(NY // TY, TY, NX), side_moves).reshape(NY, NX)
    noise_field = jax.random.normal(random_seedlings[5], (NY, NX), jnp.float32)
    second = 0.8 * shifted + 0.6 * noise_field
    return jnp.clip(jnp.stack([texture, second]), -16.0, 16.0).astype(jnp.bfloat16)


def plant(values, own_key, smallest, high):
    place = [jax.random.randint(jax.random.fold_in(own_key, axis), (), 0, length) for axis, length in enumerate(values.shape)]
    longest = values.shape.index(max(values.shape))
    neighbour = place[:longest] + [(place[longest] + 1) % values.shape[longest]] + place[longest + 1:]
    return values.at[tuple(place)].set(smallest).at[tuple(neighbour)].set(high)


def setup_inputs(seed: int = 0, part: int = 0) -> dict:
    splits = jax.random.split(jax.random.key(seed), 5)
    part_keys = jax.random.split(jax.random.fold_in(splits[4], part), 5)
    sections = draw_sections(jax.random.fold_in(jax.random.fold_in(splits[4], part), 71), part)
    fine_offsets = jax.random.randint(part_keys[1], (2,), 0, STRIDE).astype(jnp.int32)
    coarse_offset = jax.random.randint(part_keys[2], (1,), 0, P_SIZE).astype(jnp.int32)
    tissue_mask = plant((jax.random.randint(part_keys[3], (FR * N_GY, FC * N_GX), 0, 4) < 3).astype(jnp.int32), jax.random.fold_in(part_keys[3], 1), 0, 1)
    return {"sections": sections, "fine_offsets": fine_offsets, "coarse_offset": coarse_offset, "tissue_mask": tissue_mask}


sharpness_divisor = 12.0


def peak_offsets(first_patch, second_patch, prior_shift):
    square_edge_pixels = first_patch.shape[-1]
    number_squares = first_patch.shape[0]
    first_spec = jnp.fft.fft2(first_patch)
    second_spec = jnp.fft.fft2(second_patch)
    signed = ((jnp.arange(square_edge_pixels) + square_edge_pixels // 2) % square_edge_pixels - square_edge_pixels // 2).astype(first_patch.dtype)
    phases = 2.0 * jnp.pi * (signed[None, :, None] * prior_shift[0][:, None, None] + signed[None, None, :] * prior_shift[1][:, None, None]) / square_edge_pixels
    spectrum = second_spec * jnp.conj(first_spec) * (jnp.cos(phases) + 1j * jnp.sin(phases))
    match_landscape = jnp.real(jnp.fft.ifft2(spectrum))
    maximum_response = (sharpness_divisor / (square_edge_pixels * square_edge_pixels)) * match_landscape.reshape(number_squares, square_edge_pixels * square_edge_pixels)
    weights = jax.nn.softmax(maximum_response, axis=-1).reshape(number_squares, square_edge_pixels, square_edge_pixels)
    along_rows = jnp.sum(weights * signed[None, :, None], axis=(1, 2))
    along_columns = jnp.sum(weights * signed[None, None, :], axis=(1, 2))
    return jnp.stack([along_rows, along_columns])


def reference(sections, fine_offsets, coarse_offset, tissue_mask):
    pixels = sections.astype(jnp.float32)
    summed = pixels.reshape(2, NY // DOWN, DOWN, NX // DOWN, DOWN).sum(axis=(2, 4)) / DOWN
    coarse = lax.optimization_barrier(summed.astype(jnp.bfloat16)).astype(jnp.float32)
    coarse_rows = NCR * N_GY
    widened = jnp.pad(coarse, ((0, 0), (0, 0), (0, P_SIZE)))
    window = lax.dynamic_slice_in_dim(widened, coarse_offset[0].astype(jnp.int32), NCC * P_SIZE, 2)
    coarse_patches = window.reshape(2, coarse_rows, P_SIZE, NCC, P_SIZE).transpose(0, 1, 3, 2, 4).reshape(2, coarse_rows * NCC, P_SIZE, P_SIZE)
    coarse_flow = peak_offsets(coarse_patches[0], coarse_patches[1], jnp.zeros((2, coarse_rows * NCC), jnp.float32))
    coarse_flow = coarse_flow.reshape(2, coarse_rows, NCC)
    blended_flow = 0.5 * (coarse_flow + jnp.mean(coarse_flow, axis=2, keepdims=True))
    padded = jnp.pad(sections, ((0, 0), (0, P_SIZE), (0, P_SIZE)))
    row_offset = fine_offsets[0].astype(jnp.int32)
    column_offset = fine_offsets[1].astype(jnp.int32)
    columns = jnp.arange(FC * N_GX, dtype=jnp.int32)
    centre_column = columns * STRIDE + column_offset + P_SIZE // 2
    column_pick = jnp.clip((centre_column // DOWN - coarse_offset[0]) // P_SIZE, 0, NCC - 1)

    def one_row(row_index):
        zero_index = jnp.zeros((), jnp.int32)
        beginning_line = (row_offset + STRIDE * row_index).astype(jnp.int32)
        band_rows = lax.dynamic_slice(padded, (zero_index, beginning_line, column_offset), (2, P_SIZE, NX + STRIDE)).astype(jnp.float32)
        pieces = band_rows.reshape(2, P_SIZE, FC * N_GX + 1, STRIDE)
        patches = jnp.concatenate([pieces[:, :, :-1, :], pieces[:, :, 1:, :]], axis=3).transpose(0, 2, 1, 3)
        local_centre = (row_index % FR) * STRIDE + row_offset + P_SIZE // 2
        row_pick = jnp.minimum(local_centre // (DOWN * P_SIZE), NCR - 1) + (row_index // FR) * NCR
        prior_flow = DOWN * blended_flow[:, row_pick, :][:, column_pick]
        found_flow = peak_offsets(patches[0], patches[1], prior_flow)
        return prior_flow + tissue_mask[row_index].astype(jnp.float32)[None, :] * found_flow

    patch_flow = lax.map(one_row, jnp.arange(FR * N_GY, dtype=jnp.int32)).transpose(1, 0, 2)
    paired = patch_flow.reshape(2, FR * N_GY, FC * N_GX // 2, 2)
    parity = jnp.arange(FR * N_GY) % 2
    layers = [jnp.where(((parity + section_side) % 2 == 0)[None, :, None], paired[..., 0], paired[..., 1]) for section_side in range(2)]
    return jnp.stack(layers, axis=1)
```

```python
import math

import jax
import jax.numpy as jnp
import numpy as np
from jax import lax
from jax.experimental import pallas as pl
from jax.experimental.pallas import tpu as pltpu
from jax.sharding import PartitionSpec as P

P_SIZE = 64
HALF = P_SIZE // 2
STRIDE = 32
DOWN = 8
LANES = 128
GROUP = LANES // HALF
SHARPNESS = 12.0
SCALE = SHARPNESS / float(P_SIZE) ** 4 * math.log2(math.e)

f32 = jnp.float32
bf16 = jnp.bfloat16


def basis_table():
    y = np.arange(P_SIZE)
    k = np.arange(HALF)
    angle = 2.0 * np.pi * (k[:, None] * y[None, :] % P_SIZE) / P_SIZE
    sines = np.sin(angle)
    sines[0] = np.cos(np.pi * y)
    return np.stack([np.cos(angle), sines])


def split_table(table):
    high = table.astype(jnp.bfloat16)
    low = (table - high.astype(np.float64)).astype(jnp.bfloat16)
    return high, low


def forward_columns_table():
    table = basis_table()
    halves = []
    for order in ((0, 1), (1, 0)):
        out = np.zeros((2, P_SIZE, 2, 2, HALF))
        for place, kind in enumerate(order):
            for patch in range(2):
                out[patch, :, place, patch, :] = table[kind].T
        halves.append(out.reshape(2 * P_SIZE, LANES))
    high_even, low_even = split_table(halves[0])
    high_odd, low_odd = split_table(halves[1])
    return np.concatenate([high_even, low_even, high_odd, low_odd], axis=1)


def inverse_columns_table():
    table = basis_table()
    out = np.zeros((2, GROUP, HALF, GROUP, P_SIZE))
    for patch in range(GROUP):
        out[:, patch, :, patch, :] = table
    return np.concatenate(split_table(out.reshape(2 * LANES, GROUP * P_SIZE)), axis=1)


def stacked_table(matrix):
    high, low = split_table(matrix)
    return np.block([[high, high], [low, np.zeros_like(low)]])


def forward_rows_table():
    return stacked_table(basis_table().reshape(P_SIZE, P_SIZE))


def inverse_rows_table():
    return stacked_table(basis_table().reshape(P_SIZE, P_SIZE).T)


def cosine_of_turns(turns):
    square = (turns * (2.0 * math.pi)) ** 2
    total = jnp.full_like(square, 1.0 / math.factorial(20))
    for n in range(9, -1, -1):
        total = total * square + (-1.0) ** n / math.factorial(2 * n)
    return total


def sine_of_turns(turns):
    angle = turns * (2.0 * math.pi)
    square = angle * angle
    total = jnp.full_like(square, -1.0 / math.factorial(19))
    for n in range(8, -1, -1):
        total = total * square + (-1.0) ** n / math.factorial(2 * n + 1)
    return total * angle


def nearest(turns):
    return turns - jnp.round(turns)


def basis_values(frequency, kind, place):
    nyquist = (kind == 1) & (frequency == 0)
    number = jnp.where(nyquist, HALF, frequency)
    quarter = jnp.where((kind == 1) & (frequency != 0), P_SIZE // 4, 0)
    step = (number * place - quarter) & (P_SIZE - 1)
    step = jnp.where(step > HALF, P_SIZE - step, step)
    flip = step > P_SIZE // 4
    step = jnp.where(flip, HALF - step, step)
    square = (step.astype(f32) * (2.0 * math.pi / P_SIZE)) ** 2
    total = jnp.full_like(square, 1.0 / math.factorial(12))
    for n in range(5, -1, -1):
        total = total * square + (-1.0) ** n / math.factorial(2 * n)
    return jnp.where(flip, -total, total)


def iota(shape, axis):
    return lax.broadcasted_iota(jnp.int32, shape, axis)


def split(values):
    high = values.astype(bf16)
    return high, (values - high.astype(f32)).astype(bf16)


def matmul(left, right):
    return jnp.dot(left, right, preferred_element_type=f32)


def add_row_halves(values):
    half = values.shape[0] // 2
    return values[:half] + values[half:]


def first_lane(shape):
    return iota(shape, 1) % HALF == 0


def half_spectra(cc, cs, sc, ss, first):
    shape = cc.shape
    l0 = first_lane(shape)
    if not first:
        return (
            cc - jnp.where(l0, 0.0, ss),
            sc + jnp.where(l0, 0.0, cs),
            jnp.where(l0, cs, cc + ss),
            jnp.where(l0, ss, sc - cs),
        )
    r0 = iota(shape, 0) == 0
    either = l0 | r0
    return (
        cc - jnp.where(either, 0.0, ss),
        jnp.where(r0, 0.0, sc) + jnp.where(l0, 0.0, cs),
        jnp.where(l0, cs, jnp.where(r0, sc, cc + ss)),
        jnp.where(either, ss, sc - cs),
    )


def cross_spectra(own, other, sign, first):
    a = half_spectra(*own, first)
    b = half_spectra(*other, first)
    out = []
    for r, i in ((0, 1), (2, 3)):
        out.append(b[r] * a[r] + b[i] * a[i])
        out.append(sign * (b[r] * a[i] - b[i] * a[r]))
    if first:
        shape = own[0].shape
        corner = first_lane(shape) & (iota(shape, 0) == 0)
        out = [jnp.where(corner, x * y, o) for x, y, o in zip(own, other, out)]
    return out


def coefficients(g, t, first):
    gpr, gpi, gmr, gmi = g
    tpr, tpi, tmr, tmi = t
    shape = gpr.shape
    l0 = first_lane(shape)
    hpr = gpr * tpr - gpi * tpi
    hpi = gpr * tpi + gpi * tpr
    hmr = gmr * tmr - gmi * tmi
    hmi = gmr * tmi + gmi * tmr
    if not first:
        return (
            hpr + jnp.where(l0, 0.0, hmr),
            jnp.where(l0, hmr, hmi - hpi),
            -hpi - jnp.where(l0, 0.0, hmi),
            jnp.where(l0, -hmi, hmr - hpr),
        )
    r0 = iota(shape, 0) == 0
    either = l0 | r0
    corner = l0 & r0
    out = (
        hpr + jnp.where(either, 0.0, hmr),
        jnp.where(l0, hmr, jnp.where(r0, 0.0, hmi) - hpi),
        jnp.where(r0, hmr, -hpi - jnp.where(l0, 0.0, hmi)),
        jnp.where(either, -hmi, hmr - hpr),
    )
    return [jnp.where(corner, x * y, o) for x, y, o in zip(g, t, out)]


def signed(number):
    return jnp.where(number >= HALF, number - P_SIZE, number).astype(f32)


def column_sums(logits):
    largest = jnp.max(logits, axis=0, keepdims=True)
    weights = jnp.exp2(logits - largest)
    rows = signed(iota((P_SIZE, 1), 0))
    return largest, jnp.sum(weights, axis=0, keepdims=True), jnp.sum(weights * rows, axis=0, keepdims=True)


def patch_peak(largest, total, moment, patch):
    window = slice(patch * P_SIZE, (patch + 1) * P_SIZE)
    top = largest[:, window]
    peak = jnp.max(top, axis=1, keepdims=True)
    factor = jnp.exp2(top - peak)
    weight = factor * total[:, window]
    columns = signed(iota((1, P_SIZE), 1))
    bottom = jnp.sum(weight, axis=1, keepdims=True)
    along_rows = jnp.sum(factor * moment[:, window], axis=1, keepdims=True)
    along_columns = jnp.sum(weight * columns, axis=1, keepdims=True)
    return along_rows / bottom, along_columns / bottom


ROW_PARTS = ((0, 8, True), (8, HALF, False))


def quads(block, group):
    lane = group * 2 * LANES
    top, bottom = block[:HALF], block[HALF:]
    return (
        top[:, lane : lane + LANES],
        top[:, lane + LANES : lane + 2 * LANES],
        bottom[:, lane : lane + LANES],
        bottom[:, lane + LANES : lane + 2 * LANES],
    )


def shrink_kernel(tile_ref, out_ref):
    rows, width = tile_ref.shape
    columns = width // DOWN
    pick = (iota((width, columns), 0) // DOWN == iota((width, columns), 1)).astype(bf16)
    sums = matmul(tile_ref[...], pick)
    out_ref[...] = (jnp.sum(sums.reshape(rows // DOWN, DOWN, columns), axis=1) / DOWN).astype(bf16)


def forward_kernel(
    offsets_ref,
    columns_ref,
    own_ref,
    own_low_ref,
    own_right_ref,
    other_ref,
    other_low_ref,
    other_right_ref,
    out_ref,
    image,
    weights,
    stacked,
):
    rows, width = own_ref.shape
    tall = rows + P_SIZE
    blocks = tall // STRIDE
    supers = width // (GROUP * P_SIZE)
    side = lax.axis_index("gz")
    row_offset = offsets_ref[0]
    column_offset = offsets_ref[1]
    for s, (main, low, right) in enumerate(
        ((own_ref, own_low_ref, own_right_ref), (other_ref, other_low_ref, other_right_ref))
    ):
        image[s, :rows, :width] = main[...]
        image[s, rows:, :width] = low[...]
        image[s, :, width:] = jnp.zeros((tall, LANES), bf16)
        image[s, :, width : width + P_SIZE] = right[...]
    padded = jnp.concatenate(
        [columns_ref[...].astype(f32), jnp.zeros((2 * P_SIZE, 4 * LANES), f32)], axis=0
    )
    for t in range(2):
        shift = column_offset + STRIDE * ((t + side) % 2)
        weights[t] = pltpu.roll(padded, shift, axis=0).astype(bf16)
    left = iota((tall, LANES), 1) < P_SIZE
    for s in range(2):
        for t in range(2):
            for g in range(supers):
                lane = g * 2 * LANES
                a = matmul(image[s, :, lane : lane + 2 * LANES], weights[t, :, : 2 * LANES])
                b = matmul(image[s, :, lane + LANES : lane + 3 * LANES], weights[t, :, 2 * LANES :])
                a = a[:, :LANES] + a[:, LANES:]
                b = b[:, :LANES] + b[:, LANES:]
                for part, value in enumerate(
                    (jnp.where(left, a, b), pltpu.roll(jnp.where(left, b, a), P_SIZE, axis=1))
                ):
                    high, low = split(value)
                    at = slice(lane + part * LANES, lane + (part + 1) * LANES)
                    for n in range(blocks):
                        block = slice(n * STRIDE, (n + 1) * STRIDE)
                        stacked[s, t, 2 * n * STRIDE : (2 * n + 1) * STRIDE, at] = high[block]
                        stacked[s, t, (2 * n + 1) * STRIDE : (2 * n + 2) * STRIDE, at] = low[block]
    shape = (P_SIZE, 6 * STRIDE)
    number = iota(shape, 0)
    lane = iota(shape, 1)
    place = lane // P_SIZE * STRIDE + lane % STRIDE - row_offset
    values = jnp.where(
        (place >= 0) & (place < P_SIZE), basis_values(number % HALF, number // HALF, place), 0.0
    )
    high, low = split(values)
    is_low = lane % P_SIZE >= STRIDE
    left_rows = jnp.concatenate([high, jnp.where(is_low, 0.0, low.astype(f32)).astype(bf16)], axis=0)
    sign = jnp.where(side == 0, 1.0, -1.0).astype(f32)
    for i in range(rows // STRIDE):
        spectra = []
        for s in range(2):
            window = stacked[s, i % 2, 2 * STRIDE * i : 2 * STRIDE * (i + 3), :]
            spectra.append(add_row_halves(matmul(left_rows, window)))
        for g in range(supers):
            lane = g * 2 * LANES
            own = quads(spectra[0], g)
            other = quads(spectra[1], g)
            for begin, end, first in ROW_PARTS:
                out = cross_spectra(
                    [x[begin:end] for x in own], [x[begin:end] for x in other], sign, first
                )
                out_ref[i, begin:end, lane : lane + LANES] = out[0]
                out_ref[i, begin:end, lane + LANES : lane + 2 * LANES] = out[1]
                out_ref[i, HALF + begin : HALF + end, lane : lane + LANES] = out[2]
                out_ref[i, HALF + begin : HALF + end, lane + LANES : lane + 2 * LANES] = out[3]


def inverse_columns(high, low, table_ref):
    table_high = table_ref[:, : 2 * LANES]
    table_low = table_ref[:, 2 * LANES :]
    return matmul(high, table_high) + matmul(high, table_low) + matmul(low, table_high)


def coarse_peaks(offset, pieces, sources, forward_rows_ref, inverse_ref, inverse_rows_ref, table, sign):
    count = len(pieces)
    supers = count // GROUP
    wide = supers * 2 * LANES
    shape = (P_SIZE, wide)
    lane = iota(shape, 1)
    patch = lane // (2 * LANES) * GROUP + lane % LANES // HALF
    place = iota(shape, 0) - offset - patch * P_SIZE
    for j in range(count):
        here = place + j * P_SIZE
        values = jnp.where(
            (here >= 0) & (here < P_SIZE),
            basis_values(lane % HALF, lane % (2 * LANES) // LANES, here),
            0.0,
        )
        high, low = split(values)
        table[j, :, :wide] = high
        table[j, :, wide:] = low
    strips = jnp.zeros((2 * P_SIZE, wide), f32)
    for piece, source in zip(pieces, sources):
        product = matmul(piece[...], table[source])
        strips = strips + (product[:, :wide] + product[:, wide:])
    spectra = []
    for s in range(2):
        high, low = split(strips[s * P_SIZE : (s + 1) * P_SIZE])
        stack = jnp.concatenate([high, low], axis=0)
        spectra.append(add_row_halves(matmul(forward_rows_ref[...], stack)))
    peaks = []
    for g in range(supers):
        own = quads(spectra[0], g)
        other = quads(spectra[1], g)
        parts = []
        for begin, end, first in ROW_PARTS:
            shape = (end - begin, LANES)
            values = cross_spectra([x[begin:end] for x in own], [x[begin:end] for x in other], sign, first)
            corner = first_lane(shape) & (iota(shape, 0) == 0) & first
            turn = [
                jnp.where(corner, SCALE, c).astype(f32)
                for c in (2.0 * SCALE, 0.0, 2.0 * SCALE, 0.0)
            ]
            parts.append(coefficients(values, turn, first))
        cc, cs, sc, ss = (jnp.concatenate([a, b], axis=0) for a, b in zip(*parts))
        block = jnp.concatenate(
            [jnp.concatenate([cc, cs], axis=1), jnp.concatenate([sc, ss], axis=1)], axis=0
        )
        high, low = split(block)
        high, low = split(inverse_columns(high, low, inverse_ref))
        stack = jnp.concatenate([high, low], axis=0)
        sums = column_sums(add_row_halves(matmul(inverse_rows_ref[...], stack)))
        peaks += [patch_peak(*sums, n) for n in range(GROUP)]
    return peaks


def peak_kernel(
    offsets_ref,
    coarse_offset_ref,
    mask_ref,
    forward_rows_ref,
    inverse_ref,
    inverse_rows_ref,
    spectra_ref,
    *refs,
):
    pieces, (out_ref, table, turns, high_ref, low_ref, stacked) = refs[:-6], refs[-6:]
    bands, _, wide = spectra_ref.shape
    supers = wide // (2 * LANES)
    per_row = supers * GROUP
    side = lax.axis_index("gz")
    place = lax.axis_index("gx")
    count = len(pieces)
    sign = jnp.where(side == 0, 1.0, -1.0).astype(f32)
    sources = [exchange_source(place, step, count) for step in range(count)]
    column_offset = offsets_ref[1]
    coarse_offset = coarse_offset_ref[0]
    peaks = coarse_peaks(
        coarse_offset, pieces, sources, forward_rows_ref, inverse_ref, inverse_rows_ref, table, sign
    )
    blended = []
    for axis in range(2):
        values = [peak[axis] for peak in peaks]
        mean = sum(values[1:], values[0]) / count
        blended.append([(0.5 * DOWN) * (value + mean) for value in values])

    def prior(column):
        centre = (place * (2 * per_row) + column) * STRIDE + column_offset + P_SIZE // 2
        pick = jnp.clip((centre // DOWN - coarse_offset) // P_SIZE, 0, count - 1)
        out = []
        for values in blended:
            chosen = jnp.broadcast_to(values[0], column.shape)
            for j in range(1, count):
                chosen = jnp.where(pick == j, values[j], chosen)
            out.append(chosen)
        return out

    shape = (HALF, LANES)
    frequency_y = iota(shape, 0).astype(f32) / P_SIZE
    l0 = first_lane(shape)
    r0 = iota(shape, 0) == 0
    lane_row = iota((1, LANES), 1)
    frequency_x = (lane_row % HALF).astype(f32) / P_SIZE
    for t in range(2):
        for g in range(supers):
            column = 2 * (g * GROUP + lane_row // HALF) + (t + side) % 2
            dy, dx = (value - P_SIZE * jnp.round(value / P_SIZE) for value in prior(column))
            turn_y = nearest(frequency_y * dy)
            turn_x = nearest(frequency_x * dx)
            cy, sy = cosine_of_turns(turn_y), sine_of_turns(turn_y)
            cx, sx = cosine_of_turns(turn_x), sine_of_turns(turn_x)
            half_y = cosine_of_turns(nearest(0.5 * dy))
            half_x = cosine_of_turns(nearest(0.5 * dx))
            half_both = cosine_of_turns(nearest(0.5 * (dy + dx)))
            plus_real = cy * cx - sy * sx
            plus_imaginary = sy * cx + cy * sx
            minus_real = cy * cx + sy * sx
            minus_imaginary = sy * cx - cy * sx
            minus_real = jnp.where(l0, cy * half_x, jnp.where(r0, cx * half_y, minus_real))
            minus_imaginary = jnp.where(l0, sy * half_x, jnp.where(r0, sx * half_y, minus_imaginary))
            corner = l0 & r0
            turn = (plus_real, plus_imaginary, minus_real, minus_imaginary)
            ends = (1.0, half_x, half_y, half_both)
            for n in range(4):
                turns[t, g, n] = SCALE * jnp.where(corner, ends[n], 2.0 * turn[n])
    for i in range(bands):
        block = spectra_ref[i]
        for g in range(supers):
            lane = g * 2 * LANES
            values = quads(block, g)
            for begin, end, first in ROW_PARTS:
                parts = coefficients(
                    [x[begin:end] for x in values],
                    [turns[i % 2, g, n, begin:end] for n in range(4)],
                    first,
                )
                stacked[begin:end, lane : lane + LANES] = parts[0]
                stacked[begin:end, lane + LANES : lane + 2 * LANES] = parts[1]
                stacked[HALF + begin : HALF + end, lane : lane + LANES] = parts[2]
                stacked[HALF + begin : HALF + end, lane + LANES : lane + 2 * LANES] = parts[3]
        high, low = split(stacked[...])
        high_ref[i * P_SIZE : (i + 1) * P_SIZE] = high
        low_ref[i * P_SIZE : (i + 1) * P_SIZE] = low
    for g in range(supers):
        at = slice(g * 2 * LANES, (g + 1) * 2 * LANES)
        high, low = split(inverse_columns(high_ref[:, at], low_ref[:, at], inverse_ref))
        high_ref[:, at] = high
        low_ref[:, at] = low
    sums = []
    for i in range(bands):
        rows = slice(i * P_SIZE, (i + 1) * P_SIZE)
        stack = jnp.concatenate([high_ref[rows], low_ref[rows]], axis=0)
        sums.append(column_sums(add_row_halves(matmul(inverse_rows_ref[...], stack))))
    sums = [jnp.concatenate(parts, axis=0) for parts in zip(*sums)]
    shape = (bands, per_row)
    lane = iota(shape, 1)
    parity = (iota(shape, 0) + side) % 2
    found = [jnp.zeros(shape, f32) for _ in range(2)]
    for m in range(per_row):
        peak = patch_peak(*sums, m)
        found = [jnp.where(lane == m, p, x) for p, x in zip(peak, found)]
    shape = (2 * per_row, per_row)
    columns = iota(shape, 0) - 2 * iota(shape, 1)
    mask = mask_ref[...].astype(f32).astype(bf16)
    masks = [matmul(mask, (columns == n).astype(bf16)) for n in range(2)]
    chosen = jnp.where(parity == 0, masks[0], masks[1])
    base = prior(2 * lane + parity)
    for axis in range(2):
        out_ref[axis] = base[axis] + chosen * found[axis]


def exchange_source(place, step, count):
    if count & (count - 1) == 0:
        return place ^ step
    return lax.rem(place + count - step, count)


def exchanged(value, axis, step):
    count = lax.axis_size(axis)
    if count & (count - 1) == 0:
        pairs = [(i, i ^ step) for i in range(count)]
    else:
        pairs = [(i, (i + step) % count) for i in range(count)]
    return lax.ppermute(value, axis, pairs)


def from_next(value, axis):
    count = lax.axis_size(axis)
    return lax.ppermute(value, axis, [(i, i - 1) for i in range(1, count)])


def swapped(value):
    return lax.ppermute(value, "gz", [(0, 1), (1, 0)])


VMEM = pl.BlockSpec(memory_space=pltpu.VMEM)
SMEM = pl.BlockSpec(memory_space=pltpu.SMEM)


def params(mebibytes):
    return pltpu.CompilerParams(vmem_limit_bytes=mebibytes * 2**20)


def local(sections, fine_offsets, coarse_offset, tissue_mask):
    own = sections[0]
    rows, width = own.shape
    bands = rows // STRIDE
    per_row = width // P_SIZE
    tall = rows + P_SIZE
    count = lax.axis_size("gx")
    assert rows == DOWN * P_SIZE and width == DOWN * P_SIZE and count % GROUP == 0
    wide = 2 * width // 2
    supers = width // (2 * LANES)
    coarse_wide = count // GROUP * 2 * LANES
    own_low = from_next(own[:P_SIZE], "gy")
    own_right = from_next(jnp.concatenate([own[:, :P_SIZE], own_low[:, :P_SIZE]], axis=0), "gx")
    other = swapped(own)
    other_low = swapped(own_low)
    other_right = swapped(own_right)
    coarse = pl.pallas_call(
        shrink_kernel,
        out_shape=jax.ShapeDtypeStruct((rows // DOWN, width // DOWN), bf16),
        in_specs=[VMEM],
        out_specs=VMEM,
        compiler_params=params(16),
    )(own)
    both = jnp.concatenate([coarse, swapped(coarse)], axis=0)
    pieces = [both] + [exchanged(both, "gx", step) for step in range(1, count)]
    spectra = pl.pallas_call(
        forward_kernel,
        out_shape=jax.ShapeDtypeStruct((bands, P_SIZE, wide), f32),
        in_specs=[SMEM] + [VMEM] * 7,
        out_specs=VMEM,
        scratch_shapes=[
            pltpu.VMEM((2, tall, width + LANES), bf16),
            pltpu.VMEM((2, 2 * LANES, 4 * LANES), bf16),
            pltpu.VMEM((2, 2, 2 * tall, wide), bf16),
        ],
        compiler_params=params(32),
    )(
        fine_offsets,
        jnp.asarray(forward_columns_table()),
        own,
        own_low,
        own_right,
        other,
        other_low,
        other_right,
    )
    flow = pl.pallas_call(
        peak_kernel,
        out_shape=jax.ShapeDtypeStruct((2, bands, per_row), f32),
        in_specs=[SMEM, SMEM] + [VMEM] * (5 + count),
        out_specs=VMEM,
        scratch_shapes=[
            pltpu.VMEM((count, P_SIZE, 2 * coarse_wide), bf16),
            pltpu.VMEM((2, supers, 4, HALF, LANES), f32),
            pltpu.VMEM((bands * P_SIZE, wide), bf16),
            pltpu.VMEM((bands * P_SIZE, wide), bf16),
            pltpu.VMEM((P_SIZE, wide), f32),
        ],
        compiler_params=params(40),
    )(
        fine_offsets,
        coarse_offset,
        tissue_mask,
        jnp.asarray(forward_rows_table()),
        jnp.asarray(inverse_columns_table()),
        jnp.asarray(inverse_rows_table()),
        spectra,
        *pieces,
    )
    return flow.reshape(2, 1, bands, per_row)


def solution(mesh):
    placed = (P("gz", ("pairs", "gy"), "gx"), P("pairs"), P("pairs"), P(("pairs", "gy"), "gx"))
    return jax.shard_map(
        local,
        mesh=mesh,
        in_specs=placed,
        out_specs=P(None, "gz", ("pairs", "gy"), "gx"),
        check_vma=False,
    )
```

```python
import math

import jax
import jax.numpy as jnp
from jax import lax
from jax.experimental import pallas as pl
from jax.experimental.pallas import tpu as pltpu
from jax.sharding import PartitionSpec as P

P_SIZE = 64
HALF = P_SIZE // 2
STRIDE = 32
DOWN = 8
LANES = 128
GROUP = LANES // HALF
SHARPNESS = 12.0
SCALE = SHARPNESS / float(P_SIZE) ** 4 * math.log2(math.e)

f32 = jnp.float32
bf16 = jnp.bfloat16


def cosine_of_turns(turns):
    square = (turns * (2.0 * math.pi)) ** 2
    total = jnp.full_like(square, 1.0 / math.factorial(20))
    for n in range(9, -1, -1):
        total = total * square + (-1.0) ** n / math.factorial(2 * n)
    return total


def sine_of_turns(turns):
    angle = turns * (2.0 * math.pi)
    square = angle * angle
    total = jnp.full_like(square, -1.0 / math.factorial(19))
    for n in range(8, -1, -1):
        total = total * square + (-1.0) ** n / math.factorial(2 * n + 1)
    return total * angle


def nearest(turns):
    return turns - jnp.round(turns)


def basis_values(frequency, kind, place):
    nyquist = (kind == 1) & (frequency == 0)
    number = jnp.where(nyquist, HALF, frequency)
    quarter = jnp.where((kind == 1) & (frequency != 0), P_SIZE // 4, 0)
    step = (number * place - quarter) & (P_SIZE - 1)
    step = jnp.where(step > HALF, P_SIZE - step, step)
    flip = step > P_SIZE // 4
    step = jnp.where(flip, HALF - step, step)
    square = (step.astype(f32) * (2.0 * math.pi / P_SIZE)) ** 2
    total = jnp.full_like(square, 1.0 / math.factorial(12))
    for n in range(5, -1, -1):
        total = total * square + (-1.0) ** n / math.factorial(2 * n)
    return jnp.where(flip, -total, total)


def iota(shape, axis):
    return lax.broadcasted_iota(jnp.int32, shape, axis)


def split(values):
    high = values.astype(bf16)
    return high, (values - high.astype(f32)).astype(bf16)


def matmul(left, right):
    return jnp.dot(left, right, preferred_element_type=f32)


def add_row_halves(values):
    half = values.shape[0] // 2
    return values[:half] + values[half:]


def first_lane(shape):
    return iota(shape, 1) % HALF == 0


def half_spectra(cc, cs, sc, ss, first):
    shape = cc.shape
    l0 = first_lane(shape)
    if not first:
        return (
            cc - jnp.where(l0, 0.0, ss),
            sc + jnp.where(l0, 0.0, cs),
            jnp.where(l0, cs, cc + ss),
            jnp.where(l0, ss, sc - cs),
        )
    r0 = iota(shape, 0) == 0
    either = l0 | r0
    return (
        cc - jnp.where(either, 0.0, ss),
        jnp.where(r0, 0.0, sc) + jnp.where(l0, 0.0, cs),
        jnp.where(l0, cs, jnp.where(r0, sc, cc + ss)),
        jnp.where(either, ss, sc - cs),
    )


def cross_spectra(own, other, sign, first):
    a = half_spectra(*own, first)
    b = half_spectra(*other, first)
    out = []
    for r, i in ((0, 1), (2, 3)):
        out.append(b[r] * a[r] + b[i] * a[i])
        out.append(sign * (b[r] * a[i] - b[i] * a[r]))
    if first:
        shape = own[0].shape
        corner = first_lane(shape) & (iota(shape, 0) == 0)
        out = [jnp.where(corner, x * y, o) for x, y, o in zip(own, other, out)]
    return out


def coefficients(g, t, first):
    gpr, gpi, gmr, gmi = g
    tpr, tpi, tmr, tmi = t
    shape = gpr.shape
    l0 = first_lane(shape)
    hpr = gpr * tpr - gpi * tpi
    hpi = gpr * tpi + gpi * tpr
    hmr = gmr * tmr - gmi * tmi
    hmi = gmr * tmi + gmi * tmr
    if not first:
        return (
            hpr + jnp.where(l0, 0.0, hmr),
            jnp.where(l0, hmr, hmi - hpi),
            -hpi - jnp.where(l0, 0.0, hmi),
            jnp.where(l0, -hmi, hmr - hpr),
        )
    r0 = iota(shape, 0) == 0
    either = l0 | r0
    corner = l0 & r0
    out = (
        hpr + jnp.where(either, 0.0, hmr),
        jnp.where(l0, hmr, jnp.where(r0, 0.0, hmi) - hpi),
        jnp.where(r0, hmr, -hpi - jnp.where(l0, 0.0, hmi)),
        jnp.where(either, -hmi, hmr - hpr),
    )
    return [jnp.where(corner, x * y, o) for x, y, o in zip(g, t, out)]


def signed(number):
    return jnp.where(number >= HALF, number - P_SIZE, number).astype(f32)


def column_sums(logits):
    largest = jnp.max(logits, axis=0, keepdims=True)
    weights = jnp.exp2(logits - largest)
    rows = signed(iota((P_SIZE, 1), 0))
    return largest, jnp.sum(weights, axis=0, keepdims=True), jnp.sum(weights * rows, axis=0, keepdims=True)


def patch_peak(largest, total, moment, patch):
    window = slice(patch * P_SIZE, (patch + 1) * P_SIZE)
    top = largest[:, window]
    peak = jnp.max(top, axis=1, keepdims=True)
    factor = jnp.exp2(top - peak)
    weight = factor * total[:, window]
    columns = signed(iota((1, P_SIZE), 1))
    bottom = jnp.sum(weight, axis=1, keepdims=True)
    along_rows = jnp.sum(factor * moment[:, window], axis=1, keepdims=True)
    along_columns = jnp.sum(weight * columns, axis=1, keepdims=True)
    return along_rows / bottom, along_columns / bottom


ROW_PARTS = ((0, 8, True), (8, HALF, False))


def quads(block, group):
    lane = group * 2 * LANES
    top, bottom = block[:HALF], block[HALF:]
    return (
        top[:, lane : lane + LANES],
        top[:, lane + LANES : lane + 2 * LANES],
        bottom[:, lane : lane + LANES],
        bottom[:, lane + LANES : lane + 2 * LANES],
    )


def unpack(packed):
    wide = packed.astype(f32)
    return jnp.concatenate([wide, pltpu.roll(wide, P_SIZE, axis=1)], axis=0).astype(bf16)


def prepare_kernel(tile_ref, out_ref, low_ref, packed_ref, sem):
    rows, width = tile_ref.shape
    columns = width // DOWN
    copy = pltpu.make_async_copy(tile_ref, out_ref, sem)
    copy.start()
    pick = (iota((width, LANES), 0) // DOWN == iota((width, LANES), 1) % columns).astype(bf16)
    left = iota((columns // 2, LANES), 1) < P_SIZE
    copy.wait()
    sums = matmul(out_ref[...], pick)
    coarse = jnp.sum(sums.reshape(rows // DOWN, DOWN, LANES), axis=1) / DOWN
    half = coarse.shape[0] // 2
    packed_ref[:half] = jnp.where(left, coarse[:half], coarse[half:]).astype(bf16)
    low_ref[...] = out_ref[:P_SIZE]
    edge = out_ref[:, :LANES].astype(f32)
    half_rows = rows // 2
    left = iota((half_rows, LANES), 1) < P_SIZE
    edge = jnp.where(left, edge[:half_rows], pltpu.roll(edge[half_rows:], P_SIZE, axis=1))
    packed_ref[half:] = edge.astype(bf16)


def tables_kernel(
    offsets_hbm,
    coarse_offset_hbm,
    mask_hbm,
    weights_ref,
    rows_ref,
    picks_ref,
    chosen_ref,
    mask_out_ref,
    forward_rows_ref,
    inverse_ref,
    inverse_rows_ref,
    offsets_ref,
    coarse_offset_ref,
    mask_ref,
    sems,
):
    copies = [
        pltpu.make_async_copy(source, target, sems.at[n])
        for n, (source, target) in enumerate(
            (
                (offsets_hbm, offsets_ref),
                (coarse_offset_hbm, coarse_offset_ref),
                (mask_hbm, mask_ref),
            )
        )
    ]
    for copy in copies:
        copy.start()
    count = lax.axis_size("gx")
    bands, per_row = chosen_ref.shape
    supers = per_row // GROUP
    side = lax.axis_index("gz")
    gx_place = lax.axis_index("gx")
    shape = (2 * P_SIZE, LANES)
    lane = iota(shape, 1)
    row = iota(shape, 0)
    values = jnp.where(
        row // P_SIZE == lane % P_SIZE // HALF,
        basis_values(lane % HALF, lane // P_SIZE, row % P_SIZE),
        0.0,
    )
    padded = jnp.concatenate([values, jnp.zeros((2 * P_SIZE, LANES), f32)], axis=0)
    shape = (P_SIZE, LANES)
    row = iota(shape, 0)
    lane = iota(shape, 1)
    basis = basis_values(row % HALF, row // HALF, lane % P_SIZE)
    high, low = split(basis)
    forward_rows_ref[:P_SIZE] = high
    forward_rows_ref[P_SIZE:] = jnp.where(lane < P_SIZE, low.astype(f32), 0.0).astype(bf16)
    wide_high = jnp.concatenate([high.astype(f32)] * 2, axis=1)
    wide_low = jnp.concatenate([low.astype(f32)] * 2, axis=1)
    for kind in range(2):
        rows = slice(kind * HALF, (kind + 1) * HALF)
        for patch in range(GROUP):
            mine = iota((HALF, GROUP * P_SIZE), 1) // P_SIZE == patch
            at = (kind * GROUP + patch) * HALF
            for part, value in enumerate((wide_high, wide_low)):
                inverse_ref[at : at + HALF, part * 2 * LANES : (part + 1) * 2 * LANES] = jnp.where(
                    mine, value[rows], 0.0
                ).astype(bf16)
    high, low = split(basis_values(lane % HALF, lane % P_SIZE // HALF, row))
    inverse_rows_ref[:P_SIZE] = high
    inverse_rows_ref[P_SIZE:] = jnp.where(lane < P_SIZE, low.astype(f32), 0.0).astype(bf16)
    for copy in copies:
        copy.wait()
    row_offset = offsets_ref[0]
    column_offset = offsets_ref[1]
    coarse_offset = coarse_offset_ref[0]
    shifts = [column_offset + STRIDE * ((t + side) % 2) for t in range(2)] + [coarse_offset]
    for t, shift in enumerate(shifts):
        moved = pltpu.roll(padded, shift, axis=0)
        for part, value in enumerate(split(moved)):
            weights_ref[t, :, part * LANES : (part + 1) * LANES] = value
            value = pltpu.roll(value.astype(f32), P_SIZE, axis=1).astype(bf16)
            weights_ref[t, :, (part + 2) * LANES : (part + 3) * LANES] = value
    shape = (P_SIZE, 6 * STRIDE)
    number = iota(shape, 0)
    lane = iota(shape, 1)
    place = lane // P_SIZE * STRIDE + lane % STRIDE - row_offset
    values = jnp.where(
        (place >= 0) & (place < P_SIZE), basis_values(number % HALF, number // HALF, place), 0.0
    )
    high, low = split(values)
    is_low = lane % P_SIZE >= STRIDE
    rows_ref[:P_SIZE] = high
    rows_ref[P_SIZE:] = jnp.where(is_low, 0.0, low.astype(f32)).astype(bf16)
    def pick(column):
        centre = (gx_place * (2 * per_row) + column) * STRIDE + column_offset + P_SIZE // 2
        return jnp.clip((centre // DOWN - coarse_offset) // P_SIZE, 0, count - 1)

    lane_row = iota((1, LANES), 1)
    for t in range(2):
        for g in range(supers):
            column = 2 * (g * GROUP + lane_row // HALF) + (t + side) % 2
            picks_ref[t, g] = jnp.broadcast_to(pick(column), (8, LANES))
    shape = (bands, per_row)
    parity = (iota(shape, 0) + side) % 2
    chosen_ref[...] = pick(2 * iota(shape, 1) + parity)
    shape = (2 * per_row, per_row)
    columns = iota(shape, 0) - 2 * iota(shape, 1)
    mask = mask_ref[...].astype(f32).astype(bf16)
    masks = [matmul(mask, (columns == n).astype(bf16)) for n in range(2)]
    mask_out_ref[...] = jnp.where(parity == 0, masks[0], masks[1])


def forward_bands(image, stacked, weights, left_rows, first_band, out_ref):
    bands = out_ref.shape[0]
    tall = image.shape[1]
    wide = out_ref.shape[2]
    blocks = tall // STRIDE
    supers = wide // (2 * LANES)
    left = iota((tall, LANES), 1) < P_SIZE
    for s in range(2):
        for t in range(2):
            for g in range(supers):
                lane = g * 2 * LANES
                a = matmul(image[s, :, lane : lane + 2 * LANES], weights[t, :, : 2 * LANES])
                b = matmul(image[s, :, lane + LANES : lane + 3 * LANES], weights[t, :, 2 * LANES :])
                a = a[:, :LANES] + a[:, LANES:]
                b = b[:, :LANES] + b[:, LANES:]
                for part, value in enumerate(
                    (jnp.where(left, a, b), pltpu.roll(jnp.where(left, b, a), P_SIZE, axis=1))
                ):
                    high, low = split(value)
                    at = slice(lane + part * LANES, lane + (part + 1) * LANES)
                    for n in range(blocks):
                        block = slice(n * STRIDE, (n + 1) * STRIDE)
                        stacked[s, t, 2 * n * STRIDE : (2 * n + 1) * STRIDE, at] = high[block]
                        stacked[s, t, (2 * n + 1) * STRIDE : (2 * n + 2) * STRIDE, at] = low[block]
    sign = jnp.where(lax.axis_index("gz") == 0, 1.0, -1.0).astype(f32)
    for i in range(bands):
        spectra = []
        for s in range(2):
            window = stacked[s, (first_band + i) % 2, 2 * STRIDE * i : 2 * STRIDE * (i + 3), :]
            spectra.append(add_row_halves(matmul(left_rows, window)))
        for g in range(supers):
            lane = g * 2 * LANES
            own = quads(spectra[0], g)
            other = quads(spectra[1], g)
            for begin, end, first in ROW_PARTS:
                out = cross_spectra(
                    [x[begin:end] for x in own], [x[begin:end] for x in other], sign, first
                )
                out_ref[i, begin:end, lane : lane + LANES] = out[0]
                out_ref[i, begin:end, lane + LANES : lane + 2 * LANES] = out[1]
                out_ref[i, HALF + begin : HALF + end, lane : lane + LANES] = out[2]
                out_ref[i, HALF + begin : HALF + end, lane + LANES : lane + 2 * LANES] = out[3]


def is_last(axis):
    return lax.axis_index(axis) == lax.axis_size(axis) - 1


def upper_kernel(
    weights, left_rows_ref, own_ref, own_right_ref, other_ref, other_right_ref, out_ref, image, stacked
):
    width = own_ref.shape[1]
    for s, (main, right) in enumerate(((own_ref, own_right_ref), (other_ref, other_right_ref))):
        image[s, :, :width] = main[...]
        image[s, :, width:] = unpack(right[...])

    @pl.when(is_last("gx"))
    def _():
        image[:, :, width:] = jnp.zeros((2, image.shape[1], LANES), bf16)

    forward_bands(image, stacked, weights, left_rows_ref[...], 0, out_ref)


def lower_kernel(
    weights,
    left_rows_ref,
    own_ref,
    own_right_ref,
    own_low_ref,
    other_ref,
    other_right_ref,
    other_low_ref,
    out_ref,
    image,
    stacked,
):
    rows, width = own_ref.shape
    for s, (main, right, low) in enumerate(
        ((own_ref, own_right_ref, own_low_ref), (other_ref, other_right_ref, other_low_ref))
    ):
        image[s, :P_SIZE, :width] = main[rows - P_SIZE :]
        edge = right[rows // 2 - P_SIZE :].astype(f32)
        image[s, :P_SIZE, width:] = pltpu.roll(edge, P_SIZE, axis=1).astype(bf16)
        image[s, P_SIZE:] = low[...]

    @pl.when(is_last("gx"))
    def _():
        image[:, :, width:] = jnp.zeros((2, 2 * P_SIZE, LANES), bf16)

    @pl.when(is_last("gy"))
    def _():
        image[:, P_SIZE:, :] = jnp.zeros((2, P_SIZE, width + LANES), bf16)

    forward_bands(
        image, stacked, weights, left_rows_ref[...], rows // STRIDE - out_ref.shape[0], out_ref
    )


def inverse_columns(high, low, table_ref):
    table_high = table_ref[:, : 2 * LANES]
    table_low = table_ref[:, 2 * LANES :]
    return matmul(high, table_high) + matmul(high, table_low) + matmul(low, table_high)


def coarse_peaks(strip, forward_rows_ref, inverse_ref, inverse_rows_ref, weights, sign):
    supers = len(strip) * 2 // GROUP
    left = iota((2 * P_SIZE, LANES), 1) < P_SIZE
    strip = strip + [jnp.zeros_like(strip[0])]
    columns = []
    for g in range(supers):
        a, b = (
            matmul(
                jnp.concatenate(strip[2 * g + n : 2 * g + n + 2], axis=1),
                weights[:, 2 * n * LANES : 2 * (n + 1) * LANES],
            )
            for n in range(2)
        )
        a = a[:, :LANES] + a[:, LANES:]
        b = b[:, :LANES] + b[:, LANES:]
        columns += [jnp.where(left, a, b), pltpu.roll(jnp.where(left, b, a), P_SIZE, axis=1)]
    strips = jnp.concatenate(columns, axis=1)
    spectra = []
    for s in range(2):
        high, low = split(strips[s * P_SIZE : (s + 1) * P_SIZE])
        stack = jnp.concatenate([high, low], axis=0)
        spectra.append(add_row_halves(matmul(forward_rows_ref[...], stack)))
    peaks = []
    for g in range(supers):
        own = quads(spectra[0], g)
        other = quads(spectra[1], g)
        parts = []
        for begin, end, first in ROW_PARTS:
            shape = (end - begin, LANES)
            values = cross_spectra([x[begin:end] for x in own], [x[begin:end] for x in other], sign, first)
            corner = first_lane(shape) & (iota(shape, 0) == 0) & first
            turn = [
                jnp.where(corner, SCALE, c).astype(f32)
                for c in (2.0 * SCALE, 0.0, 2.0 * SCALE, 0.0)
            ]
            parts.append(coefficients(values, turn, first))
        cc, cs, sc, ss = (jnp.concatenate([a, b], axis=0) for a, b in zip(*parts))
        block = jnp.concatenate(
            [jnp.concatenate([cc, cs], axis=1), jnp.concatenate([sc, ss], axis=1)], axis=0
        )
        high, low = split(block)
        high, low = split(inverse_columns(high, low, inverse_ref))
        stack = jnp.concatenate([high, low], axis=0)
        sums = column_sums(add_row_halves(matmul(inverse_rows_ref[...], stack)))
        peaks += [patch_peak(*sums, n) for n in range(GROUP)]
    return peaks


def turn_kernel(
    forward_rows_ref,
    inverse_ref,
    inverse_rows_ref,
    weights,
    picks_ref,
    chosen_ref,
    own_part_ref,
    other_part_ref,
    turns,
    base_ref,
    ordered,
):
    count = ordered.shape[0]
    supers = turns.shape[1]
    side = lax.axis_index("gz")
    place = lax.axis_index("gx")
    sign = jnp.where(side == 0, 1.0, -1.0).astype(f32)
    for step in range(count):
        for part, ref in enumerate((own_part_ref, other_part_ref)):
            tile = ref[step * HALF : (step + 1) * HALF].astype(f32)
            tile = jnp.concatenate([tile, pltpu.roll(tile, P_SIZE, axis=1)], axis=0)
            ordered[place ^ step, part * P_SIZE : (part + 1) * P_SIZE] = tile
    left = iota((2 * P_SIZE, LANES), 1) < P_SIZE
    strip = []
    for j in range(0, count, 2):
        both = jnp.where(left, ordered[j], pltpu.roll(ordered[j + 1], P_SIZE, axis=1))
        strip.append(both.astype(bf16))
    peaks = coarse_peaks(
        strip, forward_rows_ref, inverse_ref, inverse_rows_ref, weights.at[2], sign
    )
    blended = []
    for axis in range(2):
        values = [peak[axis] for peak in peaks]
        mean = sum(values[1:], values[0]) / count
        blended.append([(0.5 * DOWN) * (value + mean) for value in values])

    def prior(pick):
        out = []
        for values in blended:
            chosen = jnp.broadcast_to(values[0], pick.shape)
            for j in range(1, count):
                chosen = jnp.where(pick == j, values[j], chosen)
            out.append(chosen)
        return out

    shape = (HALF, LANES)
    frequency_y = iota(shape, 0).astype(f32) / P_SIZE
    l0 = first_lane(shape)
    r0 = iota(shape, 0) == 0
    lane_row = iota((1, LANES), 1)
    frequency_x = (lane_row % HALF).astype(f32) / P_SIZE
    for t in range(2):
        for g in range(supers):
            dy, dx = (
                value - P_SIZE * jnp.round(value / P_SIZE) for value in prior(picks_ref[t, g, :1])
            )
            turn_y = nearest(frequency_y * dy)
            turn_x = nearest(frequency_x * dx)
            cy, sy = cosine_of_turns(turn_y), sine_of_turns(turn_y)
            cx, sx = cosine_of_turns(turn_x), sine_of_turns(turn_x)
            half_y = cosine_of_turns(nearest(0.5 * dy))
            half_x = cosine_of_turns(nearest(0.5 * dx))
            half_both = cosine_of_turns(nearest(0.5 * (dy + dx)))
            plus_real = cy * cx - sy * sx
            plus_imaginary = sy * cx + cy * sx
            minus_real = cy * cx + sy * sx
            minus_imaginary = sy * cx - cy * sx
            minus_real = jnp.where(l0, cy * half_x, jnp.where(r0, cx * half_y, minus_real))
            minus_imaginary = jnp.where(l0, sy * half_x, jnp.where(r0, sx * half_y, minus_imaginary))
            corner = l0 & r0
            turn = (plus_real, plus_imaginary, minus_real, minus_imaginary)
            ends = (1.0, half_x, half_y, half_both)
            for n in range(4):
                turns[t, g, n] = SCALE * jnp.where(corner, ends[n], 2.0 * turn[n])
    base = prior(chosen_ref[...])
    for axis in range(2):
        base_ref[axis] = base[axis]


def peak_kernel(
    inverse_ref,
    inverse_rows_ref,
    mask_ref,
    base_ref,
    turns,
    upper_ref,
    lower_ref,
    out_ref,
    high_ref,
    low_ref,
    stacked,
):
    _, _, wide = upper_ref.shape
    supers = wide // (2 * LANES)
    per_row = supers * GROUP
    refs = [upper_ref.at[i] for i in range(upper_ref.shape[0])]
    refs += [lower_ref.at[i] for i in range(lower_ref.shape[0])]
    bands = len(refs)
    for i in range(bands):
        block = refs[i][...]
        for g in range(supers):
            lane = g * 2 * LANES
            values = quads(block, g)
            for begin, end, first in ROW_PARTS:
                parts = coefficients(
                    [x[begin:end] for x in values],
                    [turns[i % 2, g, n, begin:end] for n in range(4)],
                    first,
                )
                stacked[begin:end, lane : lane + LANES] = parts[0]
                stacked[begin:end, lane + LANES : lane + 2 * LANES] = parts[1]
                stacked[HALF + begin : HALF + end, lane : lane + LANES] = parts[2]
                stacked[HALF + begin : HALF + end, lane + LANES : lane + 2 * LANES] = parts[3]
        high, low = split(stacked[...])
        high_ref[i * P_SIZE : (i + 1) * P_SIZE] = high
        low_ref[i * P_SIZE : (i + 1) * P_SIZE] = low
    for g in range(supers):
        at = slice(g * 2 * LANES, (g + 1) * 2 * LANES)
        high, low = split(inverse_columns(high_ref[:, at], low_ref[:, at], inverse_ref))
        high_ref[:, at] = high
        low_ref[:, at] = low
    sums = []
    for i in range(bands):
        rows = slice(i * P_SIZE, (i + 1) * P_SIZE)
        stack = jnp.concatenate([high_ref[rows], low_ref[rows]], axis=0)
        sums.append(column_sums(add_row_halves(matmul(inverse_rows_ref[...], stack))))
    sums = [jnp.concatenate(parts, axis=0) for parts in zip(*sums)]
    lane = iota((bands, LANES), 1)
    found = [jnp.zeros((bands, LANES), f32) for _ in range(2)]
    for m in range(per_row):
        peak = patch_peak(*sums, m)
        found = [jnp.where(lane == m, p, x) for p, x in zip(peak, found)]
    for axis in range(2):
        flow = base_ref[axis] + mask_ref[...] * found[axis][:, :per_row]
        out_ref[axis, 0] = jnp.transpose(flow)


def exchanged(value, axis, step):
    return lax.ppermute(value, axis, [(i, i ^ step) for i in range(lax.axis_size(axis))])


def from_later(value, axis, step):
    return lax.ppermute(value, axis, [(i, i - step) for i in range(step, lax.axis_size(axis))])


def swapped(value):
    return lax.ppermute(value, "gz", [(0, 1), (1, 0)])


VMEM = pl.BlockSpec(memory_space=pltpu.VMEM)
SMEM = pl.BlockSpec(memory_space=pltpu.SMEM)


def cost(microseconds):
    return pl.CostEstimate(
        flops=0, bytes_accessed=int(microseconds * 3.0e6), transcendentals=0
    )


def params(mebibytes):
    return pltpu.CompilerParams(vmem_limit_bytes=mebibytes * 2**20)


def local(sections, fine_offsets, coarse_offset, tissue_mask):
    own = sections[0]
    rows, width = own.shape
    bands = rows // STRIDE
    per_row = width // P_SIZE
    count = lax.axis_size("gx")
    assert rows == DOWN * P_SIZE and width == DOWN * P_SIZE
    assert count % GROUP == 0 and count & (count - 1) == 0
    wide = width
    supers = width // (2 * LANES)
    other = swapped(own)
    own_tile, own_edge, packed = pl.pallas_call(
        prepare_kernel,
        out_shape=(
            jax.ShapeDtypeStruct((rows, width), bf16),
            jax.ShapeDtypeStruct((P_SIZE, width), bf16),
            jax.ShapeDtypeStruct((HALF + rows // 2, LANES), bf16),
        ),
        in_specs=[pl.BlockSpec(memory_space=pl.ANY)],
        out_specs=(VMEM,) * 3,
        scratch_shapes=[pltpu.SemaphoreType.DMA],
        compiler_params=params(16),
    )(own)
    tables = pl.pallas_call(
        tables_kernel,
        out_shape=(
            jax.ShapeDtypeStruct((3, 2 * LANES, 4 * LANES), bf16),
            jax.ShapeDtypeStruct((2 * P_SIZE, 6 * STRIDE), bf16),
            jax.ShapeDtypeStruct((2, supers, 8, LANES), jnp.int32),
            jax.ShapeDtypeStruct((bands, per_row), jnp.int32),
            jax.ShapeDtypeStruct((bands, per_row), f32),
            jax.ShapeDtypeStruct((2 * P_SIZE, LANES), bf16),
            jax.ShapeDtypeStruct((2 * LANES, 4 * LANES), bf16),
            jax.ShapeDtypeStruct((2 * P_SIZE, LANES), bf16),
        ),
        in_specs=[pl.BlockSpec(memory_space=pltpu.HBM)] * 3,
        out_specs=(VMEM,) * 8,
        scratch_shapes=[
            pltpu.SMEM(fine_offsets.shape, jnp.int32),
            pltpu.SMEM(coarse_offset.shape, jnp.int32),
            pltpu.VMEM(tissue_mask.shape, jnp.int32),
            pltpu.SemaphoreType.DMA((3,)),
        ],
        compiler_params=params(16),
        cost_estimate=cost(1.5),
    )(fine_offsets, coarse_offset, tissue_mask)
    got_even = exchanged(packed, "gx", 1)
    got_odd = lax.ppermute(packed[HALF:], "gx", [(i + 1, i) for i in range(1, count - 1, 2)])
    steps = [packed[:HALF], got_even[:HALF]]
    right = jnp.where(lax.axis_index("gx") % 2 == 0, got_even[HALF:], got_odd)
    tiles = jnp.concatenate(steps, axis=0)
    step = 2
    while step < count:
        tiles = jnp.concatenate([tiles, exchanged(tiles, "gx", step)], axis=0)
        step *= 2
    weights, left_rows, picks, chosen, mask, forward_rows, inverse, inverse_rows = tables
    low_payload = jnp.concatenate([own_edge, right[:P_SIZE]], axis=1)
    low_payload, weights = lax.optimization_barrier((low_payload, weights))
    own_low = from_later(low_payload, "gy", 1)
    other_right = swapped(right)
    other_tiles = swapped(tiles)
    other_low = swapped(own_low)
    low_bands = P_SIZE // STRIDE
    upper = pl.pallas_call(
        upper_kernel,
        out_shape=jax.ShapeDtypeStruct((bands - low_bands, P_SIZE, wide), f32),
        in_specs=[VMEM] * 6,
        out_specs=VMEM,
        scratch_shapes=[
            pltpu.VMEM((2, rows, width + LANES), bf16),
            pltpu.VMEM((2, 2, 2 * rows, wide), bf16),
        ],
        compiler_params=params(32),
        cost_estimate=cost(2.6),
    )(weights, left_rows, own_tile, right, other, other_right)
    other_tiles, upper = lax.optimization_barrier((other_tiles, upper))
    turns, base = pl.pallas_call(
        turn_kernel,
        out_shape=(
            jax.ShapeDtypeStruct((2, supers, 4, HALF, LANES), f32),
            jax.ShapeDtypeStruct((2, bands, per_row), f32),
        ),
        in_specs=[VMEM] * 8,
        out_specs=(VMEM,) * 2,
        scratch_shapes=[pltpu.VMEM((count, 2 * P_SIZE, LANES), f32)],
        compiler_params=params(32),
        cost_estimate=cost(1.2),
    )(
        forward_rows,
        inverse,
        inverse_rows,
        weights,
        picks,
        chosen,
        tiles,
        other_tiles,
    )
    lower = pl.pallas_call(
        lower_kernel,
        out_shape=jax.ShapeDtypeStruct((low_bands, P_SIZE, wide), f32),
        in_specs=[VMEM] * 8,
        out_specs=VMEM,
        scratch_shapes=[
            pltpu.VMEM((2, 2 * P_SIZE, width + LANES), bf16),
            pltpu.VMEM((2, 2, 4 * P_SIZE, wide), bf16),
        ],
        compiler_params=params(32),
        cost_estimate=cost(0.6),
    )(weights, left_rows, own_tile, right, own_low, other, other_right, other_low)
    flow = pl.pallas_call(
        peak_kernel,
        out_shape=jax.ShapeDtypeStruct((2, 1, per_row, bands), f32),
        in_specs=[VMEM] * 7,
        out_specs=VMEM,
        scratch_shapes=[
            pltpu.VMEM((bands * P_SIZE, wide), bf16),
            pltpu.VMEM((bands * P_SIZE, wide), bf16),
            pltpu.VMEM((P_SIZE, wide), f32),
        ],
        compiler_params=params(40),
        cost_estimate=cost(3.5),
    )(
        inverse,
        inverse_rows,
        mask,
        base,
        turns,
        upper,
        lower,
    )
    return jnp.swapaxes(flow, 2, 3)


def solution(mesh):
    placed = (P("gz", ("pairs", "gy"), "gx"), P("pairs"), P("pairs"), P(("pairs", "gy"), "gx"))
    return jax.shard_map(
        local,
        mesh=mesh,
        in_specs=placed,
        out_specs=P(None, "gz", ("pairs", "gy"), "gx"),
        check_vma=False,
    )
```

```python
import functools
import math

import jax
import jax.numpy as jnp
from jax import lax
from jax.experimental import pallas as pl
from jax.experimental.pallas import tpu as pltpu
from jax.sharding import PartitionSpec as P

P_SIZE = 64
HALF = P_SIZE // 2
STRIDE = 32
DOWN = 8
LANES = 128
GROUP = LANES // HALF
SHARPNESS = 12.0
PARTS = 1
SCALE = SHARPNESS / float(P_SIZE) ** 4 * math.log2(math.e)

f32 = jnp.float32
bf16 = jnp.bfloat16


def cosine_of_turns(turns):
    square = (turns * (2.0 * math.pi)) ** 2
    total = jnp.full_like(square, 1.0 / math.factorial(20))
    for n in range(9, -1, -1):
        total = total * square + (-1.0) ** n / math.factorial(2 * n)
    return total


def sine_of_turns(turns):
    angle = turns * (2.0 * math.pi)
    square = angle * angle
    total = jnp.full_like(square, -1.0 / math.factorial(19))
    for n in range(8, -1, -1):
        total = total * square + (-1.0) ** n / math.factorial(2 * n + 1)
    return total * angle


def nearest(turns):
    return turns - jnp.round(turns)


def basis_values(frequency, kind, place):
    nyquist = (kind == 1) & (frequency == 0)
    number = jnp.where(nyquist, HALF, frequency)
    quarter = jnp.where((kind == 1) & (frequency != 0), P_SIZE // 4, 0)
    step = (number * place - quarter) & (P_SIZE - 1)
    step = jnp.where(step > HALF, P_SIZE - step, step)
    flip = step > P_SIZE // 4
    step = jnp.where(flip, HALF - step, step)
    square = (step.astype(f32) * (2.0 * math.pi / P_SIZE)) ** 2
    total = jnp.full_like(square, 1.0 / math.factorial(12))
    for n in range(5, -1, -1):
        total = total * square + (-1.0) ** n / math.factorial(2 * n)
    return jnp.where(flip, -total, total)


def iota(shape, axis):
    return lax.broadcasted_iota(jnp.int32, shape, axis)


def split(values):
    high = values.astype(bf16)
    return high, (values - high.astype(f32)).astype(bf16)


def matmul(left, right):
    return jnp.dot(left, right, preferred_element_type=f32)


def add_row_halves(values):
    half = values.shape[0] // 2
    return values[:half] + values[half:]


def first_lane(shape):
    return iota(shape, 1) % HALF == 0


def half_spectra(cc, cs, sc, ss, first):
    shape = cc.shape
    l0 = first_lane(shape)
    if not first:
        return (
            cc - jnp.where(l0, 0.0, ss),
            sc + jnp.where(l0, 0.0, cs),
            jnp.where(l0, cs, cc + ss),
            jnp.where(l0, ss, sc - cs),
        )
    r0 = iota(shape, 0) == 0
    either = l0 | r0
    return (
        cc - jnp.where(either, 0.0, ss),
        jnp.where(r0, 0.0, sc) + jnp.where(l0, 0.0, cs),
        jnp.where(l0, cs, jnp.where(r0, sc, cc + ss)),
        jnp.where(either, ss, sc - cs),
    )


def cross_spectra(own, other, sign, first):
    a = half_spectra(*own, first)
    b = half_spectra(*other, first)
    out = []
    for r, i in ((0, 1), (2, 3)):
        out.append(b[r] * a[r] + b[i] * a[i])
        out.append(sign * (b[r] * a[i] - b[i] * a[r]))
    if first:
        shape = own[0].shape
        corner = first_lane(shape) & (iota(shape, 0) == 0)
        out = [jnp.where(corner, x * y, o) for x, y, o in zip(own, other, out)]
    return out


def coefficients(g, t, first):
    gpr, gpi, gmr, gmi = g
    tpr, tpi, tmr, tmi = t
    shape = gpr.shape
    l0 = first_lane(shape)
    hpr = gpr * tpr - gpi * tpi
    hpi = gpr * tpi + gpi * tpr
    hmr = gmr * tmr - gmi * tmi
    hmi = gmr * tmi + gmi * tmr
    if not first:
        return (
            hpr + jnp.where(l0, 0.0, hmr),
            jnp.where(l0, hmr, hmi - hpi),
            -hpi - jnp.where(l0, 0.0, hmi),
            jnp.where(l0, -hmi, hmr - hpr),
        )
    r0 = iota(shape, 0) == 0
    either = l0 | r0
    corner = l0 & r0
    out = (
        hpr + jnp.where(either, 0.0, hmr),
        jnp.where(l0, hmr, jnp.where(r0, 0.0, hmi) - hpi),
        jnp.where(r0, hmr, -hpi - jnp.where(l0, 0.0, hmi)),
        jnp.where(either, -hmi, hmr - hpr),
    )
    return [jnp.where(corner, x * y, o) for x, y, o in zip(g, t, out)]


def signed(number):
    return jnp.where(number >= HALF, number - P_SIZE, number).astype(f32)


def column_sums(logits):
    largest = jnp.max(logits, axis=0, keepdims=True)
    weights = jnp.exp2(logits - largest)
    rows = signed(iota((P_SIZE, 1), 0))
    return largest, jnp.sum(weights, axis=0, keepdims=True), jnp.sum(weights * rows, axis=0, keepdims=True)


def patch_peak(largest, total, moment, patch):
    window = slice(patch * P_SIZE, (patch + 1) * P_SIZE)
    top = largest[:, window]
    peak = jnp.max(top, axis=1, keepdims=True)
    factor = jnp.exp2(top - peak)
    weight = factor * total[:, window]
    columns = signed(iota((1, P_SIZE), 1))
    bottom = jnp.sum(weight, axis=1, keepdims=True)
    along_rows = jnp.sum(factor * moment[:, window], axis=1, keepdims=True)
    along_columns = jnp.sum(weight * columns, axis=1, keepdims=True)
    return along_rows / bottom, along_columns / bottom


ROW_PARTS = ((0, 8, True), (8, HALF, False))


def quads(block, group):
    lane = group * 2 * LANES
    top, bottom = block[:HALF], block[HALF:]
    return (
        top[:, lane : lane + LANES],
        top[:, lane + LANES : lane + 2 * LANES],
        bottom[:, lane : lane + LANES],
        bottom[:, lane + LANES : lane + 2 * LANES],
    )


def unpack(packed):
    wide = packed.astype(f32)
    return jnp.concatenate([wide, pltpu.roll(wide, P_SIZE, axis=1)], axis=0).astype(bf16)


def prepare_kernel(tile_ref, out_ref, low_ref, packed_ref, sem):
    rows, width = tile_ref.shape
    columns = width // DOWN
    chunk = rows // PARTS
    copies = []
    for n in range(PARTS):
        at = pl.ds(n * chunk, chunk)
        copies.append(pltpu.make_async_copy(tile_ref.at[at], out_ref.at[at], sem.at[n]))
        copies[-1].start()
    pick = (iota((width, LANES), 0) // DOWN == iota((width, LANES), 1) % columns).astype(bf16)
    left = iota((columns // 2, LANES), 1) < P_SIZE
    sums = []
    for n in range(PARTS):
        copies[n].wait()
        part = matmul(out_ref[n * chunk : (n + 1) * chunk], pick)
        sums.append(jnp.sum(part.reshape(chunk // DOWN, DOWN, LANES), axis=1))
    coarse = jnp.concatenate(sums, axis=0) / DOWN
    half = coarse.shape[0] // 2
    packed_ref[:half] = jnp.where(left, coarse[:half], coarse[half:]).astype(bf16)
    low_ref[...] = out_ref[:P_SIZE]
    edge = out_ref[:, :LANES].astype(f32)
    half_rows = rows // 2
    left = iota((half_rows, LANES), 1) < P_SIZE
    edge = jnp.where(left, edge[:half_rows], pltpu.roll(edge[half_rows:], P_SIZE, axis=1))
    packed_ref[half:] = edge.astype(bf16)


def tables_kernel(
    offsets_in,
    weights_ref,
    rows_ref,
    picks_ref,
    chosen_ref,
    forward_rows_ref,
    inverse_ref,
    inverse_rows_ref,
    offsets_ref,
    sem,
):
    copy = pltpu.make_async_copy(offsets_in, offsets_ref, sem)
    copy.start()
    count = lax.axis_size("gx")
    bands, per_row = chosen_ref.shape
    supers = per_row // GROUP
    side = lax.axis_index("gz")
    gx_place = lax.axis_index("gx")
    shape = (2 * P_SIZE, LANES)
    lane = iota(shape, 1)
    row = iota(shape, 0)
    values = jnp.where(
        row // P_SIZE == lane % P_SIZE // HALF,
        basis_values(lane % HALF, lane // P_SIZE, row % P_SIZE),
        0.0,
    )
    padded = jnp.concatenate([values, jnp.zeros((2 * P_SIZE, LANES), f32)], axis=0)
    shape = (P_SIZE, LANES)
    row = iota(shape, 0)
    lane = iota(shape, 1)
    basis = basis_values(row % HALF, row // HALF, lane % P_SIZE)
    high, low = split(basis)
    forward_rows_ref[:P_SIZE] = high
    forward_rows_ref[P_SIZE:] = jnp.where(lane < P_SIZE, low.astype(f32), 0.0).astype(bf16)
    wide_high = jnp.concatenate([high.astype(f32)] * 2, axis=1)
    wide_low = jnp.concatenate([low.astype(f32)] * 2, axis=1)
    for kind in range(2):
        rows = slice(kind * HALF, (kind + 1) * HALF)
        for patch in range(GROUP):
            mine = iota((HALF, GROUP * P_SIZE), 1) // P_SIZE == patch
            at = (kind * GROUP + patch) * HALF
            for part, value in enumerate((wide_high, wide_low)):
                inverse_ref[at : at + HALF, part * 2 * LANES : (part + 1) * 2 * LANES] = jnp.where(
                    mine, value[rows], 0.0
                ).astype(bf16)
    high, low = split(basis_values(lane % HALF, lane % P_SIZE // HALF, row))
    inverse_rows_ref[:P_SIZE] = high
    inverse_rows_ref[P_SIZE:] = jnp.where(lane < P_SIZE, low.astype(f32), 0.0).astype(bf16)
    copy.wait()
    row_offset = offsets_ref[0]
    column_offset = offsets_ref[1]
    coarse_offset = offsets_ref[2]
    shifts = [column_offset + STRIDE * ((t + side) % 2) for t in range(2)] + [coarse_offset]
    for t, shift in enumerate(shifts):
        moved = pltpu.roll(padded, shift, axis=0)
        for part, value in enumerate(split(moved)):
            weights_ref[t, :, part * LANES : (part + 1) * LANES] = value
            value = pltpu.roll(value.astype(f32), P_SIZE, axis=1).astype(bf16)
            weights_ref[t, :, (part + 2) * LANES : (part + 3) * LANES] = value
    shape = (P_SIZE, 6 * STRIDE)
    number = iota(shape, 0)
    lane = iota(shape, 1)
    place = lane // P_SIZE * STRIDE + lane % STRIDE - row_offset
    values = jnp.where(
        (place >= 0) & (place < P_SIZE), basis_values(number % HALF, number // HALF, place), 0.0
    )
    high, low = split(values)
    is_low = lane % P_SIZE >= STRIDE
    rows_ref[:P_SIZE] = high
    rows_ref[P_SIZE:] = jnp.where(is_low, 0.0, low.astype(f32)).astype(bf16)
    def pick(column):
        centre = (gx_place * (2 * per_row) + column) * STRIDE + column_offset + P_SIZE // 2
        return jnp.clip((centre // DOWN - coarse_offset) // P_SIZE, 0, count - 1)

    lane_row = iota((1, LANES), 1)
    for t in range(2):
        for g in range(supers):
            column = 2 * (g * GROUP + lane_row // HALF) + (t + side) % 2
            picks_ref[t, g] = jnp.broadcast_to(pick(column), (8, LANES))
    shape = (bands, per_row)
    parity = (iota(shape, 0) + side) % 2
    chosen_ref[...] = pick(2 * iota(shape, 1) + parity)


def forward_bands(image, stacked, weights, left_rows, first_band, out_ref):
    bands = out_ref.shape[0]
    tall = image.shape[1]
    wide = out_ref.shape[2]
    blocks = tall // STRIDE
    supers = wide // (2 * LANES)
    left = iota((tall, LANES), 1) < P_SIZE
    for s in range(2):
        for t in range(2):
            for g in range(supers):
                lane = g * 2 * LANES
                a = matmul(image[s, :, lane : lane + 2 * LANES], weights[t, :, : 2 * LANES])
                b = matmul(image[s, :, lane + LANES : lane + 3 * LANES], weights[t, :, 2 * LANES :])
                a = a[:, :LANES] + a[:, LANES:]
                b = b[:, :LANES] + b[:, LANES:]
                for part, value in enumerate(
                    (jnp.where(left, a, b), pltpu.roll(jnp.where(left, b, a), P_SIZE, axis=1))
                ):
                    high, low = split(value)
                    at = slice(lane + part * LANES, lane + (part + 1) * LANES)
                    for n in range(blocks):
                        block = slice(n * STRIDE, (n + 1) * STRIDE)
                        stacked[s, t, 2 * n * STRIDE : (2 * n + 1) * STRIDE, at] = high[block]
                        stacked[s, t, (2 * n + 1) * STRIDE : (2 * n + 2) * STRIDE, at] = low[block]
    sign = jnp.where(lax.axis_index("gz") == 0, 1.0, -1.0).astype(f32)
    for i in range(bands):
        spectra = []
        for s in range(2):
            window = stacked[s, (first_band + i) % 2, 2 * STRIDE * i : 2 * STRIDE * (i + 3), :]
            spectra.append(add_row_halves(matmul(left_rows, window)))
        for g in range(supers):
            lane = g * 2 * LANES
            own = quads(spectra[0], g)
            other = quads(spectra[1], g)
            for begin, end, first in ROW_PARTS:
                out = cross_spectra(
                    [x[begin:end] for x in own], [x[begin:end] for x in other], sign, first
                )
                out_ref[i, begin:end, lane : lane + LANES] = out[0]
                out_ref[i, begin:end, lane + LANES : lane + 2 * LANES] = out[1]
                out_ref[i, HALF + begin : HALF + end, lane : lane + LANES] = out[2]
                out_ref[i, HALF + begin : HALF + end, lane + LANES : lane + 2 * LANES] = out[3]


def is_last(axis):
    return lax.axis_index(axis) == lax.axis_size(axis) - 1


def upper_kernel(group, weights, left_rows_ref, own_ref, other_ref, *refs):
    rights, (out_ref, image, stacked) = refs[:-3], refs[-3:]
    lane = group * 2 * LANES
    wide = 2 * LANES if rights else 3 * LANES
    for s, main in enumerate((own_ref, other_ref)):
        image[s, :, :wide] = main[:, lane : lane + wide]
        if rights:
            image[s, :, wide:] = unpack(rights[s][...])
    if rights:

        @pl.when(is_last("gx"))
        def _():
            image[:, :, wide:] = jnp.zeros((2, image.shape[1], LANES), bf16)

    forward_bands(image, stacked, weights, left_rows_ref[...], 0, out_ref)


def lower_kernel(
    weights,
    left_rows_ref,
    own_ref,
    own_right_ref,
    own_low_ref,
    other_ref,
    other_right_ref,
    other_low_ref,
    out_ref,
    image,
    stacked,
):
    rows, width = own_ref.shape
    for s, (main, right, low) in enumerate(
        ((own_ref, own_right_ref, own_low_ref), (other_ref, other_right_ref, other_low_ref))
    ):
        image[s, :P_SIZE, :width] = main[rows - P_SIZE :]
        edge = right[rows // 2 - P_SIZE :].astype(f32)
        image[s, :P_SIZE, width:] = pltpu.roll(edge, P_SIZE, axis=1).astype(bf16)
        image[s, P_SIZE:] = low[...]

    @pl.when(is_last("gx"))
    def _():
        image[:, :, width:] = jnp.zeros((2, 2 * P_SIZE, LANES), bf16)

    @pl.when(is_last("gy"))
    def _():
        image[:, P_SIZE:, :] = jnp.zeros((2, P_SIZE, width + LANES), bf16)

    forward_bands(
        image, stacked, weights, left_rows_ref[...], rows // STRIDE - out_ref.shape[0], out_ref
    )


def inverse_columns(high, low, table_ref):
    table_high = table_ref[:, : 2 * LANES]
    table_low = table_ref[:, 2 * LANES :]
    return matmul(high, table_high) + matmul(high, table_low) + matmul(low, table_high)


def coarse_peaks(strip, forward_rows_ref, inverse_ref, inverse_rows_ref, weights, sign):
    supers = len(strip) * 2 // GROUP
    left = iota((2 * P_SIZE, LANES), 1) < P_SIZE
    strip = strip + [jnp.zeros_like(strip[0])]
    columns = []
    for g in range(supers):
        a, b = (
            matmul(
                jnp.concatenate(strip[2 * g + n : 2 * g + n + 2], axis=1),
                weights[:, 2 * n * LANES : 2 * (n + 1) * LANES],
            )
            for n in range(2)
        )
        a = a[:, :LANES] + a[:, LANES:]
        b = b[:, :LANES] + b[:, LANES:]
        columns += [jnp.where(left, a, b), pltpu.roll(jnp.where(left, b, a), P_SIZE, axis=1)]
    strips = jnp.concatenate(columns, axis=1)
    spectra = []
    for s in range(2):
        high, low = split(strips[s * P_SIZE : (s + 1) * P_SIZE])
        stack = jnp.concatenate([high, low], axis=0)
        spectra.append(add_row_halves(matmul(forward_rows_ref[...], stack)))
    peaks = []
    for g in range(supers):
        own = quads(spectra[0], g)
        other = quads(spectra[1], g)
        parts = []
        for begin, end, first in ROW_PARTS:
            shape = (end - begin, LANES)
            values = cross_spectra([x[begin:end] for x in own], [x[begin:end] for x in other], sign, first)
            corner = first_lane(shape) & (iota(shape, 0) == 0) & first
            turn = [
                jnp.where(corner, SCALE, c).astype(f32)
                for c in (2.0 * SCALE, 0.0, 2.0 * SCALE, 0.0)
            ]
            parts.append(coefficients(values, turn, first))
        cc, cs, sc, ss = (jnp.concatenate([a, b], axis=0) for a, b in zip(*parts))
        block = jnp.concatenate(
            [jnp.concatenate([cc, cs], axis=1), jnp.concatenate([sc, ss], axis=1)], axis=0
        )
        high, low = split(block)
        high, low = split(inverse_columns(high, low, inverse_ref))
        stack = jnp.concatenate([high, low], axis=0)
        sums = column_sums(add_row_halves(matmul(inverse_rows_ref[...], stack)))
        peaks += [patch_peak(*sums, n) for n in range(GROUP)]
    return peaks


def turn_kernel(
    forward_rows_ref,
    inverse_ref,
    inverse_rows_ref,
    weights,
    picks_ref,
    chosen_ref,
    own_part_ref,
    other_part_ref,
    turns,
    base_ref,
    ordered,
):
    count = ordered.shape[0]
    supers = turns.shape[1]
    side = lax.axis_index("gz")
    place = lax.axis_index("gx")
    sign = jnp.where(side == 0, 1.0, -1.0).astype(f32)
    for step in range(count):
        for part, ref in enumerate((own_part_ref, other_part_ref)):
            tile = ref[step * HALF : (step + 1) * HALF].astype(f32)
            tile = jnp.concatenate([tile, pltpu.roll(tile, P_SIZE, axis=1)], axis=0)
            ordered[place ^ step, part * P_SIZE : (part + 1) * P_SIZE] = tile
    left = iota((2 * P_SIZE, LANES), 1) < P_SIZE
    strip = []
    for j in range(0, count, 2):
        both = jnp.where(left, ordered[j], pltpu.roll(ordered[j + 1], P_SIZE, axis=1))
        strip.append(both.astype(bf16))
    peaks = coarse_peaks(
        strip, forward_rows_ref, inverse_ref, inverse_rows_ref, weights.at[2], sign
    )
    blended = []
    for axis in range(2):
        values = [peak[axis] for peak in peaks]
        mean = sum(values[1:], values[0]) / count
        blended.append([(0.5 * DOWN) * (value + mean) for value in values])

    def prior(pick):
        out = []
        for values in blended:
            chosen = jnp.broadcast_to(values[0], pick.shape)
            for j in range(1, count):
                chosen = jnp.where(pick == j, values[j], chosen)
            out.append(chosen)
        return out

    shape = (HALF, LANES)
    frequency_y = iota(shape, 0).astype(f32) / P_SIZE
    l0 = first_lane(shape)
    r0 = iota(shape, 0) == 0
    lane_row = iota((1, LANES), 1)
    frequency_x = (lane_row % HALF).astype(f32) / P_SIZE
    for t in range(2):
        for g in range(supers):
            dy, dx = (
                value - P_SIZE * jnp.round(value / P_SIZE) for value in prior(picks_ref[t, g, :1])
            )
            turn_y = nearest(frequency_y * dy)
            turn_x = nearest(frequency_x * dx)
            cy, sy = cosine_of_turns(turn_y), sine_of_turns(turn_y)
            cx, sx = cosine_of_turns(turn_x), sine_of_turns(turn_x)
            half_y = cosine_of_turns(nearest(0.5 * dy))
            half_x = cosine_of_turns(nearest(0.5 * dx))
            half_both = cosine_of_turns(nearest(0.5 * (dy + dx)))
            plus_real = cy * cx - sy * sx
            plus_imaginary = sy * cx + cy * sx
            minus_real = cy * cx + sy * sx
            minus_imaginary = sy * cx - cy * sx
            minus_real = jnp.where(l0, cy * half_x, jnp.where(r0, cx * half_y, minus_real))
            minus_imaginary = jnp.where(l0, sy * half_x, jnp.where(r0, sx * half_y, minus_imaginary))
            corner = l0 & r0
            turn = (plus_real, plus_imaginary, minus_real, minus_imaginary)
            ends = (1.0, half_x, half_y, half_both)
            for n in range(4):
                turns[t, g, n] = SCALE * jnp.where(corner, ends[n], 2.0 * turn[n])
    base = prior(chosen_ref[...])
    for axis in range(2):
        base_ref[axis] = base[axis]


def peak_kernel(
    first_band,
    inverse_ref,
    inverse_rows_ref,
    mask_ref,
    base_ref,
    turns,
    *refs,
):
    spectra, (out_ref, high_ref, low_ref, stacked) = refs[:-4], refs[-4:]
    supers = turns.shape[1]
    per_row = supers * GROUP
    bands = spectra[0].shape[0]
    for i in range(bands):
        for g in range(supers):
            lane = g * 2 * LANES
            values = quads(spectra[g][i], 0) if len(spectra) > 1 else quads(spectra[0][i], g)
            for begin, end, first in ROW_PARTS:
                parts = coefficients(
                    [x[begin:end] for x in values],
                    [turns[(first_band + i) % 2, g, n, begin:end] for n in range(4)],
                    first,
                )
                stacked[begin:end, lane : lane + LANES] = parts[0]
                stacked[begin:end, lane + LANES : lane + 2 * LANES] = parts[1]
                stacked[HALF + begin : HALF + end, lane : lane + LANES] = parts[2]
                stacked[HALF + begin : HALF + end, lane + LANES : lane + 2 * LANES] = parts[3]
        high, low = split(stacked[...])
        high_ref[i * P_SIZE : (i + 1) * P_SIZE] = high
        low_ref[i * P_SIZE : (i + 1) * P_SIZE] = low
    for g in range(supers):
        at = slice(g * 2 * LANES, (g + 1) * 2 * LANES)
        high, low = split(inverse_columns(high_ref[:, at], low_ref[:, at], inverse_ref))
        high_ref[:, at] = high
        low_ref[:, at] = low
    sums = []
    for i in range(bands):
        rows = slice(i * P_SIZE, (i + 1) * P_SIZE)
        stack = jnp.concatenate([high_ref[rows], low_ref[rows]], axis=0)
        sums.append(column_sums(add_row_halves(matmul(inverse_rows_ref[...], stack))))
    sums = [jnp.concatenate(parts, axis=0) for parts in zip(*sums)]
    lane = iota((bands, LANES), 1)
    found = [jnp.zeros((bands, LANES), f32) for _ in range(2)]
    for m in range(per_row):
        peak = patch_peak(*sums, m)
        found = [jnp.where(lane == m, p, x) for p, x in zip(peak, found)]
    shape = (2 * per_row, per_row)
    columns = iota(shape, 0) - 2 * iota(shape, 1)
    mask = mask_ref[first_band : first_band + bands].astype(f32).astype(bf16)
    masks = [matmul(mask, (columns == n).astype(bf16)) for n in range(2)]
    parity = (iota((bands, per_row), 0) + (first_band + lax.axis_index("gz"))) % 2
    chosen = jnp.where(parity == 0, masks[0], masks[1])
    for axis in range(2):
        base = base_ref[axis, first_band : first_band + bands]
        flow = base + chosen * found[axis][:, :per_row]
        out_ref[axis] = jnp.transpose(flow)


def lower_peak_kernel(first_band, upper_flow_ref, *refs):
    out_ref, *scratch = refs[-5:]
    flow, scratch = scratch[-1], scratch[:-1]
    peak_kernel(first_band, *refs[:-5], flow, *scratch)
    for axis in range(2):
        out_ref[axis, 0] = jnp.concatenate([upper_flow_ref[axis], flow[axis]], axis=1)


def exchanged(value, axis, step):
    return lax.ppermute(value, axis, [(i, i ^ step) for i in range(lax.axis_size(axis))])


def from_later(value, axis, step):
    return lax.ppermute(value, axis, [(i, i - step) for i in range(step, lax.axis_size(axis))])


def swapped(value):
    return lax.ppermute(value, "gz", [(0, 1), (1, 0)])


VMEM = pl.BlockSpec(memory_space=pltpu.VMEM)
SMEM = pl.BlockSpec(memory_space=pltpu.SMEM)


def cost(microseconds):
    return pl.CostEstimate(
        flops=0, bytes_accessed=int(microseconds * 3.0e6), transcendentals=0
    )


def params(mebibytes):
    return pltpu.CompilerParams(vmem_limit_bytes=mebibytes * 2**20)


def local(sections, fine_offsets, coarse_offset, tissue_mask):
    own = sections[0]
    rows, width = own.shape
    bands = rows // STRIDE
    per_row = width // P_SIZE
    count = lax.axis_size("gx")
    assert rows == DOWN * P_SIZE and width == DOWN * P_SIZE
    assert count % GROUP == 0 and count & (count - 1) == 0
    wide = width
    supers = width // (2 * LANES)
    other = swapped(own)
    own_tile, own_edge, packed = pl.pallas_call(
        prepare_kernel,
        out_shape=(
            jax.ShapeDtypeStruct((rows, width), bf16),
            jax.ShapeDtypeStruct((P_SIZE, width), bf16),
            jax.ShapeDtypeStruct((HALF + rows // 2, LANES), bf16),
        ),
        in_specs=[pl.BlockSpec(memory_space=pltpu.HBM)],
        out_specs=(VMEM,) * 3,
        scratch_shapes=[pltpu.SemaphoreType.DMA((PARTS,))],
        compiler_params=params(16),
        cost_estimate=cost(5.0),
    )(own)
    tables = pl.pallas_call(
        tables_kernel,
        out_shape=(
            jax.ShapeDtypeStruct((3, 2 * LANES, 4 * LANES), bf16),
            jax.ShapeDtypeStruct((2 * P_SIZE, 6 * STRIDE), bf16),
            jax.ShapeDtypeStruct((2, supers, 8, LANES), jnp.int32),
            jax.ShapeDtypeStruct((bands, per_row), jnp.int32),
            jax.ShapeDtypeStruct((2 * P_SIZE, LANES), bf16),
            jax.ShapeDtypeStruct((2 * LANES, 4 * LANES), bf16),
            jax.ShapeDtypeStruct((2 * P_SIZE, LANES), bf16),
        ),
        in_specs=[pl.BlockSpec(memory_space=pl.ANY)],
        out_specs=(VMEM,) * 7,
        scratch_shapes=[pltpu.SMEM((3,), jnp.int32), pltpu.SemaphoreType.DMA],
        compiler_params=params(16),
        cost_estimate=cost(0.1),
    )(jnp.concatenate([fine_offsets, coarse_offset]))
    weights, left_rows, picks, chosen, forward_rows, inverse, inverse_rows = tables
    low_bands = P_SIZE // STRIDE
    uppers = []

    def upper(group, *operands):
        return pl.pallas_call(
            functools.partial(upper_kernel, group),
            out_shape=jax.ShapeDtypeStruct((bands - low_bands, P_SIZE, 2 * LANES), f32),
            in_specs=[VMEM] * (4 + len(operands)),
            out_specs=VMEM,
            scratch_shapes=[
                pltpu.VMEM((2, rows, 3 * LANES), bf16),
                pltpu.VMEM((2, 2, 2 * rows, 2 * LANES), bf16),
            ],
            compiler_params=params(32),
            cost_estimate=cost(0.1),
        )(weights, left_rows, own_tile, other, *operands)

    got_even = exchanged(packed, "gx", 1)
    got_odd = lax.ppermute(packed[HALF:], "gx", [(i + 1, i) for i in range(1, count - 1, 2)])
    tiles = jnp.concatenate([packed[:HALF], got_even[:HALF]], axis=0)
    step = 2
    while 2 * step < count:
        tiles = jnp.concatenate([tiles, exchanged(tiles, "gx", step)], axis=0)
        step *= 2
    last_tiles = exchanged(tiles, "gx", step)
    right = jnp.where(lax.axis_index("gx") % 2 == 0, got_even[HALF:], got_odd)
    other_right = swapped(right)
    low_payload = jnp.concatenate([own_edge, right[:P_SIZE]], axis=1)
    low_payload, other_right = lax.optimization_barrier((low_payload, other_right))
    own_low = from_later(low_payload, "gy", 1)
    uppers = [upper(group) for group in range(supers - 1)]
    last_tiles, *uppers = lax.optimization_barrier((last_tiles, *uppers))
    tiles = jnp.concatenate([tiles, last_tiles], axis=0)
    other_tiles = swapped(tiles)
    uppers.append(upper(supers - 1, right, other_right))
    other_tiles, *uppers = lax.optimization_barrier((other_tiles, *uppers))
    turns, base = pl.pallas_call(
        turn_kernel,
        out_shape=(
            jax.ShapeDtypeStruct((2, supers, 4, HALF, LANES), f32),
            jax.ShapeDtypeStruct((2, bands, per_row), f32),
        ),
        in_specs=[VMEM] * 8,
        out_specs=(VMEM,) * 2,
        scratch_shapes=[pltpu.VMEM((count, 2 * P_SIZE, LANES), f32)],
        compiler_params=params(32),
        cost_estimate=cost(0.1),
    )(
        forward_rows,
        inverse,
        inverse_rows,
        weights,
        picks,
        chosen,
        tiles,
        other_tiles,
    )
    def peak_scratch(count):
        return [
            pltpu.VMEM((count * P_SIZE, wide), bf16),
            pltpu.VMEM((count * P_SIZE, wide), bf16),
            pltpu.VMEM((P_SIZE, wide), f32),
        ]

    upper_bands = bands - low_bands
    own_low, turns = lax.optimization_barrier((own_low, turns))
    other_low = swapped(own_low)
    upper_flow = pl.pallas_call(
        functools.partial(peak_kernel, 0),
        out_shape=jax.ShapeDtypeStruct((2, per_row, upper_bands), f32),
        in_specs=[VMEM] * (5 + supers),
        out_specs=VMEM,
        scratch_shapes=peak_scratch(upper_bands),
        compiler_params=params(40),
        cost_estimate=cost(0.1),
    )(inverse, inverse_rows, tissue_mask, base, turns, *uppers)
    other_low, upper_flow = lax.optimization_barrier((other_low, upper_flow))
    lower = pl.pallas_call(
        lower_kernel,
        out_shape=jax.ShapeDtypeStruct((low_bands, P_SIZE, wide), f32),
        in_specs=[VMEM] * 8,
        out_specs=VMEM,
        scratch_shapes=[
            pltpu.VMEM((2, 2 * P_SIZE, width + LANES), bf16),
            pltpu.VMEM((2, 2, 4 * P_SIZE, wide), bf16),
        ],
        compiler_params=params(32),
        cost_estimate=cost(0.1),
    )(weights, left_rows, own_tile, right, own_low, other, other_right, other_low)
    flow = pl.pallas_call(
        functools.partial(lower_peak_kernel, upper_bands),
        out_shape=jax.ShapeDtypeStruct((2, 1, per_row, bands), f32),
        in_specs=[VMEM] * 7,
        out_specs=VMEM,
        scratch_shapes=peak_scratch(low_bands) + [pltpu.VMEM((2, per_row, low_bands), f32)],
        compiler_params=params(40),
        cost_estimate=cost(0.1),
    )(upper_flow, inverse, inverse_rows, tissue_mask, base, turns, lower)
    return jnp.swapaxes(flow, 2, 3)


def solution(mesh):
    placed = (P("gz", ("pairs", "gy"), "gx"), P("pairs"), P("pairs"), P(("pairs", "gy"), "gx"))
    return jax.shard_map(
        local,
        mesh=mesh,
        in_specs=placed,
        out_specs=P(None, "gz", ("pairs", "gy"), "gx"),
        check_vma=False,
    )
```

```python
import functools
import math

import jax
import jax.numpy as jnp
from jax import lax
from jax.experimental import pallas as pl
from jax.experimental.pallas import tpu as pltpu
from jax.sharding import PartitionSpec as P

P_SIZE = 64
HALF = P_SIZE // 2
STRIDE = 32
DOWN = 8
LANES = 128
GROUP = LANES // HALF
SHARPNESS = 12.0
PARTS = 1
SCALE = SHARPNESS / float(P_SIZE) ** 4 * math.log2(math.e)

f32 = jnp.float32
bf16 = jnp.bfloat16


def cosine_of_turns(turns):
    square = (turns * (2.0 * math.pi)) ** 2
    total = jnp.full_like(square, 1.0 / math.factorial(20))
    for n in range(9, -1, -1):
        total = total * square + (-1.0) ** n / math.factorial(2 * n)
    return total


def sine_of_turns(turns):
    angle = turns * (2.0 * math.pi)
    square = angle * angle
    total = jnp.full_like(square, -1.0 / math.factorial(19))
    for n in range(8, -1, -1):
        total = total * square + (-1.0) ** n / math.factorial(2 * n + 1)
    return total * angle


def nearest(turns):
    return turns - jnp.round(turns)


def basis_values(frequency, kind, place):
    nyquist = (kind == 1) & (frequency == 0)
    number = jnp.where(nyquist, HALF, frequency)
    quarter = jnp.where((kind == 1) & (frequency != 0), P_SIZE // 4, 0)
    step = (number * place - quarter) & (P_SIZE - 1)
    step = jnp.where(step > HALF, P_SIZE - step, step)
    flip = step > P_SIZE // 4
    step = jnp.where(flip, HALF - step, step)
    square = (step.astype(f32) * (2.0 * math.pi / P_SIZE)) ** 2
    total = jnp.full_like(square, 1.0 / math.factorial(12))
    for n in range(5, -1, -1):
        total = total * square + (-1.0) ** n / math.factorial(2 * n)
    return jnp.where(flip, -total, total)


def iota(shape, axis):
    return lax.broadcasted_iota(jnp.int32, shape, axis)


def split(values):
    high = values.astype(bf16)
    return high, (values - high.astype(f32)).astype(bf16)


def matmul(left, right):
    return jnp.dot(left, right, preferred_element_type=f32)


def add_row_halves(values):
    half = values.shape[0] // 2
    return values[:half] + values[half:]


def first_lane(shape):
    return iota(shape, 1) % HALF == 0


def half_spectra(cc, cs, sc, ss, first):
    shape = cc.shape
    l0 = first_lane(shape)
    if not first:
        return (
            cc - jnp.where(l0, 0.0, ss),
            sc + jnp.where(l0, 0.0, cs),
            jnp.where(l0, cs, cc + ss),
            jnp.where(l0, ss, sc - cs),
        )
    r0 = iota(shape, 0) == 0
    either = l0 | r0
    return (
        cc - jnp.where(either, 0.0, ss),
        jnp.where(r0, 0.0, sc) + jnp.where(l0, 0.0, cs),
        jnp.where(l0, cs, jnp.where(r0, sc, cc + ss)),
        jnp.where(either, ss, sc - cs),
    )


def cross_spectra(own, other, sign, first):
    a = half_spectra(*own, first)
    b = half_spectra(*other, first)
    out = []
    for r, i in ((0, 1), (2, 3)):
        out.append(b[r] * a[r] + b[i] * a[i])
        out.append(sign * (b[r] * a[i] - b[i] * a[r]))
    if first:
        shape = own[0].shape
        corner = first_lane(shape) & (iota(shape, 0) == 0)
        out = [jnp.where(corner, x * y, o) for x, y, o in zip(own, other, out)]
    return out


def coefficients(g, t, first):
    gpr, gpi, gmr, gmi = g
    tpr, tpi, tmr, tmi = t
    shape = gpr.shape
    l0 = first_lane(shape)
    hpr = gpr * tpr - gpi * tpi
    hpi = gpr * tpi + gpi * tpr
    hmr = gmr * tmr - gmi * tmi
    hmi = gmr * tmi + gmi * tmr
    if not first:
        return (
            hpr + jnp.where(l0, 0.0, hmr),
            jnp.where(l0, hmr, hmi - hpi),
            -hpi - jnp.where(l0, 0.0, hmi),
            jnp.where(l0, -hmi, hmr - hpr),
        )
    r0 = iota(shape, 0) == 0
    either = l0 | r0
    corner = l0 & r0
    out = (
        hpr + jnp.where(either, 0.0, hmr),
        jnp.where(l0, hmr, jnp.where(r0, 0.0, hmi) - hpi),
        jnp.where(r0, hmr, -hpi - jnp.where(l0, 0.0, hmi)),
        jnp.where(either, -hmi, hmr - hpr),
    )
    return [jnp.where(corner, x * y, o) for x, y, o in zip(g, t, out)]


def signed(number):
    return jnp.where(number >= HALF, number - P_SIZE, number).astype(f32)


def column_sums(logits):
    largest = jnp.max(logits, axis=0, keepdims=True)
    weights = jnp.exp2(logits - largest)
    rows = signed(iota((P_SIZE, 1), 0))
    return largest, jnp.sum(weights, axis=0, keepdims=True), jnp.sum(weights * rows, axis=0, keepdims=True)


def patch_peak(largest, total, moment, patch):
    window = slice(patch * P_SIZE, (patch + 1) * P_SIZE)
    top = largest[:, window]
    peak = jnp.max(top, axis=1, keepdims=True)
    factor = jnp.exp2(top - peak)
    weight = factor * total[:, window]
    columns = signed(iota((1, P_SIZE), 1))
    bottom = jnp.sum(weight, axis=1, keepdims=True)
    along_rows = jnp.sum(factor * moment[:, window], axis=1, keepdims=True)
    along_columns = jnp.sum(weight * columns, axis=1, keepdims=True)
    return along_rows / bottom, along_columns / bottom


def band_peaks(largest, total, moment):
    bands, wide = largest.shape
    largest, total, moment = (
        jnp.transpose(x).reshape(wide // P_SIZE, P_SIZE, bands) for x in (largest, total, moment)
    )
    factor = jnp.exp2(largest - jnp.max(largest, axis=1, keepdims=True))
    weight = factor * total
    columns = signed(lax.broadcasted_iota(jnp.int32, (1, P_SIZE, 1), 1))
    bottom = jnp.sum(weight, axis=1)
    return jnp.sum(factor * moment, axis=1) / bottom, jnp.sum(weight * columns, axis=1) / bottom


ROW_PARTS = ((0, 8, True), (8, HALF, False))


def quads(block, group):
    lane = group * 2 * LANES
    top, bottom = block[:HALF], block[HALF:]
    return (
        top[:, lane : lane + LANES],
        top[:, lane + LANES : lane + 2 * LANES],
        bottom[:, lane : lane + LANES],
        bottom[:, lane + LANES : lane + 2 * LANES],
    )


def unpack(packed):
    wide = packed.astype(f32)
    return jnp.concatenate([wide, pltpu.roll(wide, P_SIZE, axis=1)], axis=0).astype(bf16)


def prepare_kernel(tile_ref, out_ref, low_ref, packed_ref, sem):
    rows, width = tile_ref.shape
    columns = width // DOWN
    chunk = rows // PARTS
    copies = []
    for n in range(PARTS):
        at = pl.ds(n * chunk, chunk)
        copies.append(pltpu.make_async_copy(tile_ref.at[at], out_ref.at[at], sem.at[n]))
        copies[-1].start()
    pick = (iota((width, LANES), 0) // DOWN == iota((width, LANES), 1) % columns).astype(bf16)
    left = iota((columns // 2, LANES), 1) < P_SIZE
    sums = []
    for n in range(PARTS):
        copies[n].wait()
        part = matmul(out_ref[n * chunk : (n + 1) * chunk], pick)
        sums.append(jnp.sum(part.reshape(chunk // DOWN, DOWN, LANES), axis=1))
    coarse = jnp.concatenate(sums, axis=0) / DOWN
    half = coarse.shape[0] // 2
    packed_ref[:half] = jnp.where(left, coarse[:half], coarse[half:]).astype(bf16)
    low_ref[...] = out_ref[:P_SIZE]
    edge = out_ref[:, :LANES].astype(f32)
    half_rows = rows // 2
    left = iota((half_rows, LANES), 1) < P_SIZE
    edge = jnp.where(left, edge[:half_rows], pltpu.roll(edge[half_rows:], P_SIZE, axis=1))
    packed_ref[half:] = edge.astype(bf16)


def beside(high, low):
    left = iota(high.shape, 1) < P_SIZE
    return jnp.concatenate([high, jnp.where(left, low, 0.0)], axis=1).astype(bf16)


def tables_kernel(
    offsets_in,
    weights_ref,
    coarse_weights_ref,
    rows_ref,
    picks_ref,
    chosen_ref,
    forward_rows_ref,
    inverse_ref,
    inverse_rows_ref,
    offsets_ref,
    sem,
):
    copy = pltpu.make_async_copy(offsets_in, offsets_ref, sem)
    copy.start()
    count = lax.axis_size("gx")
    per_row, bands = chosen_ref.shape
    supers = per_row // GROUP
    side = lax.axis_index("gz")
    gx_place = lax.axis_index("gx")
    shape = (2 * P_SIZE, LANES)
    lane = iota(shape, 1)
    row = iota(shape, 0)
    values = jnp.where(
        row // P_SIZE == lane % P_SIZE // HALF,
        basis_values(lane % HALF, lane // P_SIZE, row % P_SIZE),
        0.0,
    )
    padded = jnp.concatenate([values, jnp.zeros((2 * P_SIZE, LANES), f32)], axis=0)
    shape = (P_SIZE, LANES)
    row = iota(shape, 0)
    lane = iota(shape, 1)
    basis = basis_values(row % HALF, row // HALF, lane % P_SIZE)
    high, low = (value.astype(f32) for value in split(basis))
    forward_rows_ref[...] = beside(high, low)
    wide_high = jnp.concatenate([high] * 2, axis=1)
    wide_low = jnp.concatenate([low] * 2, axis=1)
    for kind in range(2):
        rows = slice(kind * HALF, (kind + 1) * HALF)
        for patch in range(GROUP):
            mine = iota((HALF, GROUP * P_SIZE), 1) // P_SIZE == patch
            at = (kind * GROUP + patch) * HALF
            for part, value in enumerate((wide_high, wide_high, wide_low)):
                begin = at + part * 2 * LANES
                inverse_ref[begin : begin + HALF] = jnp.where(mine, value[rows], 0.0).astype(bf16)
    high, low = split(basis_values(lane % HALF, lane % P_SIZE // HALF, row))
    inverse_rows_ref[...] = beside(high.astype(f32), low.astype(f32))
    copy.wait()
    row_offset = offsets_ref[0]
    column_offset = offsets_ref[1]
    coarse_offset = offsets_ref[2]
    shifts = [column_offset + STRIDE * ((t + side) % 2) for t in range(2)] + [coarse_offset]
    for t, shift in enumerate(shifts):
        moved = pltpu.roll(padded, shift, axis=0)
        for part, value in enumerate(split(moved)):
            rows = slice(part * 2 * LANES, (part + 1) * 2 * LANES)
            turned = pltpu.roll(value.astype(f32), P_SIZE, axis=1).astype(bf16)
            for order, entry in enumerate((value, turned)):
                if t < 2:
                    weights_ref[order, rows, t * LANES : (t + 1) * LANES] = entry
                else:
                    coarse_weights_ref[order, rows] = entry
    shape = (P_SIZE, 6 * STRIDE)
    number = iota(shape, 0)
    lane = iota(shape, 1)
    place = lane // P_SIZE * STRIDE + lane % STRIDE - row_offset
    values = jnp.where(
        (place >= 0) & (place < P_SIZE), basis_values(number % HALF, number // HALF, place), 0.0
    )
    high, low = split(values)
    is_low = lane % P_SIZE >= STRIDE
    rows_ref[:P_SIZE] = high
    rows_ref[P_SIZE:] = jnp.where(is_low, 0.0, low.astype(f32)).astype(bf16)
    def pick(column):
        centre = (gx_place * (2 * per_row) + column) * STRIDE + column_offset + P_SIZE // 2
        return jnp.clip((centre // DOWN - coarse_offset) // P_SIZE, 0, count - 1)

    lane_row = iota((1, LANES), 1)
    for t in range(2):
        for g in range(supers):
            column = 2 * (g * GROUP + lane_row // HALF) + (t + side) % 2
            picks_ref[t, g] = jnp.broadcast_to(pick(column), (8, LANES))
    shape = (per_row, bands)
    parity = (iota(shape, 1) + side) % 2
    chosen_ref[...] = pick(2 * iota(shape, 0) + parity)


def column_transform(pixels, weights):
    out = []
    for order in range(2):
        part = pixels[:, order * LANES : (order + 2) * LANES]
        out.append(matmul(jnp.concatenate([part, part], axis=1), weights[order]))
    return out


def pair_up(a, b):
    left = iota(a.shape, 1) < P_SIZE
    return jnp.where(left, a, b), pltpu.roll(jnp.where(left, b, a), P_SIZE, axis=1)


def forward_bands(image, stacked, weights, left_rows, first_band, out_ref):
    bands = out_ref.shape[0]
    tall = image.shape[1]
    wide = out_ref.shape[2]
    blocks = tall // STRIDE
    supers = wide // (2 * LANES)
    for s in range(2):
        for g in range(supers):
            lane = g * 2 * LANES
            a, b = column_transform(image[s, :, lane : lane + 3 * LANES], weights)
            for t in range(2):
                half = slice(t * LANES, (t + 1) * LANES)
                for part, value in enumerate(pair_up(a[:, half], b[:, half])):
                    high, low = split(value)
                    at = slice(lane + part * LANES, lane + (part + 1) * LANES)
                    for n in range(blocks):
                        block = slice(n * STRIDE, (n + 1) * STRIDE)
                        stacked[s, t, 2 * n * STRIDE : (2 * n + 1) * STRIDE, at] = high[block]
                        stacked[s, t, (2 * n + 1) * STRIDE : (2 * n + 2) * STRIDE, at] = low[block]
    sign = jnp.where(lax.axis_index("gz") == 0, 1.0, -1.0).astype(f32)
    for i in range(bands):
        spectra = []
        for s in range(2):
            window = stacked[s, (first_band + i) % 2, 2 * STRIDE * i : 2 * STRIDE * (i + 3), :]
            spectra.append(add_row_halves(matmul(left_rows, window)))
        for g in range(supers):
            lane = g * 2 * LANES
            own = quads(spectra[0], g)
            other = quads(spectra[1], g)
            for begin, end, first in ROW_PARTS:
                out = cross_spectra(
                    [x[begin:end] for x in own], [x[begin:end] for x in other], sign, first
                )
                out_ref[i, begin:end, lane : lane + LANES] = out[0]
                out_ref[i, begin:end, lane + LANES : lane + 2 * LANES] = out[1]
                out_ref[i, HALF + begin : HALF + end, lane : lane + LANES] = out[2]
                out_ref[i, HALF + begin : HALF + end, lane + LANES : lane + 2 * LANES] = out[3]


def is_last(axis):
    return lax.axis_index(axis) == lax.axis_size(axis) - 1


def upper_kernel(group, weights, left_rows_ref, own_ref, other_ref, *refs):
    rights, (out_ref, image, stacked) = refs[:-3], refs[-3:]
    lane = group * 2 * LANES
    wide = 2 * LANES if rights else 3 * LANES
    for s, main in enumerate((own_ref, other_ref)):
        image[s, :, :wide] = main[:, lane : lane + wide]
        if rights:
            image[s, :, wide:] = unpack(rights[s][...])
    if rights:

        @pl.when(is_last("gx"))
        def _():
            image[:, :, wide:] = jnp.zeros((2, image.shape[1], LANES), bf16)

    forward_bands(image, stacked, weights, left_rows_ref[...], 0, out_ref)


def lower_kernel(
    weights,
    left_rows_ref,
    own_ref,
    own_right_ref,
    own_low_ref,
    other_ref,
    other_right_ref,
    other_low_ref,
    out_ref,
    image,
    stacked,
):
    rows, width = own_ref.shape
    for s, (main, right, low) in enumerate(
        ((own_ref, own_right_ref, own_low_ref), (other_ref, other_right_ref, other_low_ref))
    ):
        image[s, :P_SIZE, :width] = main[rows - P_SIZE :]
        edge = right[rows // 2 - P_SIZE :].astype(f32)
        image[s, :P_SIZE, width:] = pltpu.roll(edge, P_SIZE, axis=1).astype(bf16)
        image[s, P_SIZE:] = low[...]

    @pl.when(is_last("gx"))
    def _():
        image[:, :, width:] = jnp.zeros((2, 2 * P_SIZE, LANES), bf16)

    @pl.when(is_last("gy"))
    def _():
        image[:, P_SIZE:, :] = jnp.zeros((2, P_SIZE, width + LANES), bf16)

    forward_bands(
        image, stacked, weights, left_rows_ref[...], rows // STRIDE - out_ref.shape[0], out_ref
    )


def inverse_columns(high, low, table_ref):
    return matmul(jnp.concatenate([high, low, high], axis=1), table_ref[...])


def row_transform(table_ref, high, low):
    return matmul(table_ref[:, : 3 * P_SIZE], jnp.concatenate([high, low, high], axis=0))


def coarse_peaks(strip, forward_rows_ref, inverse_ref, inverse_rows_ref, weights, sign):
    supers = len(strip) * 2 // GROUP
    strip = strip + [jnp.zeros_like(strip[0])]
    columns = []
    for g in range(supers):
        columns += pair_up(
            *column_transform(jnp.concatenate(strip[2 * g : 2 * g + 3], axis=1), weights)
        )
    strips = jnp.concatenate(columns, axis=1)
    spectra = []
    for s in range(2):
        spectra.append(
            row_transform(forward_rows_ref, *split(strips[s * P_SIZE : (s + 1) * P_SIZE]))
        )
    peaks = []
    for g in range(supers):
        own = quads(spectra[0], g)
        other = quads(spectra[1], g)
        parts = []
        for begin, end, first in ROW_PARTS:
            shape = (end - begin, LANES)
            values = cross_spectra([x[begin:end] for x in own], [x[begin:end] for x in other], sign, first)
            corner = first_lane(shape) & (iota(shape, 0) == 0) & first
            turn = [
                jnp.where(corner, SCALE, c).astype(f32)
                for c in (2.0 * SCALE, 0.0, 2.0 * SCALE, 0.0)
            ]
            parts.append(coefficients(values, turn, first))
        cc, cs, sc, ss = (jnp.concatenate([a, b], axis=0) for a, b in zip(*parts))
        block = jnp.concatenate(
            [jnp.concatenate([cc, cs], axis=1), jnp.concatenate([sc, ss], axis=1)], axis=0
        )
        found = inverse_columns(*split(block), inverse_ref)
        sums = column_sums(row_transform(inverse_rows_ref, *split(found)))
        peaks += [patch_peak(*sums, n) for n in range(GROUP)]
    return peaks


def turn_kernel(
    forward_rows_ref,
    inverse_ref,
    inverse_rows_ref,
    weights,
    picks_ref,
    chosen_ref,
    own_part_ref,
    other_part_ref,
    turns,
    base_ref,
    ordered,
):
    count = ordered.shape[0]
    supers = turns.shape[1]
    side = lax.axis_index("gz")
    place = lax.axis_index("gx")
    sign = jnp.where(side == 0, 1.0, -1.0).astype(f32)
    for step in range(count):
        for part, ref in enumerate((own_part_ref, other_part_ref)):
            tile = ref[step * HALF : (step + 1) * HALF].astype(f32)
            tile = jnp.concatenate([tile, pltpu.roll(tile, P_SIZE, axis=1)], axis=0)
            ordered[place ^ step, part * P_SIZE : (part + 1) * P_SIZE] = tile
    left = iota((2 * P_SIZE, LANES), 1) < P_SIZE
    strip = []
    for j in range(0, count, 2):
        both = jnp.where(left, ordered[j], pltpu.roll(ordered[j + 1], P_SIZE, axis=1))
        strip.append(both.astype(bf16))
    peaks = coarse_peaks(
        strip, forward_rows_ref, inverse_ref, inverse_rows_ref, weights, sign
    )
    blended = []
    for axis in range(2):
        values = [peak[axis] for peak in peaks]
        mean = sum(values[1:], values[0]) / count
        blended.append([(0.5 * DOWN) * (value + mean) for value in values])

    def prior(pick):
        out = []
        for values in blended:
            chosen = jnp.broadcast_to(values[0], pick.shape)
            for j in range(1, count):
                chosen = jnp.where(pick == j, values[j], chosen)
            out.append(chosen)
        return out

    shape = (HALF, LANES)
    frequency_y = iota(shape, 0).astype(f32) / P_SIZE
    l0 = first_lane(shape)
    r0 = iota(shape, 0) == 0
    lane_row = iota((1, LANES), 1)
    frequency_x = (lane_row % HALF).astype(f32) / P_SIZE
    for t in range(2):
        for g in range(supers):
            dy, dx = (
                value - P_SIZE * jnp.round(value / P_SIZE) for value in prior(picks_ref[t, g, :1])
            )
            turn_y = nearest(frequency_y * dy)
            turn_x = nearest(frequency_x * dx)
            cy, sy = cosine_of_turns(turn_y), sine_of_turns(turn_y)
            cx, sx = cosine_of_turns(turn_x), sine_of_turns(turn_x)
            half_y = cosine_of_turns(nearest(0.5 * dy))
            half_x = cosine_of_turns(nearest(0.5 * dx))
            half_both = cosine_of_turns(nearest(0.5 * (dy + dx)))
            plus_real = cy * cx - sy * sx
            plus_imaginary = sy * cx + cy * sx
            minus_real = cy * cx + sy * sx
            minus_imaginary = sy * cx - cy * sx
            minus_real = jnp.where(l0, cy * half_x, jnp.where(r0, cx * half_y, minus_real))
            minus_imaginary = jnp.where(l0, sy * half_x, jnp.where(r0, sx * half_y, minus_imaginary))
            corner = l0 & r0
            turn = (plus_real, plus_imaginary, minus_real, minus_imaginary)
            ends = (1.0, half_x, half_y, half_both)
            for n in range(4):
                turns[t, g, n] = SCALE * jnp.where(corner, ends[n], 2.0 * turn[n])
    base = prior(chosen_ref[...])
    for axis in range(2):
        base_ref[axis] = base[axis]


def peak_kernel(
    inverse_ref,
    inverse_rows_ref,
    mask_ref,
    base_ref,
    turns,
    lower_ref,
    *refs,
):
    spectra, (out_ref, high_ref, low_ref) = refs[:-3], refs[-3:]
    supers = turns.shape[1]
    per_row = supers * GROUP
    upper_bands = spectra[0].shape[0]
    bands = upper_bands + lower_ref.shape[0]
    for i in range(bands):
        for g in range(supers):
            lane = g * 2 * LANES
            if i < upper_bands:
                values = quads(spectra[g][i], 0)
            else:
                values = quads(lower_ref[i - upper_bands], g)
            parts = []
            for begin, end, first in ROW_PARTS:
                parts.append(
                    coefficients(
                        [x[begin:end] for x in values],
                        [turns[i % 2, g, n, begin:end] for n in range(4)],
                        first,
                    )
                )
            for n, (a, b) in enumerate(zip(*parts)):
                high, low = split(jnp.concatenate([a, b], axis=0))
                at = slice(i * P_SIZE + n // 2 * HALF, i * P_SIZE + (n // 2 + 1) * HALF)
                lanes = slice(lane + n % 2 * LANES, lane + (n % 2 + 1) * LANES)
                high_ref[at, lanes] = high
                low_ref[at, lanes] = low
    for g in range(supers):
        at = slice(g * 2 * LANES, (g + 1) * 2 * LANES)
        high, low = split(inverse_columns(high_ref[:, at], low_ref[:, at], inverse_ref))
        high_ref[:, at] = high
        low_ref[:, at] = low
    sums = []
    for i in range(bands):
        rows = slice(i * P_SIZE, (i + 1) * P_SIZE)
        sums.append(column_sums(row_transform(inverse_rows_ref, high_ref[rows], low_ref[rows])))
    found = band_peaks(*(jnp.concatenate(parts, axis=0) for parts in zip(*sums)))
    shape = (per_row, 2 * per_row)
    columns = iota(shape, 1) - 2 * iota(shape, 0)
    mask = mask_ref[...].astype(f32).astype(bf16)
    masks = [
        lax.dot_general(
            (columns == n).astype(bf16),
            mask,
            (((1,), (1,)), ((), ())),
            preferred_element_type=f32,
        )
        for n in range(2)
    ]
    parity = (iota((per_row, bands), 1) + lax.axis_index("gz")) % 2
    chosen = jnp.where(parity == 0, masks[0], masks[1])
    for axis in range(2):
        out_ref[axis, 0] = base_ref[axis] + chosen * found[axis]


def exchanged(value, axis, step):
    return lax.ppermute(value, axis, [(i, i ^ step) for i in range(lax.axis_size(axis))])


def from_next(value, axis):
    count = lax.axis_size(axis)
    got = []
    for odd in range(min(2, count - 1)):
        pairs = [(i, i + 1) for i in range(odd, count - 1, 2)]
        got.append(lax.ppermute(value, axis, pairs + [(j, i) for i, j in pairs]))
    if len(got) < 2:
        return got[0] if got else value
    return jnp.where(lax.axis_index(axis) % 2 == 0, got[0], got[1])


def swapped(value):
    return lax.ppermute(value, "gz", [(0, 1), (1, 0)])


VMEM = pl.BlockSpec(memory_space=pltpu.VMEM)
SMEM = pl.BlockSpec(memory_space=pltpu.SMEM)


def cost(microseconds):
    return pl.CostEstimate(
        flops=0, bytes_accessed=int(microseconds * 3.0e6), transcendentals=0
    )


def params(mebibytes):
    return pltpu.CompilerParams(vmem_limit_bytes=mebibytes * 2**20)


def local(sections, fine_offsets, coarse_offset, tissue_mask):
    own = sections[0]
    rows, width = own.shape
    bands = rows // STRIDE
    per_row = width // P_SIZE
    count = lax.axis_size("gx")
    assert rows == DOWN * P_SIZE and width == DOWN * P_SIZE
    assert count % GROUP == 0 and count & (count - 1) == 0
    wide = width
    supers = width // (2 * LANES)
    other = swapped(own)
    own_tile, own_edge, packed = pl.pallas_call(
        prepare_kernel,
        out_shape=(
            jax.ShapeDtypeStruct((rows, width), bf16),
            jax.ShapeDtypeStruct((P_SIZE, width), bf16),
            jax.ShapeDtypeStruct((HALF + rows // 2, LANES), bf16),
        ),
        in_specs=[pl.BlockSpec(memory_space=pltpu.HBM)],
        out_specs=(VMEM,) * 3,
        scratch_shapes=[pltpu.SemaphoreType.DMA((PARTS,))],
        compiler_params=params(16),
        cost_estimate=cost(5.0),
    )(own)
    tables = pl.pallas_call(
        tables_kernel,
        out_shape=(
            jax.ShapeDtypeStruct((2, 4 * LANES, 2 * LANES), bf16),
            jax.ShapeDtypeStruct((2, 4 * LANES, LANES), bf16),
            jax.ShapeDtypeStruct((2 * P_SIZE, 6 * STRIDE), bf16),
            jax.ShapeDtypeStruct((2, supers, 8, LANES), jnp.int32),
            jax.ShapeDtypeStruct((per_row, bands), jnp.int32),
            jax.ShapeDtypeStruct((P_SIZE, 2 * LANES), bf16),
            jax.ShapeDtypeStruct((6 * LANES, 2 * LANES), bf16),
            jax.ShapeDtypeStruct((P_SIZE, 2 * LANES), bf16),
        ),
        in_specs=[pl.BlockSpec(memory_space=pl.ANY)],
        out_specs=(VMEM,) * 8,
        scratch_shapes=[pltpu.SMEM((3,), jnp.int32), pltpu.SemaphoreType.DMA],
        compiler_params=params(16),
        cost_estimate=cost(0.1),
    )(jnp.concatenate([fine_offsets, coarse_offset]))
    weights, coarse_weights, left_rows, picks, chosen, forward_rows, inverse, inverse_rows = tables
    low_bands = P_SIZE // STRIDE
    got_even = exchanged(packed, "gx", 1)
    got_odd = lax.ppermute(packed[HALF:], "gx", [(i + 1, i) for i in range(1, count - 1, 2)])
    right = jnp.where(lax.axis_index("gx") % 2 == 0, got_even[HALF:], got_odd)
    other_right = swapped(right)
    low_payload = jnp.concatenate([own_edge, right[:P_SIZE]], axis=1)
    low_payload, other_right = lax.optimization_barrier((low_payload, other_right))
    own_low = from_next(low_payload, "gy")
    tiles = jnp.concatenate([packed[:HALF], got_even[:HALF]], axis=0)
    step = 2
    while 2 * step < count:
        tiles = jnp.concatenate([tiles, exchanged(tiles, "gx", step)], axis=0)
        step *= 2
    last_tiles = exchanged(tiles, "gx", step)
    def upper(group, *operands):
        return pl.pallas_call(
            functools.partial(upper_kernel, group),
            out_shape=jax.ShapeDtypeStruct((bands - low_bands, P_SIZE, 2 * LANES), f32),
            in_specs=[VMEM] * (4 + len(operands)),
            out_specs=VMEM,
            scratch_shapes=[
                pltpu.VMEM((2, rows, 3 * LANES), bf16),
                pltpu.VMEM((2, 2, 2 * rows, 2 * LANES), bf16),
            ],
            compiler_params=params(32),
            cost_estimate=cost(0.1),
        )(weights, left_rows, own_tile, other, *operands)

    uppers = [upper(group) for group in range(supers - 1)]
    last_tiles, *uppers = lax.optimization_barrier((last_tiles, *uppers))
    tiles = jnp.concatenate([tiles, last_tiles], axis=0)
    other_tiles = swapped(tiles)
    uppers.append(upper(supers - 1, right, other_right))
    other_tiles, own_low, *uppers = lax.optimization_barrier((other_tiles, own_low, *uppers))
    turns, base = pl.pallas_call(
        turn_kernel,
        out_shape=(
            jax.ShapeDtypeStruct((2, supers, 4, HALF, LANES), f32),
            jax.ShapeDtypeStruct((2, per_row, bands), f32),
        ),
        in_specs=[VMEM] * 8,
        out_specs=(VMEM,) * 2,
        scratch_shapes=[pltpu.VMEM((count, 2 * P_SIZE, LANES), f32)],
        compiler_params=params(32),
        cost_estimate=cost(0.1),
    )(
        forward_rows,
        inverse,
        inverse_rows,
        coarse_weights,
        picks,
        chosen,
        tiles,
        other_tiles,
    )
    other_low = swapped(own_low)
    lower = pl.pallas_call(
        lower_kernel,
        out_shape=jax.ShapeDtypeStruct((low_bands, P_SIZE, wide), f32),
        in_specs=[VMEM] * 8,
        out_specs=VMEM,
        scratch_shapes=[
            pltpu.VMEM((2, 2 * P_SIZE, width + LANES), bf16),
            pltpu.VMEM((2, 2, 4 * P_SIZE, wide), bf16),
        ],
        compiler_params=params(32),
        cost_estimate=cost(0.1),
    )(weights, left_rows, own_tile, right, own_low, other, other_right, other_low)
    flow = pl.pallas_call(
        peak_kernel,
        out_shape=jax.ShapeDtypeStruct((2, 1, per_row, bands), f32),
        in_specs=[VMEM] * (6 + supers),
        out_specs=VMEM,
        scratch_shapes=[pltpu.VMEM((bands * P_SIZE, wide), bf16)] * 2,
        compiler_params=params(40),
        cost_estimate=cost(0.1),
    )(inverse, inverse_rows, tissue_mask, base, turns, lower, *uppers)
    return jnp.swapaxes(flow, 2, 3)


def solution(mesh):
    placed = (P("gz", ("pairs", "gy"), "gx"), P("pairs"), P("pairs"), P(("pairs", "gy"), "gx"))
    return jax.shard_map(
        local,
        mesh=mesh,
        in_specs=placed,
        out_specs=P(None, "gz", ("pairs", "gy"), "gx"),
        check_vma=False,
    )
```

```python
import functools
import math

import jax
import jax.numpy as jnp
from jax import lax
from jax.experimental import pallas as pl
from jax.experimental.pallas import tpu as pltpu
from jax.sharding import PartitionSpec as P

P_SIZE = 64
HALF = P_SIZE // 2
STRIDE = 32
DOWN = 8
LANES = 128
GROUP = LANES // HALF
SHARPNESS = 12.0
SCALE = SHARPNESS / float(P_SIZE) ** 4 * math.log2(math.e)

f32 = jnp.float32
bf16 = jnp.bfloat16


def cosine_of_turns(turns):
    square = (turns * (2.0 * math.pi)) ** 2
    total = jnp.full_like(square, 1.0 / math.factorial(20))
    for n in range(9, -1, -1):
        total = total * square + (-1.0) ** n / math.factorial(2 * n)
    return total


def sine_of_turns(turns):
    angle = turns * (2.0 * math.pi)
    square = angle * angle
    total = jnp.full_like(square, -1.0 / math.factorial(19))
    for n in range(8, -1, -1):
        total = total * square + (-1.0) ** n / math.factorial(2 * n + 1)
    return total * angle


def nearest(turns):
    return turns - jnp.round(turns)


def basis_values(frequency, kind, place):
    nyquist = (kind == 1) & (frequency == 0)
    number = jnp.where(nyquist, HALF, frequency)
    quarter = jnp.where((kind == 1) & (frequency != 0), P_SIZE // 4, 0)
    step = (number * place - quarter) & (P_SIZE - 1)
    step = jnp.where(step > HALF, P_SIZE - step, step)
    flip = step > P_SIZE // 4
    step = jnp.where(flip, HALF - step, step)
    square = (step.astype(f32) * (2.0 * math.pi / P_SIZE)) ** 2
    total = jnp.full_like(square, 1.0 / math.factorial(12))
    for n in range(5, -1, -1):
        total = total * square + (-1.0) ** n / math.factorial(2 * n)
    return jnp.where(flip, -total, total)


def quotient(number, divisor):
    return number >> (divisor.bit_length() - 1)


def remainder(number, divisor):
    return number & (divisor - 1)


def iota(shape, axis):
    return lax.broadcasted_iota(jnp.int32, shape, axis)


def split(values):
    high = values.astype(bf16)
    return high, (values - high.astype(f32)).astype(bf16)


def matmul(left, right):
    return jnp.dot(left, right, preferred_element_type=f32)


def add_row_halves(values):
    half = values.shape[0] // 2
    return values[:half] + values[half:]


def first_lane(shape):
    return remainder(iota(shape, 1), HALF) == 0


def half_spectra(cc, cs, sc, ss, first):
    shape = cc.shape
    l0 = first_lane(shape)
    if not first:
        return (
            cc - jnp.where(l0, 0.0, ss),
            sc + jnp.where(l0, 0.0, cs),
            jnp.where(l0, cs, cc + ss),
            jnp.where(l0, ss, sc - cs),
        )
    r0 = iota(shape, 0) == 0
    either = l0 | r0
    return (
        cc - jnp.where(either, 0.0, ss),
        jnp.where(r0, 0.0, sc) + jnp.where(l0, 0.0, cs),
        jnp.where(l0, cs, jnp.where(r0, sc, cc + ss)),
        jnp.where(either, ss, sc - cs),
    )


def cross_spectra(own, other, sign, first):
    a = half_spectra(*own, first)
    b = half_spectra(*other, first)
    out = []
    for r, i in ((0, 1), (2, 3)):
        out.append(b[r] * a[r] + b[i] * a[i])
        out.append(sign * (b[r] * a[i] - b[i] * a[r]))
    if first:
        shape = own[0].shape
        corner = first_lane(shape) & (iota(shape, 0) == 0)
        out = [jnp.where(corner, x * y, o) for x, y, o in zip(own, other, out)]
    return out


def coefficients(g, t, first):
    gpr, gpi, gmr, gmi = g
    tpr, tpi, tmr, tmi = t
    shape = gpr.shape
    l0 = first_lane(shape)
    hpr = gpr * tpr - gpi * tpi
    hpi = gpr * tpi + gpi * tpr
    hmr = gmr * tmr - gmi * tmi
    hmi = gmr * tmi + gmi * tmr
    if not first:
        return (
            hpr + jnp.where(l0, 0.0, hmr),
            jnp.where(l0, hmr, hmi - hpi),
            -hpi - jnp.where(l0, 0.0, hmi),
            jnp.where(l0, -hmi, hmr - hpr),
        )
    r0 = iota(shape, 0) == 0
    either = l0 | r0
    corner = l0 & r0
    out = (
        hpr + jnp.where(either, 0.0, hmr),
        jnp.where(l0, hmr, jnp.where(r0, 0.0, hmi) - hpi),
        jnp.where(r0, hmr, -hpi - jnp.where(l0, 0.0, hmi)),
        jnp.where(either, -hmi, hmr - hpr),
    )
    return [jnp.where(corner, x * y, o) for x, y, o in zip(g, t, out)]


def signed(number):
    return jnp.where(number >= HALF, number - P_SIZE, number).astype(f32)


def column_sums(logits):
    largest = jnp.max(logits, axis=0, keepdims=True)
    weights = jnp.exp2(logits - largest)
    rows = signed(iota((P_SIZE, 1), 0))
    return largest, jnp.sum(weights, axis=0, keepdims=True), jnp.sum(weights * rows, axis=0, keepdims=True)


def band_peaks(largest, total, moment):
    bands, wide = largest.shape
    largest, total, moment = (
        jnp.transpose(x).reshape(wide // P_SIZE, P_SIZE, bands) for x in (largest, total, moment)
    )
    factor = jnp.exp2(largest - jnp.max(largest, axis=1, keepdims=True))
    weight = factor * total
    columns = signed(lax.broadcasted_iota(jnp.int32, (1, P_SIZE, 1), 1))
    bottom = jnp.sum(weight, axis=1)
    return jnp.sum(factor * moment, axis=1) / bottom, jnp.sum(weight * columns, axis=1) / bottom


ROW_PARTS = ((0, 8, True), (8, HALF, False))


def quads(block, group):
    lane = group * 2 * LANES
    top, bottom = block[:HALF], block[HALF:]
    return (
        top[:, lane : lane + LANES],
        top[:, lane + LANES : lane + 2 * LANES],
        bottom[:, lane : lane + LANES],
        bottom[:, lane + LANES : lane + 2 * LANES],
    )


def unpack(packed):
    wide = packed.astype(f32)
    return jnp.concatenate([wide, pltpu.roll(wide, P_SIZE, axis=1)], axis=0).astype(bf16)


def prepare_kernel(tile_ref, out_ref, low_ref, packed_ref):
    rows, width = tile_ref.shape
    columns = width // DOWN
    pick = quotient(iota((width, LANES), 0), DOWN) == remainder(iota((width, LANES), 1), columns)
    pick = pick.astype(bf16)
    left = iota((columns // 2, LANES), 1) < P_SIZE
    sums = matmul(tile_ref[...], pick)
    coarse = jnp.sum(sums.reshape(rows // DOWN, DOWN, LANES), axis=1) / DOWN
    half = coarse.shape[0] // 2
    packed_ref[:half] = jnp.where(left, coarse[:half], coarse[half:]).astype(bf16)
    low_ref[...] = tile_ref[:P_SIZE]
    edge = tile_ref[:, :LANES].astype(f32)
    half_rows = rows // 2
    left = iota((half_rows, LANES), 1) < P_SIZE
    edge = jnp.where(left, edge[:half_rows], pltpu.roll(edge[half_rows:], P_SIZE, axis=1))
    packed_ref[half:] = edge.astype(bf16)
    out_ref[...] = tile_ref[...]


def beside(high, low):
    left = iota(high.shape, 1) < P_SIZE
    return jnp.concatenate([high, jnp.where(left, low, 0.0)], axis=1).astype(bf16)


def tables_kernel(
    offsets_in,
    weights_ref,
    coarse_weights_ref,
    rows_ref,
    picks_ref,
    chosen_ref,
    forward_rows_ref,
    inverse_ref,
    inverse_rows_ref,
):
    offsets = offsets_in[...].astype(f32).reshape(1, 3)
    row_offset, column_offset, coarse_offset = (
        jnp.max(offsets[:, n : n + 1]).astype(jnp.int32) for n in range(3)
    )
    count = lax.axis_size("gx")
    per_row, bands = chosen_ref.shape
    supers = per_row // GROUP
    side = lax.axis_index("gz")
    gx_place = lax.axis_index("gx")
    shape = (2 * P_SIZE, LANES)
    lane = iota(shape, 1)
    row = iota(shape, 0)
    values = jnp.where(
        quotient(row, P_SIZE) == quotient(remainder(lane, P_SIZE), HALF),
        basis_values(remainder(lane, HALF), quotient(lane, P_SIZE), remainder(row, P_SIZE)),
        0.0,
    )
    padded = jnp.concatenate([values, jnp.zeros((2 * P_SIZE, LANES), f32)], axis=0)
    shape = (P_SIZE, LANES)
    row = iota(shape, 0)
    lane = iota(shape, 1)
    basis = basis_values(remainder(row, HALF), quotient(row, HALF), remainder(lane, P_SIZE))
    high, low = (value.astype(f32) for value in split(basis))
    forward_rows_ref[...] = beside(high, low)
    wide_high = jnp.concatenate([high] * 2, axis=1)
    wide_low = jnp.concatenate([low] * 2, axis=1)
    for kind in range(2):
        rows = slice(kind * HALF, (kind + 1) * HALF)
        for patch in range(GROUP):
            mine = quotient(iota((HALF, GROUP * P_SIZE), 1), P_SIZE) == patch
            at = (kind * GROUP + patch) * HALF
            for part, value in enumerate((wide_high, wide_high, wide_low)):
                begin = at + part * 2 * LANES
                inverse_ref[begin : begin + HALF] = jnp.where(mine, value[rows], 0.0).astype(bf16)
    kind = quotient(remainder(lane, P_SIZE), HALF)
    high, low = split(basis_values(remainder(lane, HALF), kind, row))
    inverse_rows_ref[...] = beside(high.astype(f32), low.astype(f32))
    shifts = [column_offset + STRIDE * ((t + side) % 2) for t in range(2)] + [coarse_offset]
    for t, shift in enumerate(shifts):
        moved = pltpu.roll(padded, shift, axis=0)
        for part, value in enumerate(split(moved)):
            rows = slice(part * 2 * LANES, (part + 1) * 2 * LANES)
            turned = pltpu.roll(value.astype(f32), P_SIZE, axis=1).astype(bf16)
            for order, entry in enumerate((value, turned)):
                if t < 2:
                    weights_ref[order, rows, t * LANES : (t + 1) * LANES] = entry
                else:
                    coarse_weights_ref[order, rows] = entry
    shape = (P_SIZE, 6 * STRIDE)
    number = iota(shape, 0)
    lane = iota(shape, 1)
    place = quotient(lane, P_SIZE) * STRIDE + remainder(lane, STRIDE) - row_offset
    values = jnp.where(
        (place >= 0) & (place < P_SIZE),
        basis_values(remainder(number, HALF), quotient(number, HALF), place),
        0.0,
    )
    high, low = split(values)
    is_low = remainder(lane, P_SIZE) >= STRIDE
    rows_ref[:P_SIZE] = high
    rows_ref[P_SIZE:] = jnp.where(is_low, 0.0, low.astype(f32)).astype(bf16)
    def pick(column):
        centre = (gx_place * (2 * per_row) + column) * STRIDE + column_offset + P_SIZE // 2
        return jnp.clip(quotient(quotient(centre, DOWN) - coarse_offset, P_SIZE), 0, count - 1)

    lane_row = iota((1, LANES), 1)
    for t in range(2):
        for g in range(supers):
            column = 2 * (g * GROUP + quotient(lane_row, HALF)) + remainder(t + side, 2)
            picks_ref[t, g] = jnp.broadcast_to(pick(column), (8, LANES))
    shape = (per_row, bands)
    parity = remainder(iota(shape, 1) + side, 2)
    chosen_ref[...] = pick(2 * iota(shape, 0) + parity)


def column_transform(strips, weights):
    rows = strips[0].shape[0]
    out = []
    for order in range(2):
        part = [x[:, order * LANES : (order + 2) * LANES] for x in strips]
        left = jnp.concatenate([jnp.concatenate([x, x], axis=1) for x in part], axis=0)
        out.append(matmul(left, weights[order]))
    return [[x[n * rows : (n + 1) * rows] for x in out] for n in range(len(strips))]


def pair_up(a, b):
    left = iota(a.shape, 1) < P_SIZE
    return jnp.where(left, a, b), pltpu.roll(jnp.where(left, b, a), P_SIZE, axis=1)


def forward_bands(image, stacked, weights, left_rows, first_band, out_ref):
    bands = out_ref.shape[0]
    tall = image.shape[1]
    wide = out_ref.shape[2]
    blocks = tall // STRIDE
    supers = wide // (2 * LANES)
    places = [(s, g) for s in range(2) for g in range(supers)]
    strips = [image[s, :, g * 2 * LANES : (2 * g + 3) * LANES] for s, g in places]
    for (s, g), (a, b) in zip(places, column_transform(strips, weights)):
        lane = g * 2 * LANES
        for t in range(2):
            half = slice(t * LANES, (t + 1) * LANES)
            for part, value in enumerate(pair_up(a[:, half], b[:, half])):
                high, low = split(value)
                at = slice(lane + part * LANES, lane + (part + 1) * LANES)
                for n in range(blocks):
                    block = slice(n * STRIDE, (n + 1) * STRIDE)
                    stacked[s, t, 2 * n * STRIDE : (2 * n + 1) * STRIDE, at] = high[block]
                    stacked[s, t, (2 * n + 1) * STRIDE : (2 * n + 2) * STRIDE, at] = low[block]
    sign = jnp.where(lax.axis_index("gz") == 0, 1.0, -1.0).astype(f32)
    for i in range(bands):
        spectra = []
        for s in range(2):
            window = stacked[s, (first_band + i) % 2, 2 * STRIDE * i : 2 * STRIDE * (i + 3), :]
            spectra.append(add_row_halves(matmul(left_rows, window)))
        for g in range(supers):
            lane = g * 2 * LANES
            own = quads(spectra[0], g)
            other = quads(spectra[1], g)
            for begin, end, first in ROW_PARTS:
                out = cross_spectra(
                    [x[begin:end] for x in own], [x[begin:end] for x in other], sign, first
                )
                out_ref[i, begin:end, lane : lane + LANES] = out[0]
                out_ref[i, begin:end, lane + LANES : lane + 2 * LANES] = out[1]
                out_ref[i, HALF + begin : HALF + end, lane : lane + LANES] = out[2]
                out_ref[i, HALF + begin : HALF + end, lane + LANES : lane + 2 * LANES] = out[3]


def is_last(axis):
    return lax.axis_index(axis) == lax.axis_size(axis) - 1


def upper_kernel(group, weights, left_rows_ref, own_ref, other_ref, *refs):
    rights, (out_ref, image, stacked) = refs[:-3], refs[-3:]
    lane = group * 2 * LANES
    wide = 2 * LANES if rights else 3 * LANES
    for s, main in enumerate((own_ref, other_ref)):
        image[s, :, :wide] = main[:, lane : lane + wide]
        if rights:
            image[s, :, wide:] = unpack(rights[s][...])
    if rights:

        @pl.when(is_last("gx"))
        def _():
            image[:, :, wide:] = jnp.zeros((2, image.shape[1], LANES), bf16)

    forward_bands(image, stacked, weights, left_rows_ref[...], 0, out_ref)


def lower_kernel(
    weights,
    left_rows_ref,
    own_ref,
    own_right_ref,
    own_low_ref,
    other_ref,
    other_right_ref,
    other_low_ref,
    out_ref,
    image,
    stacked,
):
    rows, width = own_ref.shape
    for s, (main, right, low) in enumerate(
        ((own_ref, own_right_ref, own_low_ref), (other_ref, other_right_ref, other_low_ref))
    ):
        image[s, :P_SIZE, :width] = main[rows - P_SIZE :]
        edge = right[rows // 2 - P_SIZE :].astype(f32)
        image[s, :P_SIZE, width:] = pltpu.roll(edge, P_SIZE, axis=1).astype(bf16)
        image[s, P_SIZE:] = low[...]

    @pl.when(is_last("gx"))
    def _():
        image[:, :, width:] = jnp.zeros((2, 2 * P_SIZE, LANES), bf16)

    @pl.when(is_last("gy"))
    def _():
        image[:, P_SIZE:, :] = jnp.zeros((2, P_SIZE, width + LANES), bf16)

    forward_bands(
        image, stacked, weights, left_rows_ref[...], rows // STRIDE - out_ref.shape[0], out_ref
    )


def inverse_columns(high, low, table_ref):
    return matmul(jnp.concatenate([high, low, high], axis=1), table_ref[...])


def row_transform(table_ref, high, low):
    return matmul(table_ref[:, : 3 * P_SIZE], jnp.concatenate([high, low, high], axis=0))


def coarse_peaks(strip, forward_rows_ref, inverse_ref, inverse_rows_ref, weights, sign):
    supers = len(strip) * 2 // GROUP
    strip = strip + [jnp.zeros_like(strip[0])]
    columns = []
    for g in range(supers):
        (pair,) = column_transform([jnp.concatenate(strip[2 * g : 2 * g + 3], axis=1)], weights)
        columns += pair_up(*pair)
    strips = jnp.concatenate(columns, axis=1)
    spectra = []
    for s in range(2):
        spectra.append(
            row_transform(forward_rows_ref, *split(strips[s * P_SIZE : (s + 1) * P_SIZE]))
        )
    peaks = []
    for g in range(supers):
        own = quads(spectra[0], g)
        other = quads(spectra[1], g)
        parts = []
        for begin, end, first in ROW_PARTS:
            shape = (end - begin, LANES)
            values = cross_spectra([x[begin:end] for x in own], [x[begin:end] for x in other], sign, first)
            corner = first_lane(shape) & (iota(shape, 0) == 0) & first
            turn = [
                jnp.where(corner, SCALE, c).astype(f32)
                for c in (2.0 * SCALE, 0.0, 2.0 * SCALE, 0.0)
            ]
            parts.append(coefficients(values, turn, first))
        cc, cs, sc, ss = (jnp.concatenate([a, b], axis=0) for a, b in zip(*parts))
        block = jnp.concatenate(
            [jnp.concatenate([cc, cs], axis=1), jnp.concatenate([sc, ss], axis=1)], axis=0
        )
        found = inverse_columns(*split(block), inverse_ref)
        sums = column_sums(row_transform(inverse_rows_ref, *split(found)))
        wide = [jnp.broadcast_to(x, (LANES, GROUP * P_SIZE)) for x in sums]
        peaks.append(band_peaks(*wide))
    return [jnp.concatenate(parts, axis=0) for parts in zip(*peaks)]


def turn_kernel(
    forward_rows_ref,
    inverse_ref,
    inverse_rows_ref,
    weights,
    picks_ref,
    chosen_ref,
    own_part_ref,
    other_part_ref,
    turns,
    base_ref,
    ordered,
):
    count = ordered.shape[0]
    supers = turns.shape[1]
    side = lax.axis_index("gz")
    place = lax.axis_index("gx")
    sign = jnp.where(side == 0, 1.0, -1.0).astype(f32)
    for step in range(count):
        for part, ref in enumerate((own_part_ref, other_part_ref)):
            tile = ref[step * HALF : (step + 1) * HALF].astype(f32)
            turned = pltpu.roll(tile, P_SIZE, axis=1)
            rows = slice(part * P_SIZE, (part + 1) * P_SIZE)
            ordered[place ^ step, 0, rows] = jnp.concatenate([tile, turned], axis=0)
            ordered[place ^ step, 1, rows] = jnp.concatenate([turned, tile], axis=0)
    left = iota((2 * P_SIZE, LANES), 1) < P_SIZE
    strip = []
    for j in range(0, count, 2):
        strip.append(jnp.where(left, ordered[j, 0], ordered[j + 1, 1]).astype(bf16))
    peaks = coarse_peaks(
        strip, forward_rows_ref, inverse_ref, inverse_rows_ref, weights, sign
    )
    blended = [
        (0.5 * DOWN) * (peak + jnp.sum(peak, axis=0, keepdims=True) / count) for peak in peaks
    ]

    def prior(pick):
        choice = pick == iota((count, LANES), 0)
        return [
            jnp.sum(jnp.where(choice, values, 0.0), axis=0, keepdims=True) for values in blended
        ]

    shape = (HALF, LANES)
    frequency_y = iota(shape, 0).astype(f32) * (1.0 / P_SIZE)
    l0 = first_lane(shape)
    r0 = iota(shape, 0) == 0
    lane_row = iota((1, LANES), 1)
    frequency_x = remainder(lane_row, HALF).astype(f32) * (1.0 / P_SIZE)
    for t in range(2):
        for g in range(supers):
            dy, dx = (
                value - P_SIZE * jnp.round(value * (1.0 / P_SIZE)) for value in prior(picks_ref[t, g, :1])
            )
            turn_y = nearest(frequency_y * dy)
            turn_x = nearest(frequency_x * dx)
            cy, sy = cosine_of_turns(turn_y), sine_of_turns(turn_y)
            cx, sx = cosine_of_turns(turn_x), sine_of_turns(turn_x)
            half_y = cosine_of_turns(nearest(0.5 * dy))
            half_x = cosine_of_turns(nearest(0.5 * dx))
            half_both = cosine_of_turns(nearest(0.5 * (dy + dx)))
            plus_real = cy * cx - sy * sx
            plus_imaginary = sy * cx + cy * sx
            minus_real = cy * cx + sy * sx
            minus_imaginary = sy * cx - cy * sx
            minus_real = jnp.where(l0, cy * half_x, jnp.where(r0, cx * half_y, minus_real))
            minus_imaginary = jnp.where(l0, sy * half_x, jnp.where(r0, sx * half_y, minus_imaginary))
            corner = l0 & r0
            turn = (plus_real, plus_imaginary, minus_real, minus_imaginary)
            ends = (1.0, half_x, half_y, half_both)
            for n in range(4):
                turns[t, g, n] = SCALE * jnp.where(corner, ends[n], 2.0 * turn[n])
    pick = chosen_ref[...]
    for axis, values in enumerate(blended):
        base = jnp.zeros(pick.shape, f32)
        for j in range(count):
            base = jnp.where(pick == j, values[j : j + 1, : pick.shape[1]], base)
        base_ref[axis] = base


def peak_kernel(
    inverse_ref,
    inverse_rows_ref,
    mask_ref,
    base_ref,
    turns,
    lower_ref,
    *refs,
):
    spectra, (out_ref, high_ref, low_ref) = refs[:-3], refs[-3:]
    supers = turns.shape[1]
    per_row = supers * GROUP
    upper_bands = spectra[0].shape[0]
    bands = upper_bands + lower_ref.shape[0]
    for i in range(bands):
        for g in range(supers):
            lane = g * 2 * LANES
            if i < upper_bands:
                values = quads(spectra[g][i], 0)
            else:
                values = quads(lower_ref[i - upper_bands], g)
            parts = []
            for begin, end, first in ROW_PARTS:
                parts.append(
                    coefficients(
                        [x[begin:end] for x in values],
                        [turns[i % 2, g, n, begin:end] for n in range(4)],
                        first,
                    )
                )
            for n, (a, b) in enumerate(zip(*parts)):
                high, low = split(jnp.concatenate([a, b], axis=0))
                at = slice(i * P_SIZE + n // 2 * HALF, i * P_SIZE + (n // 2 + 1) * HALF)
                lanes = slice(lane + n % 2 * LANES, lane + (n % 2 + 1) * LANES)
                high_ref[at, lanes] = high
                low_ref[at, lanes] = low
    for g in range(supers):
        at = slice(g * 2 * LANES, (g + 1) * 2 * LANES)
        high, low = split(inverse_columns(high_ref[:, at], low_ref[:, at], inverse_ref))
        high_ref[:, at] = high
        low_ref[:, at] = low
    sums = []
    for i in range(bands):
        rows = slice(i * P_SIZE, (i + 1) * P_SIZE)
        sums.append(column_sums(row_transform(inverse_rows_ref, high_ref[rows], low_ref[rows])))
    found = band_peaks(*(jnp.concatenate(parts, axis=0) for parts in zip(*sums)))
    shape = (per_row, 2 * per_row)
    columns = iota(shape, 1) - 2 * iota(shape, 0)
    mask = mask_ref[...].astype(f32).astype(bf16)
    masks = [
        lax.dot_general(
            (columns == n).astype(bf16),
            mask,
            (((1,), (1,)), ((), ())),
            preferred_element_type=f32,
        )
        for n in range(2)
    ]
    parity = remainder(iota((per_row, bands), 1) + lax.axis_index("gz"), 2)
    chosen = jnp.where(parity == 0, masks[0], masks[1])
    for axis in range(2):
        out_ref[axis, 0] = base_ref[axis] + chosen * found[axis]


def exchanged(value, axis, step):
    return lax.ppermute(value, axis, [(i, i ^ step) for i in range(lax.axis_size(axis))])


def from_next(value, axis):
    count = lax.axis_size(axis)
    got = []
    for odd in range(min(2, count - 1)):
        pairs = [(i, i + 1) for i in range(odd, count - 1, 2)]
        got.append(lax.ppermute(value, axis, pairs + [(j, i) for i, j in pairs]))
    if len(got) < 2:
        return got[0] if got else value
    return jnp.where(lax.axis_index(axis) % 2 == 0, got[0], got[1])


def swapped(value):
    return lax.ppermute(value, "gz", [(0, 1), (1, 0)])


VMEM = pl.BlockSpec(memory_space=pltpu.VMEM)
SMEM = pl.BlockSpec(memory_space=pltpu.SMEM)


def cost(microseconds):
    return pl.CostEstimate(
        flops=0, bytes_accessed=int(microseconds * 3.0e6), transcendentals=0
    )


def params(mebibytes):
    return pltpu.CompilerParams(vmem_limit_bytes=mebibytes * 2**20)


def local(sections, fine_offsets, coarse_offset, tissue_mask):
    own = sections[0]
    rows, width = own.shape
    bands = rows // STRIDE
    per_row = width // P_SIZE
    count = lax.axis_size("gx")
    assert rows == DOWN * P_SIZE and width == DOWN * P_SIZE
    assert count % GROUP == 0 and count & (count - 1) == 0
    wide = width
    supers = width // (2 * LANES)
    own_tile, own_edge, packed = pl.pallas_call(
        prepare_kernel,
        out_shape=(
            jax.ShapeDtypeStruct((rows, width), bf16),
            jax.ShapeDtypeStruct((P_SIZE, width), bf16),
            jax.ShapeDtypeStruct((HALF + rows // 2, LANES), bf16),
        ),
        in_specs=[VMEM],
        out_specs=(VMEM,) * 3,
        compiler_params=params(16),
        cost_estimate=cost(5.0),
    )(own)
    offsets = jnp.concatenate([fine_offsets, coarse_offset])
    tables = pl.pallas_call(
        tables_kernel,
        out_shape=(
            jax.ShapeDtypeStruct((2, 4 * LANES, 2 * LANES), bf16),
            jax.ShapeDtypeStruct((2, 4 * LANES, LANES), bf16),
            jax.ShapeDtypeStruct((2 * P_SIZE, 6 * STRIDE), bf16),
            jax.ShapeDtypeStruct((2, supers, 8, LANES), jnp.int32),
            jax.ShapeDtypeStruct((per_row, bands), jnp.int32),
            jax.ShapeDtypeStruct((P_SIZE, 2 * LANES), bf16),
            jax.ShapeDtypeStruct((6 * LANES, 2 * LANES), bf16),
            jax.ShapeDtypeStruct((P_SIZE, 2 * LANES), bf16),
        ),
        in_specs=[VMEM],
        out_specs=(VMEM,) * 8,
        compiler_params=params(16),
        cost_estimate=cost(0.1),
    )(offsets)
    weights, coarse_weights, left_rows, picks, chosen, forward_rows, inverse, inverse_rows = tables
    low_bands = P_SIZE // STRIDE
    other = swapped(own_tile)
    got_even = exchanged(packed, "gx", 1)
    got_odd = lax.ppermute(packed[HALF:], "gx", [(i + 1, i) for i in range(1, count - 1, 2)])
    right = jnp.where(lax.axis_index("gx") % 2 == 0, got_even[HALF:], got_odd)
    other_right = swapped(right)
    low_payload = jnp.concatenate([own_edge, right[:P_SIZE]], axis=1)
    low_payload, other_right = lax.optimization_barrier((low_payload, other_right))
    own_low = from_next(low_payload, "gy")
    tiles = jnp.concatenate([packed[:HALF], got_even[:HALF]], axis=0)
    step = 2
    while 2 * step < count:
        tiles = jnp.concatenate([tiles, exchanged(tiles, "gx", step)], axis=0)
        step *= 2
    last_tiles = exchanged(tiles, "gx", step)
    def upper(group, *operands):
        return pl.pallas_call(
            functools.partial(upper_kernel, group),
            out_shape=jax.ShapeDtypeStruct((bands - low_bands, P_SIZE, 2 * LANES), f32),
            in_specs=[VMEM] * (4 + len(operands)),
            out_specs=VMEM,
            scratch_shapes=[
                pltpu.VMEM((2, rows, 3 * LANES), bf16),
                pltpu.VMEM((2, 2, 2 * rows, 2 * LANES), bf16),
            ],
            compiler_params=params(32),
            cost_estimate=cost(0.1),
        )(weights, left_rows, own_tile, other, *operands)

    uppers = [upper(group) for group in range(supers - 1)]
    last_tiles, *uppers = lax.optimization_barrier((last_tiles, *uppers))
    tiles = jnp.concatenate([tiles, last_tiles], axis=0)
    other_tiles = swapped(tiles)
    uppers.append(upper(supers - 1, right, other_right))
    other_tiles, own_low, *uppers = lax.optimization_barrier((other_tiles, own_low, *uppers))
    turns, base = pl.pallas_call(
        turn_kernel,
        out_shape=(
            jax.ShapeDtypeStruct((2, supers, 4, HALF, LANES), f32),
            jax.ShapeDtypeStruct((2, per_row, bands), f32),
        ),
        in_specs=[VMEM] * 8,
        out_specs=(VMEM,) * 2,
        scratch_shapes=[pltpu.VMEM((count, 2, 2 * P_SIZE, LANES), f32)],
        compiler_params=params(32),
        cost_estimate=cost(0.1),
    )(
        forward_rows,
        inverse,
        inverse_rows,
        coarse_weights,
        picks,
        chosen,
        tiles,
        other_tiles,
    )
    other_low = swapped(own_low)
    lower = pl.pallas_call(
        lower_kernel,
        out_shape=jax.ShapeDtypeStruct((low_bands, P_SIZE, wide), f32),
        in_specs=[VMEM] * 8,
        out_specs=VMEM,
        scratch_shapes=[
            pltpu.VMEM((2, 2 * P_SIZE, width + LANES), bf16),
            pltpu.VMEM((2, 2, 4 * P_SIZE, wide), bf16),
        ],
        compiler_params=params(32),
        cost_estimate=cost(0.1),
    )(weights, left_rows, own_tile, right, own_low, other, other_right, other_low)
    flow = pl.pallas_call(
        peak_kernel,
        out_shape=jax.ShapeDtypeStruct((2, 1, per_row, bands), f32),
        in_specs=[VMEM] * (6 + supers),
        out_specs=VMEM,
        scratch_shapes=[pltpu.VMEM((bands * P_SIZE, wide), bf16)] * 2,
        compiler_params=params(40),
        cost_estimate=cost(0.1),
    )(inverse, inverse_rows, tissue_mask, base, turns, lower, *uppers)
    return jnp.swapaxes(flow, 2, 3)


def solution(mesh):
    placed = (P("gz", ("pairs", "gy"), "gx"), P("pairs"), P("pairs"), P(("pairs", "gy"), "gx"))
    return jax.shard_map(
        local,
        mesh=mesh,
        in_specs=placed,
        out_specs=P(None, "gz", ("pairs", "gy"), "gx"),
        check_vma=False,
    )
```

```python
import functools
import math

import jax
import jax.numpy as jnp
from jax import lax
from jax.experimental import pallas as pl
from jax.experimental.pallas import tpu as pltpu
from jax.sharding import PartitionSpec as P

P_SIZE = 64
HALF = P_SIZE // 2
STRIDE = 32
DOWN = 8
LANES = 128
GROUP = LANES // HALF
SHARPNESS = 12.0
SCALE = SHARPNESS / float(P_SIZE) ** 4 * math.log2(math.e)

f32 = jnp.float32
bf16 = jnp.bfloat16


def cosine_of_turns(turns):
    square = (turns * (2.0 * math.pi)) ** 2
    total = jnp.full_like(square, 1.0 / math.factorial(20))
    for n in range(9, -1, -1):
        total = total * square + (-1.0) ** n / math.factorial(2 * n)
    return total


def sine_of_turns(turns):
    angle = turns * (2.0 * math.pi)
    square = angle * angle
    total = jnp.full_like(square, -1.0 / math.factorial(19))
    for n in range(8, -1, -1):
        total = total * square + (-1.0) ** n / math.factorial(2 * n + 1)
    return total * angle


def nearest(turns):
    return turns - jnp.round(turns)


def basis_values(frequency, kind, place):
    nyquist = (kind == 1) & (frequency == 0)
    number = jnp.where(nyquist, HALF, frequency)
    quarter = jnp.where((kind == 1) & (frequency != 0), P_SIZE // 4, 0)
    step = (number * place - quarter) & (P_SIZE - 1)
    step = jnp.where(step > HALF, P_SIZE - step, step)
    flip = step > P_SIZE // 4
    step = jnp.where(flip, HALF - step, step)
    square = (step.astype(f32) * (2.0 * math.pi / P_SIZE)) ** 2
    total = jnp.full_like(square, 1.0 / math.factorial(12))
    for n in range(5, -1, -1):
        total = total * square + (-1.0) ** n / math.factorial(2 * n)
    return jnp.where(flip, -total, total)


def quotient(number, divisor):
    return number >> (divisor.bit_length() - 1)


def remainder(number, divisor):
    return number & (divisor - 1)


def iota(shape, axis):
    return lax.broadcasted_iota(jnp.int32, shape, axis)


def split(values):
    high = values.astype(bf16)
    return high, (values - high.astype(f32)).astype(bf16)


def matmul(left, right):
    return jnp.dot(left, right, preferred_element_type=f32)


def add_row_halves(values):
    half = values.shape[0] // 2
    return values[:half] + values[half:]


def first_lane(shape):
    return remainder(iota(shape, 1), HALF) == 0


def half_spectra(cc, cs, sc, ss, first):
    shape = cc.shape
    l0 = first_lane(shape)
    if not first:
        return (
            cc - jnp.where(l0, 0.0, ss),
            sc + jnp.where(l0, 0.0, cs),
            jnp.where(l0, cs, cc + ss),
            jnp.where(l0, ss, sc - cs),
        )
    r0 = iota(shape, 0) == 0
    either = l0 | r0
    return (
        cc - jnp.where(either, 0.0, ss),
        jnp.where(r0, 0.0, sc) + jnp.where(l0, 0.0, cs),
        jnp.where(l0, cs, jnp.where(r0, sc, cc + ss)),
        jnp.where(either, ss, sc - cs),
    )


def cross_spectra(own, other, sign, first):
    a = half_spectra(*own, first)
    b = half_spectra(*other, first)
    out = []
    for r, i in ((0, 1), (2, 3)):
        out.append(b[r] * a[r] + b[i] * a[i])
        out.append(sign * (b[r] * a[i] - b[i] * a[r]))
    if first:
        shape = own[0].shape
        corner = first_lane(shape) & (iota(shape, 0) == 0)
        out = [jnp.where(corner, x * y, o) for x, y, o in zip(own, other, out)]
    return out


def coefficients(g, t, first):
    gpr, gpi, gmr, gmi = g
    tpr, tpi, tmr, tmi = t
    shape = gpr.shape
    l0 = first_lane(shape)
    hpr = gpr * tpr - gpi * tpi
    hpi = gpr * tpi + gpi * tpr
    hmr = gmr * tmr - gmi * tmi
    hmi = gmr * tmi + gmi * tmr
    if not first:
        return (
            hpr + jnp.where(l0, 0.0, hmr),
            jnp.where(l0, hmr, hmi - hpi),
            -hpi - jnp.where(l0, 0.0, hmi),
            jnp.where(l0, -hmi, hmr - hpr),
        )
    r0 = iota(shape, 0) == 0
    either = l0 | r0
    corner = l0 & r0
    out = (
        hpr + jnp.where(either, 0.0, hmr),
        jnp.where(l0, hmr, jnp.where(r0, 0.0, hmi) - hpi),
        jnp.where(r0, hmr, -hpi - jnp.where(l0, 0.0, hmi)),
        jnp.where(either, -hmi, hmr - hpr),
    )
    return [jnp.where(corner, x * y, o) for x, y, o in zip(g, t, out)]


def signed(number):
    return jnp.where(number >= HALF, number - P_SIZE, number).astype(f32)


def column_sums(logits):
    largest = jnp.max(logits, axis=0, keepdims=True)
    weights = jnp.exp2(logits - largest)
    rows = signed(iota((P_SIZE, 1), 0))
    return largest, jnp.sum(weights, axis=0, keepdims=True), jnp.sum(weights * rows, axis=0, keepdims=True)


def band_peaks(largest, total, moment):
    bands, wide = largest.shape
    largest, total, moment = (
        jnp.transpose(x).reshape(wide // P_SIZE, P_SIZE, bands) for x in (largest, total, moment)
    )
    factor = jnp.exp2(largest - jnp.max(largest, axis=1, keepdims=True))
    weight = factor * total
    columns = signed(lax.broadcasted_iota(jnp.int32, (1, P_SIZE, 1), 1))
    bottom = jnp.sum(weight, axis=1)
    return jnp.sum(factor * moment, axis=1) / bottom, jnp.sum(weight * columns, axis=1) / bottom


ROW_PARTS = ((0, 8, True), (8, HALF, False))


def quads(block, group):
    lane = group * 2 * LANES
    top, bottom = block[:HALF], block[HALF:]
    return (
        top[:, lane : lane + LANES],
        top[:, lane + LANES : lane + 2 * LANES],
        bottom[:, lane : lane + LANES],
        bottom[:, lane + LANES : lane + 2 * LANES],
    )


def unpack(packed):
    wide = packed.astype(f32)
    return jnp.concatenate([wide, pltpu.roll(wide, P_SIZE, axis=1)], axis=0).astype(bf16)


def prepare_kernel(tile_ref, out_ref, low_ref, packed_ref):
    rows, width = tile_ref.shape
    columns = width // DOWN
    pick = quotient(iota((width, LANES), 0), DOWN) == remainder(iota((width, LANES), 1), columns)
    pick = pick.astype(bf16)
    left = iota((columns // 2, LANES), 1) < P_SIZE
    sums = matmul(tile_ref[...], pick)
    coarse = jnp.sum(sums.reshape(rows // DOWN, DOWN, LANES), axis=1) / DOWN
    half = coarse.shape[0] // 2
    packed_ref[:half] = jnp.where(left, coarse[:half], coarse[half:]).astype(bf16)
    low_ref[...] = tile_ref[:P_SIZE]
    edge = tile_ref[:, :LANES].astype(f32)
    half_rows = rows // 2
    left = iota((half_rows, LANES), 1) < P_SIZE
    edge = jnp.where(left, edge[:half_rows], pltpu.roll(edge[half_rows:], P_SIZE, axis=1))
    packed_ref[half:] = edge.astype(bf16)
    out_ref[...] = tile_ref[...]


def beside(high, low):
    left = iota(high.shape, 1) < P_SIZE
    return jnp.concatenate([high, jnp.where(left, low, 0.0)], axis=1).astype(bf16)


def tables_kernel(
    offsets_in,
    weights_ref,
    coarse_weights_ref,
    rows_ref,
    picks_ref,
    chosen_ref,
    forward_rows_ref,
    inverse_ref,
    inverse_rows_ref,
):
    offsets = offsets_in[...].astype(f32).reshape(1, 3)
    row_offset, column_offset, coarse_offset = (
        jnp.max(offsets[:, n : n + 1]).astype(jnp.int32) for n in range(3)
    )
    count = lax.axis_size("gx")
    per_row, bands = chosen_ref.shape
    supers = per_row // GROUP
    side = lax.axis_index("gz")
    gx_place = lax.axis_index("gx")
    shape = (2 * P_SIZE, LANES)
    lane = iota(shape, 1)
    row = iota(shape, 0)
    values = jnp.where(
        quotient(row, P_SIZE) == quotient(remainder(lane, P_SIZE), HALF),
        basis_values(remainder(lane, HALF), quotient(lane, P_SIZE), remainder(row, P_SIZE)),
        0.0,
    )
    padded = jnp.concatenate([values, jnp.zeros((2 * P_SIZE, LANES), f32)], axis=0)
    shape = (P_SIZE, LANES)
    row = iota(shape, 0)
    lane = iota(shape, 1)
    basis = basis_values(remainder(row, HALF), quotient(row, HALF), remainder(lane, P_SIZE))
    high, low = (value.astype(f32) for value in split(basis))
    forward_rows_ref[...] = beside(high, low)
    wide_high = jnp.concatenate([high] * 2, axis=1)
    wide_low = jnp.concatenate([low] * 2, axis=1)
    for kind in range(2):
        rows = slice(kind * HALF, (kind + 1) * HALF)
        for patch in range(GROUP):
            mine = quotient(iota((HALF, GROUP * P_SIZE), 1), P_SIZE) == patch
            at = (kind * GROUP + patch) * HALF
            for part, value in enumerate((wide_high, wide_high, wide_low)):
                begin = at + part * 2 * LANES
                inverse_ref[begin : begin + HALF] = jnp.where(mine, value[rows], 0.0).astype(bf16)
    kind = quotient(remainder(lane, P_SIZE), HALF)
    high, low = split(basis_values(remainder(lane, HALF), kind, row))
    inverse_rows_ref[...] = beside(high.astype(f32), low.astype(f32))
    shifts = [column_offset + STRIDE * ((t + side) % 2) for t in range(2)] + [coarse_offset]
    for t, shift in enumerate(shifts):
        moved = pltpu.roll(padded, shift, axis=0)
        for part, value in enumerate(split(moved)):
            rows = slice(part * 2 * LANES, (part + 1) * 2 * LANES)
            turned = pltpu.roll(value.astype(f32), P_SIZE, axis=1).astype(bf16)
            for order, entry in enumerate((value, turned)):
                if t < 2:
                    weights_ref[order, rows, t * LANES : (t + 1) * LANES] = entry
                else:
                    coarse_weights_ref[order, rows] = entry
    shape = (P_SIZE, 6 * STRIDE)
    number = iota(shape, 0)
    lane = iota(shape, 1)
    place = quotient(lane, P_SIZE) * STRIDE + remainder(lane, STRIDE) - row_offset
    values = jnp.where(
        (place >= 0) & (place < P_SIZE),
        basis_values(remainder(number, HALF), quotient(number, HALF), place),
        0.0,
    )
    high, low = split(values)
    is_low = remainder(lane, P_SIZE) >= STRIDE
    rows_ref[:P_SIZE] = high
    rows_ref[P_SIZE:] = jnp.where(is_low, 0.0, low.astype(f32)).astype(bf16)
    def pick(column):
        centre = (gx_place * (2 * per_row) + column) * STRIDE + column_offset + P_SIZE // 2
        return jnp.clip(quotient(quotient(centre, DOWN) - coarse_offset, P_SIZE), 0, count - 1)

    lane_row = iota((1, LANES), 1)
    for t in range(2):
        for g in range(supers):
            column = 2 * (g * GROUP + quotient(lane_row, HALF)) + remainder(t + side, 2)
            picks_ref[t, g] = jnp.broadcast_to(pick(column), (8, LANES))
    shape = (per_row, bands)
    parity = remainder(iota(shape, 1) + side, 2)
    chosen_ref[...] = pick(2 * iota(shape, 0) + parity)


def column_transform(strips, weights):
    rows = strips[0].shape[0]
    out = []
    for order in range(2):
        part = [x[:, order * LANES : (order + 2) * LANES] for x in strips]
        left = jnp.concatenate([jnp.concatenate([x, x], axis=1) for x in part], axis=0)
        out.append(matmul(left, weights[order]))
    return [[x[n * rows : (n + 1) * rows] for x in out] for n in range(len(strips))]


def pair_up(a, b):
    left = iota(a.shape, 1) < P_SIZE
    return jnp.where(left, a, b), pltpu.roll(jnp.where(left, b, a), P_SIZE, axis=1)


def forward_columns(image, stacked, weights):
    blocks = image.shape[1] // STRIDE
    supers = stacked.shape[3] // (2 * LANES)
    places = [(s, g) for s in range(2) for g in range(supers)]
    strips = [image[s, :, g * 2 * LANES : (2 * g + 3) * LANES] for s, g in places]
    for (s, g), (a, b) in zip(places, column_transform(strips, weights)):
        lane = g * 2 * LANES
        for t in range(2):
            half = slice(t * LANES, (t + 1) * LANES)
            for part, value in enumerate(pair_up(a[:, half], b[:, half])):
                high, low = split(value)
                at = slice(lane + part * LANES, lane + (part + 1) * LANES)
                for n in range(blocks):
                    block = slice(n * STRIDE, (n + 1) * STRIDE)
                    stacked[s, t, 2 * n * STRIDE : (2 * n + 1) * STRIDE, at] = high[block]
                    stacked[s, t, (2 * n + 1) * STRIDE : (2 * n + 2) * STRIDE, at] = low[block]


def forward_rows(stacked, left_rows, first_band, out_ref):
    bands, _, wide = out_ref.shape
    supers = wide // (2 * LANES)
    sign = jnp.where(lax.axis_index("gz") == 0, 1.0, -1.0).astype(f32)
    for i in range(bands):
        spectra = []
        for s in range(2):
            window = stacked[s, (first_band + i) % 2, 2 * STRIDE * i : 2 * STRIDE * (i + 3), :]
            spectra.append(add_row_halves(matmul(left_rows, window)))
        for g in range(supers):
            lane = g * 2 * LANES
            own = quads(spectra[0], g)
            other = quads(spectra[1], g)
            for begin, end, first in ROW_PARTS:
                out = cross_spectra(
                    [x[begin:end] for x in own], [x[begin:end] for x in other], sign, first
                )
                out_ref[i, begin:end, lane : lane + LANES] = out[0]
                out_ref[i, begin:end, lane + LANES : lane + 2 * LANES] = out[1]
                out_ref[i, HALF + begin : HALF + end, lane : lane + LANES] = out[2]
                out_ref[i, HALF + begin : HALF + end, lane + LANES : lane + 2 * LANES] = out[3]


def is_last(axis):
    return lax.axis_index(axis) == lax.axis_size(axis) - 1


def upper_kernel(group, weights, left_rows_ref, own_ref, other_ref, *refs):
    rights, (out_ref, image, stacked) = refs[:-3], refs[-3:]
    lane = group * 2 * LANES
    wide = 2 * LANES if rights else 3 * LANES
    for s, main in enumerate((own_ref, other_ref)):
        image[s, :, :wide] = main[:, lane : lane + wide]
        if rights:
            image[s, :, wide:] = unpack(rights[s][...])
    if rights:

        @pl.when(is_last("gx"))
        def _():
            image[:, :, wide:] = jnp.zeros((2, image.shape[1], LANES), bf16)

    forward_columns(image, stacked, weights)
    forward_rows(stacked, left_rows_ref[...], 0, out_ref)


def lower_image(own_ref, own_right_ref, own_low_ref, other_ref, other_right_ref, other_low_ref, image):
    rows, width = own_ref.shape
    inside = 1.0 - is_last("gx").astype(f32)
    above = 1.0 - is_last("gy").astype(f32)
    lane = iota((P_SIZE, width + LANES), 1)
    keep = jnp.where(lane < width, above, above * inside)
    for s, (main, right, low) in enumerate(
        ((own_ref, own_right_ref, own_low_ref), (other_ref, other_right_ref, other_low_ref))
    ):
        image[s, :P_SIZE, :width] = main[rows - P_SIZE :]
        edge = right[rows // 2 - P_SIZE :].astype(f32) * inside
        image[s, :P_SIZE, width:] = pltpu.roll(edge, P_SIZE, axis=1).astype(bf16)
        image[s, P_SIZE:] = (low[...].astype(f32) * keep).astype(bf16)


def inverse_columns(high, low, table_ref):
    return matmul(jnp.concatenate([high, low, high], axis=1), table_ref[...])


def row_transform(table_ref, high, low):
    return matmul(table_ref[:, : 3 * P_SIZE], jnp.concatenate([high, low, high], axis=0))


def coarse_peaks(strip, forward_rows_ref, inverse_ref, inverse_rows_ref, weights, sign):
    supers = len(strip) * 2 // GROUP
    strip = strip + [jnp.zeros_like(strip[0])]
    columns = []
    for g in range(supers):
        (pair,) = column_transform([jnp.concatenate(strip[2 * g : 2 * g + 3], axis=1)], weights)
        columns += pair_up(*pair)
    strips = jnp.concatenate(columns, axis=1)
    spectra = []
    for s in range(2):
        spectra.append(
            row_transform(forward_rows_ref, *split(strips[s * P_SIZE : (s + 1) * P_SIZE]))
        )
    peaks = []
    for g in range(supers):
        own = quads(spectra[0], g)
        other = quads(spectra[1], g)
        parts = []
        for begin, end, first in ROW_PARTS:
            shape = (end - begin, LANES)
            values = cross_spectra([x[begin:end] for x in own], [x[begin:end] for x in other], sign, first)
            corner = first_lane(shape) & (iota(shape, 0) == 0) & first
            turn = [
                jnp.where(corner, SCALE, c).astype(f32)
                for c in (2.0 * SCALE, 0.0, 2.0 * SCALE, 0.0)
            ]
            parts.append(coefficients(values, turn, first))
        cc, cs, sc, ss = (jnp.concatenate([a, b], axis=0) for a, b in zip(*parts))
        block = jnp.concatenate(
            [jnp.concatenate([cc, cs], axis=1), jnp.concatenate([sc, ss], axis=1)], axis=0
        )
        found = inverse_columns(*split(block), inverse_ref)
        sums = column_sums(row_transform(inverse_rows_ref, *split(found)))
        wide = [jnp.broadcast_to(x, (LANES, GROUP * P_SIZE)) for x in sums]
        peaks.append(band_peaks(*wide))
    return [jnp.concatenate(parts, axis=0) for parts in zip(*peaks)]


def turn_kernel(
    forward_rows_ref,
    inverse_ref,
    inverse_rows_ref,
    weights,
    picks_ref,
    chosen_ref,
    own_part_ref,
    other_part_ref,
    turns,
    base_ref,
    ordered,
):
    count = ordered.shape[0]
    supers = turns.shape[1]
    side = lax.axis_index("gz")
    place = lax.axis_index("gx")
    sign = jnp.where(side == 0, 1.0, -1.0).astype(f32)
    for step in range(count):
        for part, ref in enumerate((own_part_ref, other_part_ref)):
            tile = ref[step * HALF : (step + 1) * HALF].astype(f32)
            turned = pltpu.roll(tile, P_SIZE, axis=1)
            rows = slice(part * P_SIZE, (part + 1) * P_SIZE)
            ordered[place ^ step, 0, rows] = jnp.concatenate([tile, turned], axis=0)
            ordered[place ^ step, 1, rows] = jnp.concatenate([turned, tile], axis=0)
    left = iota((2 * P_SIZE, LANES), 1) < P_SIZE
    strip = []
    for j in range(0, count, 2):
        strip.append(jnp.where(left, ordered[j, 0], ordered[j + 1, 1]).astype(bf16))
    peaks = coarse_peaks(
        strip, forward_rows_ref, inverse_ref, inverse_rows_ref, weights, sign
    )
    blended = [
        (0.5 * DOWN) * (peak + jnp.sum(peak, axis=0, keepdims=True) / count) for peak in peaks
    ]

    def prior(pick):
        choice = pick == iota((count, LANES), 0)
        return [
            jnp.sum(jnp.where(choice, values, 0.0), axis=0, keepdims=True) for values in blended
        ]

    shape = (HALF, LANES)
    frequency_y = iota(shape, 0).astype(f32) * (1.0 / P_SIZE)
    l0 = first_lane(shape)
    r0 = iota(shape, 0) == 0
    lane_row = iota((1, LANES), 1)
    frequency_x = remainder(lane_row, HALF).astype(f32) * (1.0 / P_SIZE)
    for t in range(2):
        for g in range(supers):
            dy, dx = (
                value - P_SIZE * jnp.round(value * (1.0 / P_SIZE)) for value in prior(picks_ref[t, g, :1])
            )
            turn_y = nearest(frequency_y * dy)
            turn_x = nearest(frequency_x * dx)
            cy, sy = cosine_of_turns(turn_y), sine_of_turns(turn_y)
            cx, sx = cosine_of_turns(turn_x), sine_of_turns(turn_x)
            half_y = cosine_of_turns(nearest(0.5 * dy))
            half_x = cosine_of_turns(nearest(0.5 * dx))
            half_both = cosine_of_turns(nearest(0.5 * (dy + dx)))
            plus_real = cy * cx - sy * sx
            plus_imaginary = sy * cx + cy * sx
            minus_real = cy * cx + sy * sx
            minus_imaginary = sy * cx - cy * sx
            minus_real = jnp.where(l0, cy * half_x, jnp.where(r0, cx * half_y, minus_real))
            minus_imaginary = jnp.where(l0, sy * half_x, jnp.where(r0, sx * half_y, minus_imaginary))
            corner = l0 & r0
            turn = (plus_real, plus_imaginary, minus_real, minus_imaginary)
            ends = (1.0, half_x, half_y, half_both)
            for n in range(4):
                turns[t, g, n] = SCALE * jnp.where(corner, ends[n], 2.0 * turn[n])
    pick = chosen_ref[...]
    for axis, values in enumerate(blended):
        base = jnp.zeros(pick.shape, f32)
        for j in range(count):
            base = jnp.where(pick == j, values[j : j + 1, : pick.shape[1]], base)
        base_ref[axis] = base


def peak_kernel(
    inverse_ref,
    inverse_rows_ref,
    mask_ref,
    base_ref,
    turns,
    weights,
    left_rows_ref,
    *refs,
):
    halves, spectra = refs[:6], refs[6:-6]
    out_ref, image, stacked, lower_ref, high_ref, low_ref = refs[-6:]
    supers = turns.shape[1]
    per_row = supers * GROUP
    upper_bands = spectra[0].shape[0]
    bands = upper_bands + lower_ref.shape[0]

    def turn_band(i):
        for g in range(supers):
            lane = g * 2 * LANES
            if i < upper_bands:
                values = quads(spectra[g][i], 0)
            else:
                values = quads(lower_ref[i - upper_bands], g)
            parts = []
            for begin, end, first in ROW_PARTS:
                parts.append(
                    coefficients(
                        [x[begin:end] for x in values],
                        [turns[i % 2, g, n, begin:end] for n in range(4)],
                        first,
                    )
                )
            for n, (a, b) in enumerate(zip(*parts)):
                high, low = split(jnp.concatenate([a, b], axis=0))
                at = slice(i * P_SIZE + n // 2 * HALF, i * P_SIZE + (n // 2 + 1) * HALF)
                lanes = slice(lane + n % 2 * LANES, lane + (n % 2 + 1) * LANES)
                high_ref[at, lanes] = high
                low_ref[at, lanes] = low

    lower_image(*halves, image)
    forward_columns(image, stacked, weights)
    for i in range(upper_bands // 2):
        turn_band(i)
    forward_rows(stacked, left_rows_ref[...], upper_bands, lower_ref)
    for i in range(upper_bands // 2, bands):
        turn_band(i)
    for g in range(supers):
        at = slice(g * 2 * LANES, (g + 1) * 2 * LANES)
        high, low = split(inverse_columns(high_ref[:, at], low_ref[:, at], inverse_ref))
        high_ref[:, at] = high
        low_ref[:, at] = low
    sums = []
    for i in range(bands):
        rows = slice(i * P_SIZE, (i + 1) * P_SIZE)
        sums.append(column_sums(row_transform(inverse_rows_ref, high_ref[rows], low_ref[rows])))
    found = band_peaks(*(jnp.concatenate(parts, axis=0) for parts in zip(*sums)))
    shape = (per_row, 2 * per_row)
    columns = iota(shape, 1) - 2 * iota(shape, 0)
    mask = mask_ref[...].astype(f32).astype(bf16)
    masks = [
        lax.dot_general(
            (columns == n).astype(bf16),
            mask,
            (((1,), (1,)), ((), ())),
            preferred_element_type=f32,
        )
        for n in range(2)
    ]
    parity = remainder(iota((per_row, bands), 1) + lax.axis_index("gz"), 2)
    chosen = jnp.where(parity == 0, masks[0], masks[1])
    for axis in range(2):
        out_ref[axis, 0] = base_ref[axis] + chosen * found[axis]


def exchanged(value, axis, step):
    return lax.ppermute(value, axis, [(i, i ^ step) for i in range(lax.axis_size(axis))])


def from_next(value, axis):
    count = lax.axis_size(axis)
    got = []
    for odd in range(min(2, count - 1)):
        pairs = [(i, i + 1) for i in range(odd, count - 1, 2)]
        got.append(lax.ppermute(value, axis, pairs + [(j, i) for i, j in pairs]))
    if len(got) < 2:
        return got[0] if got else value
    return jnp.where(lax.axis_index(axis) % 2 == 0, got[0], got[1])


def swapped(value):
    return lax.ppermute(value, "gz", [(0, 1), (1, 0)])


VMEM = pl.BlockSpec(memory_space=pltpu.VMEM)
SMEM = pl.BlockSpec(memory_space=pltpu.SMEM)


def cost(microseconds):
    return pl.CostEstimate(
        flops=0, bytes_accessed=int(microseconds * 3.0e6), transcendentals=0
    )


def params(mebibytes):
    return pltpu.CompilerParams(vmem_limit_bytes=mebibytes * 2**20)


def local(sections, fine_offsets, coarse_offset, tissue_mask):
    own = sections[0]
    rows, width = own.shape
    bands = rows // STRIDE
    per_row = width // P_SIZE
    count = lax.axis_size("gx")
    assert rows == DOWN * P_SIZE and width == DOWN * P_SIZE
    assert count % GROUP == 0 and count & (count - 1) == 0
    wide = width
    supers = width // (2 * LANES)
    own_tile, own_edge, packed = pl.pallas_call(
        prepare_kernel,
        out_shape=(
            jax.ShapeDtypeStruct((rows, width), bf16),
            jax.ShapeDtypeStruct((P_SIZE, width), bf16),
            jax.ShapeDtypeStruct((HALF + rows // 2, LANES), bf16),
        ),
        in_specs=[VMEM],
        out_specs=(VMEM,) * 3,
        compiler_params=params(16),
        cost_estimate=cost(5.0),
    )(own)
    offsets = jnp.concatenate([fine_offsets, coarse_offset])
    tables = pl.pallas_call(
        tables_kernel,
        out_shape=(
            jax.ShapeDtypeStruct((2, 4 * LANES, 2 * LANES), bf16),
            jax.ShapeDtypeStruct((2, 4 * LANES, LANES), bf16),
            jax.ShapeDtypeStruct((2 * P_SIZE, 6 * STRIDE), bf16),
            jax.ShapeDtypeStruct((2, supers, 8, LANES), jnp.int32),
            jax.ShapeDtypeStruct((per_row, bands), jnp.int32),
            jax.ShapeDtypeStruct((P_SIZE, 2 * LANES), bf16),
            jax.ShapeDtypeStruct((6 * LANES, 2 * LANES), bf16),
            jax.ShapeDtypeStruct((P_SIZE, 2 * LANES), bf16),
        ),
        in_specs=[VMEM],
        out_specs=(VMEM,) * 8,
        compiler_params=params(16),
        cost_estimate=cost(0.1),
    )(offsets)
    weights, coarse_weights, left_rows, picks, chosen, forward_rows, inverse, inverse_rows = tables
    low_bands = P_SIZE // STRIDE
    other = swapped(own_tile)
    got_even = exchanged(packed, "gx", 1)
    got_odd = lax.ppermute(packed[HALF:], "gx", [(i + 1, i) for i in range(1, count - 1, 2)])
    right = jnp.where(lax.axis_index("gx") % 2 == 0, got_even[HALF:], got_odd)
    other_right = swapped(right)
    low_payload = jnp.concatenate([own_edge, right[:P_SIZE]], axis=1)
    low_payload, other_right = lax.optimization_barrier((low_payload, other_right))
    own_low = from_next(low_payload, "gy")
    tiles = jnp.concatenate([packed[:HALF], got_even[:HALF]], axis=0)
    step = 2
    while 2 * step < count:
        tiles = jnp.concatenate([tiles, exchanged(tiles, "gx", step)], axis=0)
        step *= 2
    last_tiles = exchanged(tiles, "gx", step)
    def upper(group, *operands):
        return pl.pallas_call(
            functools.partial(upper_kernel, group),
            out_shape=jax.ShapeDtypeStruct((bands - low_bands, P_SIZE, 2 * LANES), f32),
            in_specs=[VMEM] * (4 + len(operands)),
            out_specs=VMEM,
            scratch_shapes=[
                pltpu.VMEM((2, rows, 3 * LANES), bf16),
                pltpu.VMEM((2, 2, 2 * rows, 2 * LANES), bf16),
            ],
            compiler_params=params(32),
            cost_estimate=cost(0.1),
        )(weights, left_rows, own_tile, other, *operands)

    uppers = [upper(group) for group in range(supers - 1)]
    last_tiles, *uppers = lax.optimization_barrier((last_tiles, *uppers))
    tiles = jnp.concatenate([tiles, last_tiles], axis=0)
    other_tiles = swapped(tiles)
    uppers.append(upper(supers - 1, right, other_right))
    other_tiles, own_low, *uppers = lax.optimization_barrier((other_tiles, own_low, *uppers))
    turns, base = pl.pallas_call(
        turn_kernel,
        out_shape=(
            jax.ShapeDtypeStruct((2, supers, 4, HALF, LANES), f32),
            jax.ShapeDtypeStruct((2, per_row, bands), f32),
        ),
        in_specs=[VMEM] * 8,
        out_specs=(VMEM,) * 2,
        scratch_shapes=[pltpu.VMEM((count, 2, 2 * P_SIZE, LANES), f32)],
        compiler_params=params(32),
        cost_estimate=cost(0.1),
    )(
        forward_rows,
        inverse,
        inverse_rows,
        coarse_weights,
        picks,
        chosen,
        tiles,
        other_tiles,
    )
    other_low = swapped(own_low)
    flow = pl.pallas_call(
        peak_kernel,
        out_shape=jax.ShapeDtypeStruct((2, 1, per_row, bands), f32),
        in_specs=[VMEM] * (13 + supers),
        out_specs=VMEM,
        scratch_shapes=[
            pltpu.VMEM((2, 2 * P_SIZE, width + LANES), bf16),
            pltpu.VMEM((2, 2, 4 * P_SIZE, wide), bf16),
            pltpu.VMEM((low_bands, P_SIZE, wide), f32),
            pltpu.VMEM((bands * P_SIZE, wide), bf16),
            pltpu.VMEM((bands * P_SIZE, wide), bf16),
        ],
        compiler_params=params(40),
        cost_estimate=cost(0.1),
    )(
        inverse,
        inverse_rows,
        tissue_mask,
        base,
        turns,
        weights,
        left_rows,
        own_tile,
        right,
        own_low,
        other,
        other_right,
        other_low,
        *uppers,
    )
    return jnp.swapaxes(flow, 2, 3)


def solution(mesh):
    placed = (P("gz", ("pairs", "gy"), "gx"), P("pairs"), P("pairs"), P(("pairs", "gy"), "gx"))
    return jax.shard_map(
        local,
        mesh=mesh,
        in_specs=placed,
        out_specs=P(None, "gz", ("pairs", "gy"), "gx"),
        check_vma=False,
    )
```

```python
import functools
import math

import jax
import jax.numpy as jnp
from jax import lax
from jax.experimental import pallas as pl
from jax.experimental.pallas import tpu as pltpu
from jax.sharding import PartitionSpec as P

P_SIZE = 64
HALF = P_SIZE // 2
STRIDE = 32
DOWN = 8
LANES = 128
GROUP = LANES // HALF
SHARPNESS = 12.0
SCALE = SHARPNESS / float(P_SIZE) ** 4 * math.log2(math.e)

f32 = jnp.float32
bf16 = jnp.bfloat16


def cosine_of_turns(turns):
    square = (turns * (2.0 * math.pi)) ** 2
    total = jnp.full_like(square, 1.0 / math.factorial(20))
    for n in range(9, -1, -1):
        total = total * square + (-1.0) ** n / math.factorial(2 * n)
    return total


def sine_of_turns(turns):
    angle = turns * (2.0 * math.pi)
    square = angle * angle
    total = jnp.full_like(square, -1.0 / math.factorial(19))
    for n in range(8, -1, -1):
        total = total * square + (-1.0) ** n / math.factorial(2 * n + 1)
    return total * angle


def nearest(turns):
    return turns - jnp.round(turns)


def basis_values(frequency, kind, place):
    nyquist = (kind == 1) & (frequency == 0)
    number = jnp.where(nyquist, HALF, frequency)
    quarter = jnp.where((kind == 1) & (frequency != 0), P_SIZE // 4, 0)
    step = (number * place - quarter) & (P_SIZE - 1)
    step = jnp.where(step > HALF, P_SIZE - step, step)
    flip = step > P_SIZE // 4
    step = jnp.where(flip, HALF - step, step)
    square = (step.astype(f32) * (2.0 * math.pi / P_SIZE)) ** 2
    total = jnp.full_like(square, 1.0 / math.factorial(12))
    for n in range(5, -1, -1):
        total = total * square + (-1.0) ** n / math.factorial(2 * n)
    return jnp.where(flip, -total, total)


def quotient(number, divisor):
    return number >> (divisor.bit_length() - 1)


def remainder(number, divisor):
    return number & (divisor - 1)


def iota(shape, axis):
    return lax.broadcasted_iota(jnp.int32, shape, axis)


def split(values):
    high = values.astype(bf16)
    return high, (values - high.astype(f32)).astype(bf16)


def matmul(left, right):
    return jnp.dot(left, right, preferred_element_type=f32)


def add_row_halves(values):
    half = values.shape[0] // 2
    return values[:half] + values[half:]


def first_lane(shape):
    return remainder(iota(shape, 1), HALF) == 0


def half_spectra(cc, cs, sc, ss, first):
    shape = cc.shape
    l0 = first_lane(shape)
    if not first:
        return (
            cc - jnp.where(l0, 0.0, ss),
            sc + jnp.where(l0, 0.0, cs),
            jnp.where(l0, cs, cc + ss),
            jnp.where(l0, ss, sc - cs),
        )
    r0 = iota(shape, 0) == 0
    either = l0 | r0
    return (
        cc - jnp.where(either, 0.0, ss),
        jnp.where(r0, 0.0, sc) + jnp.where(l0, 0.0, cs),
        jnp.where(l0, cs, jnp.where(r0, sc, cc + ss)),
        jnp.where(either, ss, sc - cs),
    )


def cross_spectra(own, other, sign, first):
    a = half_spectra(*own, first)
    b = half_spectra(*other, first)
    out = []
    for r, i in ((0, 1), (2, 3)):
        out.append(b[r] * a[r] + b[i] * a[i])
        out.append(sign * (b[r] * a[i] - b[i] * a[r]))
    if first:
        shape = own[0].shape
        corner = first_lane(shape) & (iota(shape, 0) == 0)
        out = [jnp.where(corner, x * y, o) for x, y, o in zip(own, other, out)]
    return out


def coefficients(g, t, first):
    gpr, gpi, gmr, gmi = g
    tpr, tpi, tmr, tmi = t
    shape = gpr.shape
    l0 = first_lane(shape)
    hpr = gpr * tpr - gpi * tpi
    hpi = gpr * tpi + gpi * tpr
    hmr = gmr * tmr - gmi * tmi
    hmi = gmr * tmi + gmi * tmr
    if not first:
        return (
            hpr + jnp.where(l0, 0.0, hmr),
            jnp.where(l0, hmr, hmi - hpi),
            -hpi - jnp.where(l0, 0.0, hmi),
            jnp.where(l0, -hmi, hmr - hpr),
        )
    r0 = iota(shape, 0) == 0
    either = l0 | r0
    corner = l0 & r0
    out = (
        hpr + jnp.where(either, 0.0, hmr),
        jnp.where(l0, hmr, jnp.where(r0, 0.0, hmi) - hpi),
        jnp.where(r0, hmr, -hpi - jnp.where(l0, 0.0, hmi)),
        jnp.where(either, -hmi, hmr - hpr),
    )
    return [jnp.where(corner, x * y, o) for x, y, o in zip(g, t, out)]


def signed(number):
    return jnp.where(number >= HALF, number - P_SIZE, number).astype(f32)


def column_sums(logits):
    largest = jnp.max(logits, axis=0, keepdims=True)
    weights = jnp.exp2(logits - largest)
    rows = signed(iota((P_SIZE, 1), 0))
    return largest, jnp.sum(weights, axis=0, keepdims=True), jnp.sum(weights * rows, axis=0, keepdims=True)


def band_peaks(largest, total, moment):
    bands, wide = largest.shape
    largest, total, moment = (
        jnp.transpose(x).reshape(wide // P_SIZE, P_SIZE, bands) for x in (largest, total, moment)
    )
    factor = jnp.exp2(largest - jnp.max(largest, axis=1, keepdims=True))
    weight = factor * total
    columns = signed(lax.broadcasted_iota(jnp.int32, (1, P_SIZE, 1), 1))
    bottom = jnp.sum(weight, axis=1)
    return jnp.sum(factor * moment, axis=1) / bottom, jnp.sum(weight * columns, axis=1) / bottom


ROW_PARTS = ((0, 8, True), (8, HALF, False))


def quads(block, group):
    lane = group * 2 * LANES
    top, bottom = block[:HALF], block[HALF:]
    return (
        top[:, lane : lane + LANES],
        top[:, lane + LANES : lane + 2 * LANES],
        bottom[:, lane : lane + LANES],
        bottom[:, lane + LANES : lane + 2 * LANES],
    )


def from_right(refs, rows):
    even = lax.axis_index("gx") % 2 == 0
    return jnp.where(even, refs[0][rows].astype(f32), refs[1][rows].astype(f32))


def unpack(packed):
    wide = packed.astype(f32)
    return jnp.concatenate([wide, pltpu.roll(wide, P_SIZE, axis=1)], axis=0).astype(bf16)


def prepare_kernel(tile_ref, out_ref, low_ref, packed_ref):
    rows, width = tile_ref.shape
    columns = width // DOWN
    pick = quotient(iota((width, LANES), 0), DOWN) == remainder(iota((width, LANES), 1), columns)
    pick = pick.astype(bf16)
    left = iota((columns // 2, LANES), 1) < P_SIZE
    sums = matmul(tile_ref[...], pick)
    coarse = jnp.sum(sums.reshape(rows // DOWN, DOWN, LANES), axis=1) / DOWN
    half = coarse.shape[0] // 2
    packed_ref[:half] = jnp.where(left, coarse[:half], coarse[half:]).astype(bf16)
    low_ref[...] = tile_ref[:P_SIZE]
    edge = tile_ref[:, :LANES].astype(f32)
    half_rows = rows // 2
    left = iota((half_rows, LANES), 1) < P_SIZE
    edge = jnp.where(left, edge[:half_rows], pltpu.roll(edge[half_rows:], P_SIZE, axis=1))
    packed_ref[half:] = edge.astype(bf16)
    out_ref[...] = tile_ref[...]


def beside(high, low):
    left = iota(high.shape, 1) < P_SIZE
    return jnp.concatenate([high, jnp.where(left, low, 0.0)], axis=1).astype(bf16)


def tables_kernel(
    offsets_in,
    weights_ref,
    coarse_weights_ref,
    rows_ref,
    picks_ref,
    chosen_ref,
    forward_rows_ref,
    inverse_ref,
    inverse_rows_ref,
):
    offsets = offsets_in[...].astype(f32).reshape(1, 3)
    row_offset, column_offset, coarse_offset = (
        jnp.max(offsets[:, n : n + 1]).astype(jnp.int32) for n in range(3)
    )
    count = lax.axis_size("gx")
    per_row, bands = chosen_ref.shape
    supers = per_row // GROUP
    side = lax.axis_index("gz")
    gx_place = lax.axis_index("gx")
    shape = (2 * P_SIZE, LANES)
    lane = iota(shape, 1)
    row = iota(shape, 0)
    values = jnp.where(
        quotient(row, P_SIZE) == quotient(remainder(lane, P_SIZE), HALF),
        basis_values(remainder(lane, HALF), quotient(lane, P_SIZE), remainder(row, P_SIZE)),
        0.0,
    )
    padded = jnp.concatenate([values, jnp.zeros((2 * P_SIZE, LANES), f32)], axis=0)
    shape = (P_SIZE, LANES)
    row = iota(shape, 0)
    lane = iota(shape, 1)
    basis = basis_values(remainder(row, HALF), quotient(row, HALF), remainder(lane, P_SIZE))
    high, low = (value.astype(f32) for value in split(basis))
    forward_rows_ref[...] = beside(high, low)
    wide_high = jnp.concatenate([high] * 2, axis=1)
    wide_low = jnp.concatenate([low] * 2, axis=1)
    for kind in range(2):
        rows = slice(kind * HALF, (kind + 1) * HALF)
        for patch in range(GROUP):
            mine = quotient(iota((HALF, GROUP * P_SIZE), 1), P_SIZE) == patch
            at = (kind * GROUP + patch) * HALF
            for part, value in enumerate((wide_high, wide_high, wide_low)):
                begin = at + part * 2 * LANES
                inverse_ref[begin : begin + HALF] = jnp.where(mine, value[rows], 0.0).astype(bf16)
    kind = quotient(remainder(lane, P_SIZE), HALF)
    high, low = split(basis_values(remainder(lane, HALF), kind, row))
    inverse_rows_ref[...] = beside(high.astype(f32), low.astype(f32))
    shifts = [column_offset + STRIDE * ((t + side) % 2) for t in range(2)] + [coarse_offset]
    for t, shift in enumerate(shifts):
        moved = pltpu.roll(padded, shift, axis=0)
        for part, value in enumerate(split(moved)):
            rows = slice(part * 2 * LANES, (part + 1) * 2 * LANES)
            turned = pltpu.roll(value.astype(f32), P_SIZE, axis=1).astype(bf16)
            for order, entry in enumerate((value, turned)):
                if t < 2:
                    weights_ref[order, rows, t * LANES : (t + 1) * LANES] = entry
                else:
                    coarse_weights_ref[order, rows] = entry
    shape = (P_SIZE, 6 * STRIDE)
    number = iota(shape, 0)
    lane = iota(shape, 1)
    place = quotient(lane, P_SIZE) * STRIDE + remainder(lane, STRIDE) - row_offset
    values = jnp.where(
        (place >= 0) & (place < P_SIZE),
        basis_values(remainder(number, HALF), quotient(number, HALF), place),
        0.0,
    )
    high, low = split(values)
    is_low = remainder(lane, P_SIZE) >= STRIDE
    rows_ref[:P_SIZE] = high
    rows_ref[P_SIZE:] = jnp.where(is_low, 0.0, low.astype(f32)).astype(bf16)
    def pick(column):
        centre = (gx_place * (2 * per_row) + column) * STRIDE + column_offset + P_SIZE // 2
        return jnp.clip(quotient(quotient(centre, DOWN) - coarse_offset, P_SIZE), 0, count - 1)

    lane_row = iota((1, LANES), 1)
    for t in range(2):
        for g in range(supers):
            column = 2 * (g * GROUP + quotient(lane_row, HALF)) + remainder(t + side, 2)
            picks_ref[t, g] = jnp.broadcast_to(pick(column), (8, LANES))
    shape = (per_row, bands)
    parity = remainder(iota(shape, 1) + side, 2)
    chosen_ref[...] = pick(2 * iota(shape, 0) + parity)


def column_transform(strips, weights):
    rows = strips[0].shape[0]
    out = []
    for order in range(2):
        part = [x[:, order * LANES : (order + 2) * LANES] for x in strips]
        left = jnp.concatenate([jnp.concatenate([x, x], axis=1) for x in part], axis=0)
        out.append(matmul(left, weights[order]))
    return [[x[n * rows : (n + 1) * rows] for x in out] for n in range(len(strips))]


def pair_up(a, b):
    left = iota(a.shape, 1) < P_SIZE
    return jnp.where(left, a, b), pltpu.roll(jnp.where(left, b, a), P_SIZE, axis=1)


def forward_columns(image, stacked, weights):
    blocks = image.shape[1] // STRIDE
    supers = stacked.shape[3] // (2 * LANES)
    places = [(s, g) for s in range(2) for g in range(supers)]
    strips = [image[s, :, g * 2 * LANES : (2 * g + 3) * LANES] for s, g in places]
    for (s, g), (a, b) in zip(places, column_transform(strips, weights)):
        lane = g * 2 * LANES
        for t in range(2):
            half = slice(t * LANES, (t + 1) * LANES)
            for part, value in enumerate(pair_up(a[:, half], b[:, half])):
                high, low = split(value)
                at = slice(lane + part * LANES, lane + (part + 1) * LANES)
                for n in range(blocks):
                    block = slice(n * STRIDE, (n + 1) * STRIDE)
                    stacked[s, t, 2 * n * STRIDE : (2 * n + 1) * STRIDE, at] = high[block]
                    stacked[s, t, (2 * n + 1) * STRIDE : (2 * n + 2) * STRIDE, at] = low[block]


def forward_rows(stacked, left_rows, first_band, out_ref):
    bands, _, wide = out_ref.shape
    supers = wide // (2 * LANES)
    sign = jnp.where(lax.axis_index("gz") == 0, 1.0, -1.0).astype(f32)
    for i in range(bands):
        spectra = []
        for s in range(2):
            window = stacked[s, (first_band + i) % 2, 2 * STRIDE * i : 2 * STRIDE * (i + 3), :]
            spectra.append(add_row_halves(matmul(left_rows, window)))
        for g in range(supers):
            lane = g * 2 * LANES
            own = quads(spectra[0], g)
            other = quads(spectra[1], g)
            for begin, end, first in ROW_PARTS:
                out = cross_spectra(
                    [x[begin:end] for x in own], [x[begin:end] for x in other], sign, first
                )
                out_ref[i, begin:end, lane : lane + LANES] = out[0]
                out_ref[i, begin:end, lane + LANES : lane + 2 * LANES] = out[1]
                out_ref[i, HALF + begin : HALF + end, lane : lane + LANES] = out[2]
                out_ref[i, HALF + begin : HALF + end, lane + LANES : lane + 2 * LANES] = out[3]


def is_last(axis):
    return lax.axis_index(axis) == lax.axis_size(axis) - 1


def upper_kernel(group, weights, left_rows_ref, own_ref, other_ref, *refs):
    rights, (out_ref, image, stacked) = refs[:-3], refs[-3:]
    lane = group * 2 * LANES
    wide = 2 * LANES if rights else 3 * LANES
    for s, main in enumerate((own_ref, other_ref)):
        image[s, :, :wide] = main[:, lane : lane + wide]
        if rights:
            image[s, :, wide:] = unpack(from_right(rights[2 * s : 2 * s + 2], slice(None)))
    if rights:

        @pl.when(is_last("gx"))
        def _():
            image[:, :, wide:] = jnp.zeros((2, image.shape[1], LANES), bf16)

    forward_columns(image, stacked, weights)
    forward_rows(stacked, left_rows_ref[...], 0, out_ref)


def lower_image(own_ref, own_rights, own_low_ref, other_ref, other_rights, other_low_ref, image):
    rows, width = own_ref.shape
    inside = 1.0 - is_last("gx").astype(f32)
    above = 1.0 - is_last("gy").astype(f32)
    lane = iota((P_SIZE, width + LANES), 1)
    keep = jnp.where(lane < width, above, above * inside)
    for s, (main, right, low) in enumerate(
        ((own_ref, own_rights, own_low_ref), (other_ref, other_rights, other_low_ref))
    ):
        image[s, :P_SIZE, :width] = main[rows - P_SIZE :]
        edge = from_right(right, slice(rows // 2 - P_SIZE, None)) * inside
        image[s, :P_SIZE, width:] = pltpu.roll(edge, P_SIZE, axis=1).astype(bf16)
        image[s, P_SIZE:] = (low[...].astype(f32) * keep).astype(bf16)


def inverse_columns(high, low, table_ref):
    return matmul(jnp.concatenate([high, low, high], axis=1), table_ref[...])


def row_transform(table_ref, high, low):
    return matmul(table_ref[:, : 3 * P_SIZE], jnp.concatenate([high, low, high], axis=0))


def coarse_peaks(strip, forward_rows_ref, inverse_ref, inverse_rows_ref, weights, sign):
    supers = len(strip) * 2 // GROUP
    strip = strip + [jnp.zeros_like(strip[0])]
    columns = []
    for g in range(supers):
        (pair,) = column_transform([jnp.concatenate(strip[2 * g : 2 * g + 3], axis=1)], weights)
        columns += pair_up(*pair)
    strips = jnp.concatenate(columns, axis=1)
    spectra = []
    for s in range(2):
        spectra.append(
            row_transform(forward_rows_ref, *split(strips[s * P_SIZE : (s + 1) * P_SIZE]))
        )
    peaks = []
    for g in range(supers):
        own = quads(spectra[0], g)
        other = quads(spectra[1], g)
        parts = []
        for begin, end, first in ROW_PARTS:
            shape = (end - begin, LANES)
            values = cross_spectra([x[begin:end] for x in own], [x[begin:end] for x in other], sign, first)
            corner = first_lane(shape) & (iota(shape, 0) == 0) & first
            turn = [
                jnp.where(corner, SCALE, c).astype(f32)
                for c in (2.0 * SCALE, 0.0, 2.0 * SCALE, 0.0)
            ]
            parts.append(coefficients(values, turn, first))
        cc, cs, sc, ss = (jnp.concatenate([a, b], axis=0) for a, b in zip(*parts))
        block = jnp.concatenate(
            [jnp.concatenate([cc, cs], axis=1), jnp.concatenate([sc, ss], axis=1)], axis=0
        )
        found = inverse_columns(*split(block), inverse_ref)
        sums = column_sums(row_transform(inverse_rows_ref, *split(found)))
        wide = [jnp.broadcast_to(x, (LANES, GROUP * P_SIZE)) for x in sums]
        peaks.append(band_peaks(*wide))
    return [jnp.concatenate(parts, axis=0) for parts in zip(*peaks)]


def turn_kernel(
    forward_rows_ref,
    inverse_ref,
    inverse_rows_ref,
    weights,
    picks_ref,
    chosen_ref,
    own_part_ref,
    other_part_ref,
    turns,
    base_ref,
    ordered,
):
    count = ordered.shape[0]
    supers = turns.shape[1]
    side = lax.axis_index("gz")
    place = lax.axis_index("gx")
    sign = jnp.where(side == 0, 1.0, -1.0).astype(f32)
    for step in range(count):
        for part, ref in enumerate((own_part_ref, other_part_ref)):
            tile = ref[step * HALF : (step + 1) * HALF].astype(f32)
            turned = pltpu.roll(tile, P_SIZE, axis=1)
            rows = slice(part * P_SIZE, (part + 1) * P_SIZE)
            ordered[place ^ step, 0, rows] = jnp.concatenate([tile, turned], axis=0)
            ordered[place ^ step, 1, rows] = jnp.concatenate([turned, tile], axis=0)
    left = iota((2 * P_SIZE, LANES), 1) < P_SIZE
    strip = []
    for j in range(0, count, 2):
        strip.append(jnp.where(left, ordered[j, 0], ordered[j + 1, 1]).astype(bf16))
    peaks = coarse_peaks(
        strip, forward_rows_ref, inverse_ref, inverse_rows_ref, weights, sign
    )
    blended = [
        (0.5 * DOWN) * (peak + jnp.sum(peak, axis=0, keepdims=True) / count) for peak in peaks
    ]

    def prior(pick):
        choice = pick == iota((count, LANES), 0)
        return [
            jnp.sum(jnp.where(choice, values, 0.0), axis=0, keepdims=True) for values in blended
        ]

    shape = (HALF, LANES)
    frequency_y = iota(shape, 0).astype(f32) * (1.0 / P_SIZE)
    l0 = first_lane(shape)
    r0 = iota(shape, 0) == 0
    lane_row = iota((1, LANES), 1)
    frequency_x = remainder(lane_row, HALF).astype(f32) * (1.0 / P_SIZE)
    for t in range(2):
        for g in range(supers):
            dy, dx = (
                value - P_SIZE * jnp.round(value * (1.0 / P_SIZE)) for value in prior(picks_ref[t, g, :1])
            )
            turn_y = nearest(frequency_y * dy)
            turn_x = nearest(frequency_x * dx)
            cy, sy = cosine_of_turns(turn_y), sine_of_turns(turn_y)
            cx, sx = cosine_of_turns(turn_x), sine_of_turns(turn_x)
            half_y = cosine_of_turns(nearest(0.5 * dy))
            half_x = cosine_of_turns(nearest(0.5 * dx))
            half_both = cosine_of_turns(nearest(0.5 * (dy + dx)))
            plus_real = cy * cx - sy * sx
            plus_imaginary = sy * cx + cy * sx
            minus_real = cy * cx + sy * sx
            minus_imaginary = sy * cx - cy * sx
            minus_real = jnp.where(l0, cy * half_x, jnp.where(r0, cx * half_y, minus_real))
            minus_imaginary = jnp.where(l0, sy * half_x, jnp.where(r0, sx * half_y, minus_imaginary))
            corner = l0 & r0
            turn = (plus_real, plus_imaginary, minus_real, minus_imaginary)
            ends = (1.0, half_x, half_y, half_both)
            for n in range(4):
                turns[t, g, n] = SCALE * jnp.where(corner, ends[n], 2.0 * turn[n])
    pick = chosen_ref[...]
    for axis, values in enumerate(blended):
        base = jnp.zeros(pick.shape, f32)
        for j in range(count):
            base = jnp.where(pick == j, values[j : j + 1, : pick.shape[1]], base)
        base_ref[axis] = base


def peak_kernel(
    inverse_ref,
    inverse_rows_ref,
    mask_ref,
    base_ref,
    turns,
    weights,
    left_rows_ref,
    *refs,
):
    own_ref, *own_rights, own_low_ref, other_ref = refs[:5]
    *other_rights, other_low_ref = refs[5:8]
    spectra = refs[8:-6]
    out_ref, image, stacked, lower_ref, high_ref, low_ref = refs[-6:]
    supers = turns.shape[1]
    per_row = supers * GROUP
    upper_bands = spectra[0].shape[0]
    bands = upper_bands + lower_ref.shape[0]

    def turn_band(i):
        for g in range(supers):
            lane = g * 2 * LANES
            if i < upper_bands:
                values = quads(spectra[g][i], 0)
            else:
                values = quads(lower_ref[i - upper_bands], g)
            parts = []
            for begin, end, first in ROW_PARTS:
                parts.append(
                    coefficients(
                        [x[begin:end] for x in values],
                        [turns[i % 2, g, n, begin:end] for n in range(4)],
                        first,
                    )
                )
            for n, (a, b) in enumerate(zip(*parts)):
                high, low = split(jnp.concatenate([a, b], axis=0))
                at = slice(i * P_SIZE + n // 2 * HALF, i * P_SIZE + (n // 2 + 1) * HALF)
                lanes = slice(lane + n % 2 * LANES, lane + (n % 2 + 1) * LANES)
                high_ref[at, lanes] = high
                low_ref[at, lanes] = low

    lower_image(own_ref, own_rights, own_low_ref, other_ref, other_rights, other_low_ref, image)
    forward_columns(image, stacked, weights)
    for i in range(upper_bands // 2):
        turn_band(i)
    forward_rows(stacked, left_rows_ref[...], upper_bands, lower_ref)
    for i in range(upper_bands // 2, bands):
        turn_band(i)
    for g in range(supers):
        at = slice(g * 2 * LANES, (g + 1) * 2 * LANES)
        high, low = split(inverse_columns(high_ref[:, at], low_ref[:, at], inverse_ref))
        high_ref[:, at] = high
        low_ref[:, at] = low
    sums = []
    for i in range(bands):
        rows = slice(i * P_SIZE, (i + 1) * P_SIZE)
        sums.append(column_sums(row_transform(inverse_rows_ref, high_ref[rows], low_ref[rows])))
    found = band_peaks(*(jnp.concatenate(parts, axis=0) for parts in zip(*sums)))
    shape = (per_row, 2 * per_row)
    columns = iota(shape, 1) - 2 * iota(shape, 0)
    mask = mask_ref[...].astype(f32).astype(bf16)
    masks = [
        lax.dot_general(
            (columns == n).astype(bf16),
            mask,
            (((1,), (1,)), ((), ())),
            preferred_element_type=f32,
        )
        for n in range(2)
    ]
    parity = remainder(iota((per_row, bands), 1) + lax.axis_index("gz"), 2)
    chosen = jnp.where(parity == 0, masks[0], masks[1])
    for axis in range(2):
        out_ref[axis, 0] = base_ref[axis] + chosen * found[axis]


def exchanged(value, axis, step):
    return lax.ppermute(value, axis, [(i, i ^ step) for i in range(lax.axis_size(axis))])


def from_next(value, axis):
    count = lax.axis_size(axis)
    got = []
    for odd in range(min(2, count - 1)):
        pairs = [(i, i + 1) for i in range(odd, count - 1, 2)]
        got.append(lax.ppermute(value, axis, pairs + [(j, i) for i, j in pairs]))
    if len(got) < 2:
        return got[0] if got else value
    return jnp.where(lax.axis_index(axis) % 2 == 0, got[0], got[1])


def swapped(value):
    return lax.ppermute(value, "gz", [(0, 1), (1, 0)])


VMEM = pl.BlockSpec(memory_space=pltpu.VMEM)
SMEM = pl.BlockSpec(memory_space=pltpu.SMEM)


def cost(microseconds):
    return pl.CostEstimate(
        flops=0, bytes_accessed=int(microseconds * 3.0e6), transcendentals=0
    )


def params(mebibytes):
    return pltpu.CompilerParams(vmem_limit_bytes=mebibytes * 2**20)


def local(sections, fine_offsets, coarse_offset, tissue_mask):
    own = sections[0]
    rows, width = own.shape
    bands = rows // STRIDE
    per_row = width // P_SIZE
    count = lax.axis_size("gx")
    assert rows == DOWN * P_SIZE and width == DOWN * P_SIZE
    assert count % GROUP == 0 and count & (count - 1) == 0
    wide = width
    supers = width // (2 * LANES)
    own_tile, own_edge, packed = pl.pallas_call(
        prepare_kernel,
        out_shape=(
            jax.ShapeDtypeStruct((rows, width), bf16),
            jax.ShapeDtypeStruct((P_SIZE, width), bf16),
            jax.ShapeDtypeStruct((HALF + rows // 2, LANES), bf16),
        ),
        in_specs=[VMEM],
        out_specs=(VMEM,) * 3,
        compiler_params=params(16),
        cost_estimate=cost(5.0),
    )(own)
    offsets = jnp.concatenate([fine_offsets, coarse_offset])
    tables = pl.pallas_call(
        tables_kernel,
        out_shape=(
            jax.ShapeDtypeStruct((2, 4 * LANES, 2 * LANES), bf16),
            jax.ShapeDtypeStruct((2, 4 * LANES, LANES), bf16),
            jax.ShapeDtypeStruct((2 * P_SIZE, 6 * STRIDE), bf16),
            jax.ShapeDtypeStruct((2, supers, 8, LANES), jnp.int32),
            jax.ShapeDtypeStruct((per_row, bands), jnp.int32),
            jax.ShapeDtypeStruct((P_SIZE, 2 * LANES), bf16),
            jax.ShapeDtypeStruct((6 * LANES, 2 * LANES), bf16),
            jax.ShapeDtypeStruct((P_SIZE, 2 * LANES), bf16),
        ),
        in_specs=[VMEM],
        out_specs=(VMEM,) * 8,
        compiler_params=params(16),
        cost_estimate=cost(0.1),
    )(offsets)
    weights, coarse_weights, left_rows, picks, chosen, forward_rows, inverse, inverse_rows = tables
    low_bands = P_SIZE // STRIDE
    other = swapped(own_tile)
    got_even = exchanged(packed, "gx", 1)
    got_odd = lax.ppermute(packed[HALF:], "gx", [(i + 1, i) for i in range(1, count - 1, 2)])
    got_right = got_even[HALF:]
    other_right = swapped(got_right)
    got_odd, other_right = lax.optimization_barrier((got_odd, other_right))
    even = lax.axis_index("gx") % 2 == 0
    corner = jnp.where(even, got_right[:P_SIZE], got_odd[:P_SIZE])
    own_low = from_next(jnp.concatenate([own_edge, corner], axis=1), "gy")
    other_odd = swapped(got_odd)
    tiles = jnp.concatenate([packed[:HALF], got_even[:HALF]], axis=0)
    step = 2
    while 2 * step < count:
        tiles = jnp.concatenate([tiles, exchanged(tiles, "gx", step)], axis=0)
        step *= 2
    last_tiles = exchanged(tiles, "gx", step)
    def upper(group, *operands):
        return pl.pallas_call(
            functools.partial(upper_kernel, group),
            out_shape=jax.ShapeDtypeStruct((bands - low_bands, P_SIZE, 2 * LANES), f32),
            in_specs=[VMEM] * (4 + len(operands)),
            out_specs=VMEM,
            scratch_shapes=[
                pltpu.VMEM((2, rows, 3 * LANES), bf16),
                pltpu.VMEM((2, 2, 2 * rows, 2 * LANES), bf16),
            ],
            compiler_params=params(32),
            cost_estimate=cost(0.1),
        )(weights, left_rows, own_tile, other, *operands)

    uppers = [upper(group) for group in range(supers - 1)]
    last_tiles, *uppers = lax.optimization_barrier((last_tiles, *uppers))
    tiles = jnp.concatenate([tiles, last_tiles], axis=0)
    other_tiles = swapped(tiles)
    uppers.append(upper(supers - 1, got_right, got_odd, other_right, other_odd))
    other_tiles, own_low, *uppers = lax.optimization_barrier((other_tiles, own_low, *uppers))
    turns, base = pl.pallas_call(
        turn_kernel,
        out_shape=(
            jax.ShapeDtypeStruct((2, supers, 4, HALF, LANES), f32),
            jax.ShapeDtypeStruct((2, per_row, bands), f32),
        ),
        in_specs=[VMEM] * 8,
        out_specs=(VMEM,) * 2,
        scratch_shapes=[pltpu.VMEM((count, 2, 2 * P_SIZE, LANES), f32)],
        compiler_params=params(32),
        cost_estimate=cost(0.1),
    )(
        forward_rows,
        inverse,
        inverse_rows,
        coarse_weights,
        picks,
        chosen,
        tiles,
        other_tiles,
    )
    other_low = swapped(own_low)
    flow = pl.pallas_call(
        peak_kernel,
        out_shape=jax.ShapeDtypeStruct((2, 1, per_row, bands), f32),
        in_specs=[VMEM] * (15 + supers),
        out_specs=VMEM,
        scratch_shapes=[
            pltpu.VMEM((2, 2 * P_SIZE, width + LANES), bf16),
            pltpu.VMEM((2, 2, 4 * P_SIZE, wide), bf16),
            pltpu.VMEM((low_bands, P_SIZE, wide), f32),
            pltpu.VMEM((bands * P_SIZE, wide), bf16),
            pltpu.VMEM((bands * P_SIZE, wide), bf16),
        ],
        compiler_params=params(40),
        cost_estimate=cost(0.1),
    )(
        inverse,
        inverse_rows,
        tissue_mask,
        base,
        turns,
        weights,
        left_rows,
        own_tile,
        got_right,
        got_odd,
        own_low,
        other,
        other_right,
        other_odd,
        other_low,
        *uppers,
    )
    return jnp.swapaxes(flow, 2, 3)


def solution(mesh):
    placed = (P("gz", ("pairs", "gy"), "gx"), P("pairs"), P("pairs"), P(("pairs", "gy"), "gx"))
    return jax.shard_map(
        local,
        mesh=mesh,
        in_specs=placed,
        out_specs=P(None, "gz", ("pairs", "gy"), "gx"),
        check_vma=False,
    )
```

```python
import functools
import math

import jax
import jax.numpy as jnp
from jax import lax
from jax.experimental import pallas as pl
from jax.experimental.pallas import tpu as pltpu
from jax.sharding import PartitionSpec as P

P_SIZE = 64
HALF = P_SIZE // 2
STRIDE = 32
DOWN = 8
LANES = 128
GROUP = LANES // HALF
SHARPNESS = 12.0
SCALE = SHARPNESS / float(P_SIZE) ** 4 * math.log2(math.e)

f32 = jnp.float32
bf16 = jnp.bfloat16


def cosine_of_turns(turns):
    square = (turns * (2.0 * math.pi)) ** 2
    total = jnp.full_like(square, 1.0 / math.factorial(20))
    for n in range(9, -1, -1):
        total = total * square + (-1.0) ** n / math.factorial(2 * n)
    return total


def sine_of_turns(turns):
    angle = turns * (2.0 * math.pi)
    square = angle * angle
    total = jnp.full_like(square, -1.0 / math.factorial(19))
    for n in range(8, -1, -1):
        total = total * square + (-1.0) ** n / math.factorial(2 * n + 1)
    return total * angle


def nearest(turns):
    return turns - jnp.round(turns)


def basis_values(frequency, kind, place):
    nyquist = (kind == 1) & (frequency == 0)
    number = jnp.where(nyquist, HALF, frequency)
    quarter = jnp.where((kind == 1) & (frequency != 0), P_SIZE // 4, 0)
    step = (number * place - quarter) & (P_SIZE - 1)
    step = jnp.where(step > HALF, P_SIZE - step, step)
    flip = step > P_SIZE // 4
    step = jnp.where(flip, HALF - step, step)
    square = (step.astype(f32) * (2.0 * math.pi / P_SIZE)) ** 2
    total = jnp.full_like(square, 1.0 / math.factorial(12))
    for n in range(5, -1, -1):
        total = total * square + (-1.0) ** n / math.factorial(2 * n)
    return jnp.where(flip, -total, total)


def quotient(number, divisor):
    return number >> (divisor.bit_length() - 1)


def remainder(number, divisor):
    return number & (divisor - 1)


def iota(shape, axis):
    return lax.broadcasted_iota(jnp.int32, shape, axis)


def split(values):
    high = values.astype(bf16)
    return high, (values - high.astype(f32)).astype(bf16)


def matmul(left, right):
    return jnp.dot(left, right, preferred_element_type=f32)


def add_row_halves(values):
    half = values.shape[0] // 2
    return values[:half] + values[half:]


def first_lane(shape):
    return remainder(iota(shape, 1), HALF) == 0


def half_spectra(cc, cs, sc, ss, first):
    shape = cc.shape
    l0 = first_lane(shape)
    if not first:
        return (
            cc - jnp.where(l0, 0.0, ss),
            sc + jnp.where(l0, 0.0, cs),
            jnp.where(l0, cs, cc + ss),
            jnp.where(l0, ss, sc - cs),
        )
    r0 = iota(shape, 0) == 0
    either = l0 | r0
    return (
        cc - jnp.where(either, 0.0, ss),
        jnp.where(r0, 0.0, sc) + jnp.where(l0, 0.0, cs),
        jnp.where(l0, cs, jnp.where(r0, sc, cc + ss)),
        jnp.where(either, ss, sc - cs),
    )


def cross_spectra(own, other, sign, first):
    a = half_spectra(*own, first)
    b = half_spectra(*other, first)
    out = []
    for r, i in ((0, 1), (2, 3)):
        out.append(b[r] * a[r] + b[i] * a[i])
        out.append(sign * (b[r] * a[i] - b[i] * a[r]))
    if first:
        shape = own[0].shape
        corner = first_lane(shape) & (iota(shape, 0) == 0)
        out = [jnp.where(corner, x * y, o) for x, y, o in zip(own, other, out)]
    return out


def coefficients(g, t, first):
    gpr, gpi, gmr, gmi = g
    tpr, tpi, tmr, tmi = t
    shape = gpr.shape
    l0 = first_lane(shape)
    hpr = gpr * tpr - gpi * tpi
    hpi = gpr * tpi + gpi * tpr
    hmr = gmr * tmr - gmi * tmi
    hmi = gmr * tmi + gmi * tmr
    if not first:
        return (
            hpr + jnp.where(l0, 0.0, hmr),
            jnp.where(l0, hmr, hmi - hpi),
            -hpi - jnp.where(l0, 0.0, hmi),
            jnp.where(l0, -hmi, hmr - hpr),
        )
    r0 = iota(shape, 0) == 0
    either = l0 | r0
    corner = l0 & r0
    out = (
        hpr + jnp.where(either, 0.0, hmr),
        jnp.where(l0, hmr, jnp.where(r0, 0.0, hmi) - hpi),
        jnp.where(r0, hmr, -hpi - jnp.where(l0, 0.0, hmi)),
        jnp.where(either, -hmi, hmr - hpr),
    )
    return [jnp.where(corner, x * y, o) for x, y, o in zip(g, t, out)]


def signed(number):
    return jnp.where(number >= HALF, number - P_SIZE, number).astype(f32)


def column_sums(logits):
    largest = jnp.max(logits, axis=0, keepdims=True)
    weights = jnp.exp2(logits - largest)
    rows = signed(iota((P_SIZE, 1), 0))
    return largest, jnp.sum(weights, axis=0, keepdims=True), jnp.sum(weights * rows, axis=0, keepdims=True)


def band_peaks(largest, total, moment):
    bands, wide = largest.shape
    largest, total, moment = (
        jnp.transpose(x).reshape(wide // P_SIZE, P_SIZE, bands) for x in (largest, total, moment)
    )
    factor = jnp.exp2(largest - jnp.max(largest, axis=1, keepdims=True))
    weight = factor * total
    columns = signed(lax.broadcasted_iota(jnp.int32, (1, P_SIZE, 1), 1))
    bottom = jnp.sum(weight, axis=1)
    return jnp.sum(factor * moment, axis=1) / bottom, jnp.sum(weight * columns, axis=1) / bottom


ROW_PARTS = ((0, 8, True), (8, HALF, False))


def quads(block, group):
    lane = group * 2 * LANES
    top, bottom = block[:HALF], block[HALF:]
    return (
        top[:, lane : lane + LANES],
        top[:, lane + LANES : lane + 2 * LANES],
        bottom[:, lane : lane + LANES],
        bottom[:, lane + LANES : lane + 2 * LANES],
    )


def from_right(refs, rows):
    even = lax.axis_index("gx") % 2 == 0
    return jnp.where(even, refs[0][rows].astype(f32), refs[1][rows].astype(f32))


def unpack(packed):
    wide = packed.astype(f32)
    return jnp.concatenate([wide, pltpu.roll(wide, P_SIZE, axis=1)], axis=0).astype(bf16)


def prepare_kernel(tile_ref, out_ref, low_ref, packed_ref):
    rows, width = tile_ref.shape
    columns = width // DOWN
    pick = quotient(iota((width, LANES), 0), DOWN) == remainder(iota((width, LANES), 1), columns)
    pick = pick.astype(bf16)
    left = iota((columns // 2, LANES), 1) < P_SIZE
    sums = matmul(tile_ref[...], pick)
    coarse = jnp.sum(sums.reshape(rows // DOWN, DOWN, LANES), axis=1) / DOWN
    half = coarse.shape[0] // 2
    packed_ref[:half] = jnp.where(left, coarse[:half], coarse[half:]).astype(bf16)
    low_ref[...] = tile_ref[:P_SIZE]
    edge = tile_ref[:, :LANES].astype(f32)
    half_rows = rows // 2
    left = iota((half_rows, LANES), 1) < P_SIZE
    edge = jnp.where(left, edge[:half_rows], pltpu.roll(edge[half_rows:], P_SIZE, axis=1))
    packed_ref[half:] = edge.astype(bf16)
    out_ref[...] = tile_ref[...]


def beside(high, low):
    left = iota(high.shape, 1) < P_SIZE
    return jnp.concatenate([high, jnp.where(left, low, 0.0)], axis=1).astype(bf16)


def tables_kernel(
    offsets_in,
    weights_ref,
    coarse_weights_ref,
    rows_ref,
    picks_ref,
    chosen_ref,
    forward_rows_ref,
    inverse_ref,
    inverse_rows_ref,
):
    offsets = offsets_in[...].astype(f32).reshape(1, 3)
    row_offset, column_offset, coarse_offset = (
        jnp.max(offsets[:, n : n + 1]).astype(jnp.int32) for n in range(3)
    )
    count = lax.axis_size("gx")
    per_row, bands = chosen_ref.shape
    supers = per_row // GROUP
    side = lax.axis_index("gz")
    gx_place = lax.axis_index("gx")
    shape = (2 * P_SIZE, LANES)
    lane = iota(shape, 1)
    row = iota(shape, 0)
    values = jnp.where(
        quotient(row, P_SIZE) == quotient(remainder(lane, P_SIZE), HALF),
        basis_values(remainder(lane, HALF), quotient(lane, P_SIZE), remainder(row, P_SIZE)),
        0.0,
    )
    padded = jnp.concatenate([values, jnp.zeros((2 * P_SIZE, LANES), f32)], axis=0)
    shape = (P_SIZE, LANES)
    row = iota(shape, 0)
    lane = iota(shape, 1)
    basis = basis_values(remainder(row, HALF), quotient(row, HALF), remainder(lane, P_SIZE))
    high, low = (value.astype(f32) for value in split(basis))
    forward_rows_ref[...] = beside(high, low)
    wide_high = jnp.concatenate([high] * 2, axis=1)
    wide_low = jnp.concatenate([low] * 2, axis=1)
    for kind in range(2):
        rows = slice(kind * HALF, (kind + 1) * HALF)
        for patch in range(GROUP):
            mine = quotient(iota((HALF, GROUP * P_SIZE), 1), P_SIZE) == patch
            at = (kind * GROUP + patch) * HALF
            for part, value in enumerate((wide_high, wide_high, wide_low)):
                begin = at + part * 2 * LANES
                inverse_ref[begin : begin + HALF] = jnp.where(mine, value[rows], 0.0).astype(bf16)
    kind = quotient(remainder(lane, P_SIZE), HALF)
    high, low = split(basis_values(remainder(lane, HALF), kind, row))
    inverse_rows_ref[...] = beside(high.astype(f32), low.astype(f32))
    shifts = [column_offset + STRIDE * ((t + side) % 2) for t in range(2)] + [coarse_offset]
    for t, shift in enumerate(shifts):
        moved = pltpu.roll(padded, shift, axis=0)
        for part, value in enumerate(split(moved)):
            rows = slice(part * 2 * LANES, (part + 1) * 2 * LANES)
            turned = pltpu.roll(value.astype(f32), P_SIZE, axis=1).astype(bf16)
            for order, entry in enumerate((value, turned)):
                if t < 2:
                    weights_ref[order, rows, t * LANES : (t + 1) * LANES] = entry
                else:
                    coarse_weights_ref[order, rows] = entry
    shape = (P_SIZE, 6 * STRIDE)
    number = iota(shape, 0)
    lane = iota(shape, 1)
    place = quotient(lane, P_SIZE) * STRIDE + remainder(lane, STRIDE) - row_offset
    values = jnp.where(
        (place >= 0) & (place < P_SIZE),
        basis_values(remainder(number, HALF), quotient(number, HALF), place),
        0.0,
    )
    high, low = split(values)
    is_low = remainder(lane, P_SIZE) >= STRIDE
    rows_ref[:P_SIZE] = high
    rows_ref[P_SIZE:] = jnp.where(is_low, 0.0, low.astype(f32)).astype(bf16)
    def pick(column):
        centre = (gx_place * (2 * per_row) + column) * STRIDE + column_offset + P_SIZE // 2
        return jnp.clip(quotient(quotient(centre, DOWN) - coarse_offset, P_SIZE), 0, count - 1)

    lane_row = iota((1, LANES), 1)
    for t in range(2):
        for g in range(supers):
            column = 2 * (g * GROUP + quotient(lane_row, HALF)) + remainder(t + side, 2)
            picks_ref[t, g] = jnp.broadcast_to(pick(column), (8, LANES))
    shape = (per_row, bands)
    parity = remainder(iota(shape, 1) + side, 2)
    chosen_ref[...] = pick(2 * iota(shape, 0) + parity)


def column_transform(strips, weights):
    rows = strips[0].shape[0]
    out = []
    for order in range(2):
        part = [x[:, order * LANES : (order + 2) * LANES] for x in strips]
        left = jnp.concatenate([jnp.concatenate([x, x], axis=1) for x in part], axis=0)
        out.append(matmul(left, weights[order]))
    return [[x[n * rows : (n + 1) * rows] for x in out] for n in range(len(strips))]


def pair_up(a, b):
    left = iota(a.shape, 1) < P_SIZE
    return jnp.where(left, a, b), pltpu.roll(jnp.where(left, b, a), P_SIZE, axis=1)


def forward_columns(image, stacked, weights, first_block=0):
    blocks = image.shape[1] // STRIDE
    supers = stacked.shape[3] // (2 * LANES)
    places = [(s, g) for s in range(2) for g in range(supers)]
    strips = [image[s, :, g * 2 * LANES : (2 * g + 3) * LANES] for s, g in places]
    for (s, g), (a, b) in zip(places, column_transform(strips, weights)):
        lane = g * 2 * LANES
        for t in range(2):
            half = slice(t * LANES, (t + 1) * LANES)
            for part, value in enumerate(pair_up(a[:, half], b[:, half])):
                high, low = split(value)
                at = slice(lane + part * LANES, lane + (part + 1) * LANES)
                for n in range(blocks):
                    block = slice(n * STRIDE, (n + 1) * STRIDE)
                    begin = 2 * (first_block + n) * STRIDE
                    stacked[s, t, begin : begin + STRIDE, at] = high[block]
                    stacked[s, t, begin + STRIDE : begin + 2 * STRIDE, at] = low[block]


def forward_rows(stacked, left_rows, first_band, out_ref):
    bands, _, wide = out_ref.shape
    supers = wide // (2 * LANES)
    sign = jnp.where(lax.axis_index("gz") == 0, 1.0, -1.0).astype(f32)
    for i in range(bands):
        spectra = []
        for s in range(2):
            window = stacked[s, (first_band + i) % 2, 2 * STRIDE * i : 2 * STRIDE * (i + 3), :]
            spectra.append(add_row_halves(matmul(left_rows, window)))
        for g in range(supers):
            lane = g * 2 * LANES
            own = quads(spectra[0], g)
            other = quads(spectra[1], g)
            for begin, end, first in ROW_PARTS:
                out = cross_spectra(
                    [x[begin:end] for x in own], [x[begin:end] for x in other], sign, first
                )
                out_ref[i, begin:end, lane : lane + LANES] = out[0]
                out_ref[i, begin:end, lane + LANES : lane + 2 * LANES] = out[1]
                out_ref[i, HALF + begin : HALF + end, lane : lane + LANES] = out[2]
                out_ref[i, HALF + begin : HALF + end, lane + LANES : lane + 2 * LANES] = out[3]


def is_last(axis):
    return lax.axis_index(axis) == lax.axis_size(axis) - 1


def upper_kernel(group, weights, left_rows_ref, own_ref, other_ref, *refs):
    rights, (out_ref, tail_ref, image, stacked) = refs[:-4], refs[-4:]
    lane = group * 2 * LANES
    wide = 2 * LANES if rights else 3 * LANES
    for s, main in enumerate((own_ref, other_ref)):
        image[s, :, :wide] = main[:, lane : lane + wide]
        if rights:
            image[s, :, wide:] = unpack(from_right(rights[2 * s : 2 * s + 2], slice(None)))
    if rights:

        @pl.when(is_last("gx"))
        def _():
            image[:, :, wide:] = jnp.zeros((2, image.shape[1], LANES), bf16)

    forward_columns(image, stacked, weights)
    tail_ref[...] = stacked[:, :, stacked.shape[2] - 2 * P_SIZE :]
    forward_rows(stacked, left_rows_ref[...], 0, out_ref)


def lower_image(own_low_ref, other_low_ref, image):
    shape = own_low_ref.shape
    inside = 1.0 - is_last("gx").astype(f32)
    above = 1.0 - is_last("gy").astype(f32)
    keep = jnp.where(iota(shape, 1) < shape[1] - LANES, above, above * inside)
    for s, low in enumerate((own_low_ref, other_low_ref)):
        image[s] = (low[...].astype(f32) * keep).astype(bf16)


def inverse_columns(high, low, table_ref):
    return matmul(jnp.concatenate([high, low, high], axis=1), table_ref[...])


def row_transform(table_ref, high, low):
    return matmul(table_ref[:, : 3 * P_SIZE], jnp.concatenate([high, low, high], axis=0))


def coarse_peaks(strip, forward_rows_ref, inverse_ref, inverse_rows_ref, weights, sign):
    supers = len(strip) * 2 // GROUP
    strip = strip + [jnp.zeros_like(strip[0])]
    columns = []
    for g in range(supers):
        (pair,) = column_transform([jnp.concatenate(strip[2 * g : 2 * g + 3], axis=1)], weights)
        columns += pair_up(*pair)
    strips = jnp.concatenate(columns, axis=1)
    spectra = []
    for s in range(2):
        spectra.append(
            row_transform(forward_rows_ref, *split(strips[s * P_SIZE : (s + 1) * P_SIZE]))
        )
    peaks = []
    for g in range(supers):
        own = quads(spectra[0], g)
        other = quads(spectra[1], g)
        parts = []
        for begin, end, first in ROW_PARTS:
            shape = (end - begin, LANES)
            values = cross_spectra([x[begin:end] for x in own], [x[begin:end] for x in other], sign, first)
            corner = first_lane(shape) & (iota(shape, 0) == 0) & first
            turn = [
                jnp.where(corner, SCALE, c).astype(f32)
                for c in (2.0 * SCALE, 0.0, 2.0 * SCALE, 0.0)
            ]
            parts.append(coefficients(values, turn, first))
        cc, cs, sc, ss = (jnp.concatenate([a, b], axis=0) for a, b in zip(*parts))
        block = jnp.concatenate(
            [jnp.concatenate([cc, cs], axis=1), jnp.concatenate([sc, ss], axis=1)], axis=0
        )
        found = inverse_columns(*split(block), inverse_ref)
        sums = column_sums(row_transform(inverse_rows_ref, *split(found)))
        wide = [jnp.broadcast_to(x, (LANES, GROUP * P_SIZE)) for x in sums]
        peaks.append(band_peaks(*wide))
    return [jnp.concatenate(parts, axis=0) for parts in zip(*peaks)]


def turn_kernel(
    forward_rows_ref,
    inverse_ref,
    inverse_rows_ref,
    weights,
    picks_ref,
    chosen_ref,
    own_part_ref,
    other_part_ref,
    turns,
    base_ref,
    ordered,
):
    count = ordered.shape[0]
    supers = turns.shape[1]
    side = lax.axis_index("gz")
    place = lax.axis_index("gx")
    sign = jnp.where(side == 0, 1.0, -1.0).astype(f32)
    for step in range(count):
        for part, ref in enumerate((own_part_ref, other_part_ref)):
            tile = ref[step * HALF : (step + 1) * HALF].astype(f32)
            turned = pltpu.roll(tile, P_SIZE, axis=1)
            rows = slice(part * P_SIZE, (part + 1) * P_SIZE)
            ordered[place ^ step, 0, rows] = jnp.concatenate([tile, turned], axis=0)
            ordered[place ^ step, 1, rows] = jnp.concatenate([turned, tile], axis=0)
    left = iota((2 * P_SIZE, LANES), 1) < P_SIZE
    strip = []
    for j in range(0, count, 2):
        strip.append(jnp.where(left, ordered[j, 0], ordered[j + 1, 1]).astype(bf16))
    peaks = coarse_peaks(
        strip, forward_rows_ref, inverse_ref, inverse_rows_ref, weights, sign
    )
    blended = [
        (0.5 * DOWN) * (peak + jnp.sum(peak, axis=0, keepdims=True) / count) for peak in peaks
    ]

    def prior(pick):
        choice = pick == iota((count, LANES), 0)
        return [
            jnp.sum(jnp.where(choice, values, 0.0), axis=0, keepdims=True) for values in blended
        ]

    shape = (HALF, LANES)
    frequency_y = iota(shape, 0).astype(f32) * (1.0 / P_SIZE)
    l0 = first_lane(shape)
    r0 = iota(shape, 0) == 0
    lane_row = iota((1, LANES), 1)
    frequency_x = remainder(lane_row, HALF).astype(f32) * (1.0 / P_SIZE)
    for t in range(2):
        for g in range(supers):
            dy, dx = (
                value - P_SIZE * jnp.round(value * (1.0 / P_SIZE)) for value in prior(picks_ref[t, g, :1])
            )
            turn_y = nearest(frequency_y * dy)
            turn_x = nearest(frequency_x * dx)
            cy, sy = cosine_of_turns(turn_y), sine_of_turns(turn_y)
            cx, sx = cosine_of_turns(turn_x), sine_of_turns(turn_x)
            half_y = cosine_of_turns(nearest(0.5 * dy))
            half_x = cosine_of_turns(nearest(0.5 * dx))
            half_both = cosine_of_turns(nearest(0.5 * (dy + dx)))
            plus_real = cy * cx - sy * sx
            plus_imaginary = sy * cx + cy * sx
            minus_real = cy * cx + sy * sx
            minus_imaginary = sy * cx - cy * sx
            minus_real = jnp.where(l0, cy * half_x, jnp.where(r0, cx * half_y, minus_real))
            minus_imaginary = jnp.where(l0, sy * half_x, jnp.where(r0, sx * half_y, minus_imaginary))
            corner = l0 & r0
            turn = (plus_real, plus_imaginary, minus_real, minus_imaginary)
            ends = (1.0, half_x, half_y, half_both)
            for n in range(4):
                turns[t, g, n] = SCALE * jnp.where(corner, ends[n], 2.0 * turn[n])
    pick = chosen_ref[...]
    for axis, values in enumerate(blended):
        base = jnp.zeros(pick.shape, f32)
        for j in range(count):
            base = jnp.where(pick == j, values[j : j + 1, : pick.shape[1]], base)
        base_ref[axis] = base


def peak_kernel(
    inverse_ref,
    inverse_rows_ref,
    mask_ref,
    base_ref,
    turns,
    weights,
    left_rows_ref,
    own_low_ref,
    other_low_ref,
    *refs,
):
    out_ref, image, stacked, lower_ref, high_ref, low_ref = refs[-6:]
    supers = turns.shape[1]
    tails, spectra = refs[:supers], refs[supers : 2 * supers]
    per_row = supers * GROUP
    upper_bands = spectra[0].shape[0]
    bands = upper_bands + lower_ref.shape[0]

    def turn_band(i):
        for g in range(supers):
            lane = g * 2 * LANES
            if i < upper_bands:
                values = quads(spectra[g][i], 0)
            else:
                values = quads(lower_ref[i - upper_bands], g)
            parts = []
            for begin, end, first in ROW_PARTS:
                parts.append(
                    coefficients(
                        [x[begin:end] for x in values],
                        [turns[i % 2, g, n, begin:end] for n in range(4)],
                        first,
                    )
                )
            for n, (a, b) in enumerate(zip(*parts)):
                high, low = split(jnp.concatenate([a, b], axis=0))
                at = slice(i * P_SIZE + n // 2 * HALF, i * P_SIZE + (n // 2 + 1) * HALF)
                lanes = slice(lane + n % 2 * LANES, lane + (n % 2 + 1) * LANES)
                high_ref[at, lanes] = high
                low_ref[at, lanes] = low

    lower_image(own_low_ref, other_low_ref, image)
    for g in range(supers):
        stacked[:, :, : 2 * P_SIZE, g * 2 * LANES : (g + 1) * 2 * LANES] = tails[g][...]
    forward_columns(image, stacked, weights, P_SIZE // STRIDE)
    for i in range(upper_bands // 2):
        turn_band(i)
    forward_rows(stacked, left_rows_ref[...], upper_bands, lower_ref)
    for i in range(upper_bands // 2, bands):
        turn_band(i)
    for g in range(supers):
        at = slice(g * 2 * LANES, (g + 1) * 2 * LANES)
        high, low = split(inverse_columns(high_ref[:, at], low_ref[:, at], inverse_ref))
        high_ref[:, at] = high
        low_ref[:, at] = low
    sums = []
    for i in range(bands):
        rows = slice(i * P_SIZE, (i + 1) * P_SIZE)
        sums.append(column_sums(row_transform(inverse_rows_ref, high_ref[rows], low_ref[rows])))
    found = band_peaks(*(jnp.concatenate(parts, axis=0) for parts in zip(*sums)))
    shape = (per_row, 2 * per_row)
    columns = iota(shape, 1) - 2 * iota(shape, 0)
    mask = mask_ref[...].astype(f32).astype(bf16)
    masks = [
        lax.dot_general(
            (columns == n).astype(bf16),
            mask,
            (((1,), (1,)), ((), ())),
            preferred_element_type=f32,
        )
        for n in range(2)
    ]
    parity = remainder(iota((per_row, bands), 1) + lax.axis_index("gz"), 2)
    chosen = jnp.where(parity == 0, masks[0], masks[1])
    for axis in range(2):
        out_ref[axis, 0] = base_ref[axis] + chosen * found[axis]


def exchanged(value, axis, step):
    return lax.ppermute(value, axis, [(i, i ^ step) for i in range(lax.axis_size(axis))])


def from_next(value, axis):
    count = lax.axis_size(axis)
    got = []
    for odd in range(min(2, count - 1)):
        pairs = [(i, i + 1) for i in range(odd, count - 1, 2)]
        got.append(lax.ppermute(value, axis, pairs + [(j, i) for i, j in pairs]))
    if len(got) < 2:
        return got[0] if got else value
    return jnp.where(lax.axis_index(axis) % 2 == 0, got[0], got[1])


def swapped(value):
    return lax.ppermute(value, "gz", [(0, 1), (1, 0)])


VMEM = pl.BlockSpec(memory_space=pltpu.VMEM)
SMEM = pl.BlockSpec(memory_space=pltpu.SMEM)


def cost(microseconds):
    return pl.CostEstimate(
        flops=0, bytes_accessed=int(microseconds * 3.0e6), transcendentals=0
    )


def params(mebibytes):
    return pltpu.CompilerParams(vmem_limit_bytes=mebibytes * 2**20)


def local(sections, fine_offsets, coarse_offset, tissue_mask):
    own = sections[0]
    rows, width = own.shape
    bands = rows // STRIDE
    per_row = width // P_SIZE
    count = lax.axis_size("gx")
    assert rows == DOWN * P_SIZE and width == DOWN * P_SIZE
    assert count % GROUP == 0 and count & (count - 1) == 0
    wide = width
    supers = width // (2 * LANES)
    own_tile, own_edge, packed = pl.pallas_call(
        prepare_kernel,
        out_shape=(
            jax.ShapeDtypeStruct((rows, width), bf16),
            jax.ShapeDtypeStruct((P_SIZE, width), bf16),
            jax.ShapeDtypeStruct((HALF + rows // 2, LANES), bf16),
        ),
        in_specs=[VMEM],
        out_specs=(VMEM,) * 3,
        compiler_params=params(16),
        cost_estimate=cost(5.0),
    )(own)
    offsets = jnp.concatenate([fine_offsets, coarse_offset])
    tables = pl.pallas_call(
        tables_kernel,
        out_shape=(
            jax.ShapeDtypeStruct((2, 4 * LANES, 2 * LANES), bf16),
            jax.ShapeDtypeStruct((2, 4 * LANES, LANES), bf16),
            jax.ShapeDtypeStruct((2 * P_SIZE, 6 * STRIDE), bf16),
            jax.ShapeDtypeStruct((2, supers, 8, LANES), jnp.int32),
            jax.ShapeDtypeStruct((per_row, bands), jnp.int32),
            jax.ShapeDtypeStruct((P_SIZE, 2 * LANES), bf16),
            jax.ShapeDtypeStruct((6 * LANES, 2 * LANES), bf16),
            jax.ShapeDtypeStruct((P_SIZE, 2 * LANES), bf16),
        ),
        in_specs=[VMEM],
        out_specs=(VMEM,) * 8,
        compiler_params=params(16),
        cost_estimate=cost(0.1),
    )(offsets)
    weights, coarse_weights, left_rows, picks, chosen, forward_rows, inverse, inverse_rows = tables
    low_bands = P_SIZE // STRIDE
    other = swapped(own_tile)
    got_even = exchanged(packed, "gx", 1)
    got_odd = lax.ppermute(packed[HALF:], "gx", [(i + 1, i) for i in range(1, count - 1, 2)])
    got_right = got_even[HALF:]
    other_right = swapped(got_right)
    got_odd, other_right = lax.optimization_barrier((got_odd, other_right))
    even = lax.axis_index("gx") % 2 == 0
    corner = jnp.where(even, got_right[:P_SIZE], got_odd[:P_SIZE])
    own_low = from_next(jnp.concatenate([own_edge, corner], axis=1), "gy")
    other_odd = swapped(got_odd)
    tiles = jnp.concatenate([packed[:HALF], got_even[:HALF]], axis=0)
    step = 2
    while 2 * step < count:
        tiles = jnp.concatenate([tiles, exchanged(tiles, "gx", step)], axis=0)
        step *= 2
    last_tiles = exchanged(tiles, "gx", step)
    def upper(group, *operands):
        return pl.pallas_call(
            functools.partial(upper_kernel, group),
            out_shape=(
                jax.ShapeDtypeStruct((bands - low_bands, P_SIZE, 2 * LANES), f32),
                jax.ShapeDtypeStruct((2, 2, 2 * P_SIZE, 2 * LANES), bf16),
            ),
            in_specs=[VMEM] * (4 + len(operands)),
            out_specs=(VMEM,) * 2,
            scratch_shapes=[
                pltpu.VMEM((2, rows, 3 * LANES), bf16),
                pltpu.VMEM((2, 2, 2 * rows, 2 * LANES), bf16),
            ],
            compiler_params=params(32),
            cost_estimate=cost(0.1),
        )(weights, left_rows, own_tile, other, *operands)

    uppers = [upper(group) for group in range(supers - 1)]
    last_tiles, *uppers = lax.optimization_barrier((last_tiles, *uppers))
    tiles = jnp.concatenate([tiles, last_tiles], axis=0)
    other_tiles = swapped(tiles)
    uppers.append(upper(supers - 1, got_right, got_odd, other_right, other_odd))
    other_tiles, own_low, *uppers = lax.optimization_barrier((other_tiles, own_low, *uppers))
    turns, base = pl.pallas_call(
        turn_kernel,
        out_shape=(
            jax.ShapeDtypeStruct((2, supers, 4, HALF, LANES), f32),
            jax.ShapeDtypeStruct((2, per_row, bands), f32),
        ),
        in_specs=[VMEM] * 8,
        out_specs=(VMEM,) * 2,
        scratch_shapes=[pltpu.VMEM((count, 2, 2 * P_SIZE, LANES), f32)],
        compiler_params=params(32),
        cost_estimate=cost(0.1),
    )(
        forward_rows,
        inverse,
        inverse_rows,
        coarse_weights,
        picks,
        chosen,
        tiles,
        other_tiles,
    )
    other_low = swapped(own_low)
    flow = pl.pallas_call(
        peak_kernel,
        out_shape=jax.ShapeDtypeStruct((2, 1, per_row, bands), f32),
        in_specs=[VMEM] * (9 + 2 * supers),
        out_specs=VMEM,
        scratch_shapes=[
            pltpu.VMEM((2, P_SIZE, width + LANES), bf16),
            pltpu.VMEM((2, 2, 4 * P_SIZE, wide), bf16),
            pltpu.VMEM((low_bands, P_SIZE, wide), f32),
            pltpu.VMEM((bands * P_SIZE, wide), bf16),
            pltpu.VMEM((bands * P_SIZE, wide), bf16),
        ],
        compiler_params=params(40),
        cost_estimate=cost(0.1),
    )(
        inverse,
        inverse_rows,
        tissue_mask,
        base,
        turns,
        weights,
        left_rows,
        own_low,
        other_low,
        *(tail for _, tail in uppers),
        *(spectra for spectra, _ in uppers),
    )
    return jnp.swapaxes(flow, 2, 3)


def solution(mesh):
    placed = (P("gz", ("pairs", "gy"), "gx"), P("pairs"), P("pairs"), P(("pairs", "gy"), "gx"))
    return jax.shard_map(
        local,
        mesh=mesh,
        in_specs=placed,
        out_specs=P(None, "gz", ("pairs", "gy"), "gx"),
        check_vma=False,
    )
```

```python
import functools
import math

import jax
import jax.numpy as jnp
from jax import lax
from jax.experimental import pallas as pl
from jax.experimental.pallas import tpu as pltpu
from jax.sharding import PartitionSpec as P

P_SIZE = 64
HALF = P_SIZE // 2
STRIDE = 32
DOWN = 8
LANES = 128
GROUP = LANES // HALF
SHARPNESS = 12.0
SUBLANES = 8
SCALE = SHARPNESS / float(P_SIZE) ** 4 * math.log2(math.e)

f32 = jnp.float32
bf16 = jnp.bfloat16


def cosine_of_turns(turns):
    square = (turns * (2.0 * math.pi)) ** 2
    total = jnp.full_like(square, 1.0 / math.factorial(20))
    for n in range(9, -1, -1):
        total = total * square + (-1.0) ** n / math.factorial(2 * n)
    return total


def sine_of_turns(turns):
    angle = turns * (2.0 * math.pi)
    square = angle * angle
    total = jnp.full_like(square, -1.0 / math.factorial(19))
    for n in range(8, -1, -1):
        total = total * square + (-1.0) ** n / math.factorial(2 * n + 1)
    return total * angle


def nearest(turns):
    return turns - jnp.round(turns)


def basis_values(frequency, kind, place):
    nyquist = (kind == 1) & (frequency == 0)
    number = jnp.where(nyquist, HALF, frequency)
    quarter = jnp.where((kind == 1) & (frequency != 0), P_SIZE // 4, 0)
    step = (number * place - quarter) & (P_SIZE - 1)
    step = jnp.where(step > HALF, P_SIZE - step, step)
    flip = step > P_SIZE // 4
    step = jnp.where(flip, HALF - step, step)
    square = (step.astype(f32) * (2.0 * math.pi / P_SIZE)) ** 2
    total = jnp.full_like(square, 1.0 / math.factorial(12))
    for n in range(5, -1, -1):
        total = total * square + (-1.0) ** n / math.factorial(2 * n)
    return jnp.where(flip, -total, total)


def quotient(number, divisor):
    return number >> (divisor.bit_length() - 1)


def remainder(number, divisor):
    return number & (divisor - 1)


def iota(shape, axis):
    return lax.broadcasted_iota(jnp.int32, shape, axis)


def split(values):
    high = values.astype(bf16)
    return high, (values - high.astype(f32)).astype(bf16)


def matmul(left, right):
    return jnp.dot(left, right, preferred_element_type=f32)


def add_row_halves(values):
    half = values.shape[0] // 2
    return values[:half] + values[half:]


def first_lane(shape):
    return remainder(iota(shape, 1), HALF) == 0


def half_spectra(cc, cs, sc, ss, first):
    shape = cc.shape
    l0 = first_lane(shape)
    if not first:
        return (
            cc - jnp.where(l0, 0.0, ss),
            sc + jnp.where(l0, 0.0, cs),
            jnp.where(l0, cs, cc + ss),
            jnp.where(l0, ss, sc - cs),
        )
    r0 = iota(shape, 0) == 0
    either = l0 | r0
    return (
        cc - jnp.where(either, 0.0, ss),
        jnp.where(r0, 0.0, sc) + jnp.where(l0, 0.0, cs),
        jnp.where(l0, cs, jnp.where(r0, sc, cc + ss)),
        jnp.where(either, ss, sc - cs),
    )


def cross_spectra(own, other, sign, first):
    a = half_spectra(*own, first)
    b = half_spectra(*other, first)
    out = []
    for r, i in ((0, 1), (2, 3)):
        out.append(b[r] * a[r] + b[i] * a[i])
        out.append(sign * (b[r] * a[i] - b[i] * a[r]))
    if first:
        shape = own[0].shape
        corner = first_lane(shape) & (iota(shape, 0) == 0)
        out = [jnp.where(corner, x * y, o) for x, y, o in zip(own, other, out)]
    return out


def coefficients(g, t, first):
    gpr, gpi, gmr, gmi = g
    tpr, tpi, tmr, tmi = t
    shape = gpr.shape
    l0 = first_lane(shape)
    hpr = gpr * tpr - gpi * tpi
    hpi = gpr * tpi + gpi * tpr
    hmr = gmr * tmr - gmi * tmi
    hmi = gmr * tmi + gmi * tmr
    if not first:
        return (
            hpr + jnp.where(l0, 0.0, hmr),
            jnp.where(l0, hmr, hmi - hpi),
            -hpi - jnp.where(l0, 0.0, hmi),
            jnp.where(l0, -hmi, hmr - hpr),
        )
    r0 = iota(shape, 0) == 0
    either = l0 | r0
    corner = l0 & r0
    out = (
        hpr + jnp.where(either, 0.0, hmr),
        jnp.where(l0, hmr, jnp.where(r0, 0.0, hmi) - hpi),
        jnp.where(r0, hmr, -hpi - jnp.where(l0, 0.0, hmi)),
        jnp.where(either, -hmi, hmr - hpr),
    )
    return [jnp.where(corner, x * y, o) for x, y, o in zip(g, t, out)]


def signed(number):
    return jnp.where(number >= HALF, number - P_SIZE, number).astype(f32)


def column_sums(logits):
    largest = jnp.max(logits, axis=0, keepdims=True)
    weights = jnp.exp2(logits - largest)
    rows = signed(iota((P_SIZE, 1), 0))
    return largest, jnp.sum(weights, axis=0, keepdims=True), jnp.sum(weights * rows, axis=0, keepdims=True)


def band_peaks(largest, total, moment):
    bands, wide = largest.shape
    largest, total, moment = (
        jnp.transpose(x).reshape(wide // P_SIZE, P_SIZE, bands) for x in (largest, total, moment)
    )
    factor = jnp.exp2(largest - jnp.max(largest, axis=1, keepdims=True))
    weight = factor * total
    columns = signed(lax.broadcasted_iota(jnp.int32, (1, P_SIZE, 1), 1))
    bottom = jnp.sum(weight, axis=1)
    return jnp.sum(factor * moment, axis=1) / bottom, jnp.sum(weight * columns, axis=1) / bottom


ROW_PARTS = ((0, 8, True), (8, HALF, False))


def quads(block, group):
    lane = group * 2 * LANES
    top, bottom = block[:HALF], block[HALF:]
    return (
        top[:, lane : lane + LANES],
        top[:, lane + LANES : lane + 2 * LANES],
        bottom[:, lane : lane + LANES],
        bottom[:, lane + LANES : lane + 2 * LANES],
    )


def from_right(refs, rows):
    even = lax.axis_index("gx") % 2 == 0
    return jnp.where(even, refs[0][rows].astype(f32), refs[1][rows].astype(f32))


def unpack(packed):
    wide = packed.astype(f32)
    return jnp.concatenate([wide, pltpu.roll(wide, P_SIZE, axis=1)], axis=0).astype(bf16)


def prepare_kernel(tile_ref, out_ref, low_ref, packed_ref):
    rows, width = tile_ref.shape
    columns = width // DOWN
    pick = quotient(iota((width, LANES), 0), DOWN) == remainder(iota((width, LANES), 1), columns)
    pick = pick.astype(bf16)
    left = iota((columns // 2, LANES), 1) < P_SIZE
    sums = matmul(tile_ref[...], pick)
    coarse = jnp.sum(sums.reshape(rows // DOWN, DOWN, LANES), axis=1) / DOWN
    half = coarse.shape[0] // 2
    packed_ref[:half] = jnp.where(left, coarse[:half], coarse[half:]).astype(bf16)
    low_ref[...] = tile_ref[:P_SIZE]
    edge = tile_ref[:, :LANES].astype(f32)
    half_rows = rows // 2
    left = iota((half_rows, LANES), 1) < P_SIZE
    edge = jnp.where(left, edge[:half_rows], pltpu.roll(edge[half_rows:], P_SIZE, axis=1))
    packed_ref[half:] = edge.astype(bf16)
    out_ref[...] = tile_ref[...]


def beside(high, low):
    left = iota(high.shape, 1) < P_SIZE
    return jnp.concatenate([high, jnp.where(left, low, 0.0)], axis=1).astype(bf16)


def tables_kernel(
    offsets_in,
    weights_ref,
    coarse_weights_ref,
    rows_ref,
    picks_ref,
    chosen_ref,
    forward_rows_ref,
    inverse_ref,
    inverse_rows_ref,
):
    offsets = offsets_in[...].astype(f32).reshape(1, 3)
    row_offset, column_offset, coarse_offset = (
        jnp.max(offsets[:, n : n + 1]).astype(jnp.int32) for n in range(3)
    )
    count = lax.axis_size("gx")
    per_row, bands = chosen_ref.shape
    supers = per_row // GROUP
    side = lax.axis_index("gz")
    gx_place = lax.axis_index("gx")
    shape = (2 * P_SIZE, LANES)
    lane = iota(shape, 1)
    row = iota(shape, 0)
    values = jnp.where(
        quotient(row, P_SIZE) == quotient(remainder(lane, P_SIZE), HALF),
        basis_values(remainder(lane, HALF), quotient(lane, P_SIZE), remainder(row, P_SIZE)),
        0.0,
    )
    padded = jnp.concatenate([values, jnp.zeros((2 * P_SIZE, LANES), f32)], axis=0)
    shape = (P_SIZE, LANES)
    row = iota(shape, 0)
    lane = iota(shape, 1)
    basis = basis_values(remainder(row, HALF), quotient(row, HALF), remainder(lane, P_SIZE))
    high, low = (value.astype(f32) for value in split(basis))
    forward_rows_ref[...] = beside(high, low)
    wide_high = jnp.concatenate([high] * 2, axis=1)
    wide_low = jnp.concatenate([low] * 2, axis=1)
    for kind in range(2):
        rows = slice(kind * HALF, (kind + 1) * HALF)
        for patch in range(GROUP):
            mine = quotient(iota((HALF, GROUP * P_SIZE), 1), P_SIZE) == patch
            at = (kind * GROUP + patch) * HALF
            for part, value in enumerate((wide_high, wide_high, wide_low)):
                begin = at + part * 2 * LANES
                inverse_ref[begin : begin + HALF] = jnp.where(mine, value[rows], 0.0).astype(bf16)
    kind = quotient(remainder(lane, P_SIZE), HALF)
    high, low = split(basis_values(remainder(lane, HALF), kind, row))
    inverse_rows_ref[...] = beside(high.astype(f32), low.astype(f32))
    shifts = [column_offset + STRIDE * ((t + side) % 2) for t in range(2)] + [coarse_offset]
    for t, shift in enumerate(shifts):
        moved = pltpu.roll(padded, shift, axis=0)
        for part, value in enumerate(split(moved)):
            rows = slice(part * 2 * LANES, (part + 1) * 2 * LANES)
            turned = pltpu.roll(value.astype(f32), P_SIZE, axis=1).astype(bf16)
            for order, entry in enumerate((value, turned)):
                if t < 2:
                    weights_ref[order, rows, t * LANES : (t + 1) * LANES] = entry
                else:
                    coarse_weights_ref[order, rows] = entry
    shape = (P_SIZE, 6 * STRIDE)
    number = iota(shape, 0)
    lane = iota(shape, 1)
    place = quotient(lane, P_SIZE) * STRIDE + remainder(lane, STRIDE) - row_offset
    values = jnp.where(
        (place >= 0) & (place < P_SIZE),
        basis_values(remainder(number, HALF), quotient(number, HALF), place),
        0.0,
    )
    high, low = split(values)
    is_low = remainder(lane, P_SIZE) >= STRIDE
    rows_ref[:P_SIZE] = high
    rows_ref[P_SIZE:] = jnp.where(is_low, 0.0, low.astype(f32)).astype(bf16)
    def pick(column):
        centre = (gx_place * (2 * per_row) + column) * STRIDE + column_offset + P_SIZE // 2
        return jnp.clip(quotient(quotient(centre, DOWN) - coarse_offset, P_SIZE), 0, count - 1)

    lane_row = iota((1, LANES), 1)
    for t in range(2):
        for g in range(supers):
            column = 2 * (g * GROUP + quotient(lane_row, HALF)) + remainder(t + side, 2)
            picks_ref[t, g] = jnp.broadcast_to(pick(column), (8, LANES))
    shape = (per_row, bands)
    parity = remainder(iota(shape, 1) + side, 2)
    chosen_ref[...] = pick(2 * iota(shape, 0) + parity)


def column_transform(strips, weights):
    rows = strips[0].shape[0]
    out = []
    for order in range(2):
        part = [x[:, order * LANES : (order + 2) * LANES] for x in strips]
        left = jnp.concatenate([jnp.concatenate([x, x], axis=1) for x in part], axis=0)
        out.append(matmul(left, weights[order]))
    return [[x[n * rows : (n + 1) * rows] for x in out] for n in range(len(strips))]


def pair_up(a, b):
    left = iota(a.shape, 1) < P_SIZE
    return jnp.where(left, a, b), pltpu.roll(jnp.where(left, b, a), P_SIZE, axis=1)


def forward_columns(image, stacked, weights, first_block=0):
    blocks = image.shape[1] // STRIDE
    supers = stacked.shape[3] // (2 * LANES)
    places = [(s, g) for s in range(2) for g in range(supers)]
    strips = [image[s, :, g * 2 * LANES : (2 * g + 3) * LANES] for s, g in places]
    for (s, g), (a, b) in zip(places, column_transform(strips, weights)):
        lane = g * 2 * LANES
        for t in range(2):
            half = slice(t * LANES, (t + 1) * LANES)
            for part, value in enumerate(pair_up(a[:, half], b[:, half])):
                high, low = split(value)
                at = slice(lane + part * LANES, lane + (part + 1) * LANES)
                for n in range(blocks):
                    block = slice(n * STRIDE, (n + 1) * STRIDE)
                    begin = 2 * (first_block + n) * STRIDE
                    stacked[s, t, begin : begin + STRIDE, at] = high[block]
                    stacked[s, t, begin + STRIDE : begin + 2 * STRIDE, at] = low[block]


def forward_rows(stacked, left_rows, first_band, out_ref):
    bands, _, wide = out_ref.shape
    supers = wide // (2 * LANES)
    sign = jnp.where(lax.axis_index("gz") == 0, 1.0, -1.0).astype(f32)
    for i in range(bands):
        spectra = []
        for s in range(2):
            window = stacked[s, (first_band + i) % 2, 2 * STRIDE * i : 2 * STRIDE * (i + 3), :]
            spectra.append(add_row_halves(matmul(left_rows, window)))
        for g in range(supers):
            lane = g * 2 * LANES
            own = quads(spectra[0], g)
            other = quads(spectra[1], g)
            for begin, end, first in ROW_PARTS:
                out = cross_spectra(
                    [x[begin:end] for x in own], [x[begin:end] for x in other], sign, first
                )
                out_ref[i, begin:end, lane : lane + LANES] = out[0]
                out_ref[i, begin:end, lane + LANES : lane + 2 * LANES] = out[1]
                out_ref[i, HALF + begin : HALF + end, lane : lane + LANES] = out[2]
                out_ref[i, HALF + begin : HALF + end, lane + LANES : lane + 2 * LANES] = out[3]


def is_last(axis):
    return lax.axis_index(axis) == lax.axis_size(axis) - 1


def upper_kernel(group, weights, left_rows_ref, own_ref, other_ref, *refs):
    rights, (out_ref, tail_ref, image, stacked) = refs[:-4], refs[-4:]
    lane = group * 2 * LANES
    wide = 2 * LANES if rights else 3 * LANES
    for s, main in enumerate((own_ref, other_ref)):
        image[s, :, :wide] = main[:, lane : lane + wide]
        if rights:
            image[s, :, wide:] = unpack(from_right(rights[2 * s : 2 * s + 2], slice(None)))
    if rights:

        @pl.when(is_last("gx"))
        def _():
            image[:, :, wide:] = jnp.zeros((2, image.shape[1], LANES), bf16)

    forward_columns(image, stacked, weights)
    tail_ref[...] = stacked[:, :, stacked.shape[2] - 2 * P_SIZE :]
    forward_rows(stacked, left_rows_ref[...], 0, out_ref)


def lower_image(own_low_ref, other_low_ref, image):
    shape = own_low_ref.shape
    inside = 1.0 - is_last("gx").astype(f32)
    above = 1.0 - is_last("gy").astype(f32)
    keep = jnp.where(iota(shape, 1) < shape[1] - LANES, above, above * inside)
    for s, low in enumerate((own_low_ref, other_low_ref)):
        image[s] = (low[...].astype(f32) * keep).astype(bf16)


def inverse_columns(high, low, table_ref):
    return matmul(jnp.concatenate([high, low, high], axis=1), table_ref[...])


def row_transform(table_ref, high, low):
    return matmul(table_ref[:, : 3 * P_SIZE], jnp.concatenate([high, low, high], axis=0))


def coarse_peaks(strip, forward_rows_ref, inverse_ref, inverse_rows_ref, weights, sign):
    supers = len(strip) * 2 // GROUP
    strip = strip + [jnp.zeros_like(strip[0])]
    columns = []
    for g in range(supers):
        (pair,) = column_transform([jnp.concatenate(strip[2 * g : 2 * g + 3], axis=1)], weights)
        columns += pair_up(*pair)
    strips = jnp.concatenate(columns, axis=1)
    spectra = []
    for s in range(2):
        spectra.append(
            row_transform(forward_rows_ref, *split(strips[s * P_SIZE : (s + 1) * P_SIZE]))
        )
    peaks = []
    for g in range(supers):
        own = quads(spectra[0], g)
        other = quads(spectra[1], g)
        parts = []
        for begin, end, first in ROW_PARTS:
            shape = (end - begin, LANES)
            values = cross_spectra([x[begin:end] for x in own], [x[begin:end] for x in other], sign, first)
            corner = first_lane(shape) & (iota(shape, 0) == 0) & first
            turn = [
                jnp.where(corner, SCALE, c).astype(f32)
                for c in (2.0 * SCALE, 0.0, 2.0 * SCALE, 0.0)
            ]
            parts.append(coefficients(values, turn, first))
        cc, cs, sc, ss = (jnp.concatenate([a, b], axis=0) for a, b in zip(*parts))
        block = jnp.concatenate(
            [jnp.concatenate([cc, cs], axis=1), jnp.concatenate([sc, ss], axis=1)], axis=0
        )
        found = inverse_columns(*split(block), inverse_ref)
        sums = column_sums(row_transform(inverse_rows_ref, *split(found)))
        wide = [jnp.broadcast_to(x, (LANES, GROUP * P_SIZE)) for x in sums]
        peaks.append(band_peaks(*wide))
    return [jnp.concatenate(parts, axis=0) for parts in zip(*peaks)]


def turn_kernel(
    forward_rows_ref,
    inverse_ref,
    inverse_rows_ref,
    weights,
    picks_ref,
    chosen_ref,
    own_part_ref,
    other_part_ref,
    turns,
    base_ref,
    ordered,
):
    count = ordered.shape[0]
    supers = turns.shape[1]
    side = lax.axis_index("gz")
    place = lax.axis_index("gx")
    sign = jnp.where(side == 0, 1.0, -1.0).astype(f32)
    for step in range(count):
        for part, ref in enumerate((own_part_ref, other_part_ref)):
            tile = ref[step * HALF : (step + 1) * HALF].astype(f32)
            turned = pltpu.roll(tile, P_SIZE, axis=1)
            rows = slice(part * P_SIZE, (part + 1) * P_SIZE)
            ordered[place ^ step, 0, rows] = jnp.concatenate([tile, turned], axis=0)
            ordered[place ^ step, 1, rows] = jnp.concatenate([turned, tile], axis=0)
    left = iota((2 * P_SIZE, LANES), 1) < P_SIZE
    strip = []
    for j in range(0, count, 2):
        strip.append(jnp.where(left, ordered[j, 0], ordered[j + 1, 1]).astype(bf16))
    peaks = coarse_peaks(
        strip, forward_rows_ref, inverse_ref, inverse_rows_ref, weights, sign
    )
    blended = [
        (0.5 * DOWN) * (peak + jnp.sum(peak, axis=0, keepdims=True) / count) for peak in peaks
    ]

    def prior(pick):
        choice = pick == iota((count, LANES), 0)
        return [
            jnp.sum(jnp.where(choice, values, 0.0), axis=0, keepdims=True) for values in blended
        ]

    shape = (HALF, LANES)
    l0 = first_lane(shape)
    r0 = iota(shape, 0) == 0
    row = iota((SUBLANES, LANES), 0)
    steps = row.astype(f32) * (1.0 / P_SIZE)
    frequency_x = remainder(iota((1, LANES), 1), HALF).astype(f32) * (1.0 / P_SIZE)
    blocks = HALF // SUBLANES
    for t in range(2):
        for g in range(supers):
            dy, dx = (
                value - P_SIZE * jnp.round(value * (1.0 / P_SIZE)) for value in prior(picks_ref[t, g, :1])
            )
            few = SUBLANES * steps * dy
            for n, value in enumerate((frequency_x * dx, 0.5 * dy, 0.5 * dx, 0.5 * (dy + dx))):
                few = jnp.where(row == blocks + n, value, few)
            few = nearest(few)
            near = nearest(steps * dy)
            few_cosine, few_sine = cosine_of_turns(few), sine_of_turns(few)
            cosine, sine = cosine_of_turns(near), sine_of_turns(near)
            cy, sy = [], []
            for n in range(blocks):
                c, s = few_cosine[n : n + 1], few_sine[n : n + 1]
                cy.append(cosine * c - sine * s)
                sy.append(sine * c + cosine * s)
            cy, sy = jnp.concatenate(cy, axis=0), jnp.concatenate(sy, axis=0)
            cx, sx = few_cosine[blocks : blocks + 1], few_sine[blocks : blocks + 1]
            half_y, half_x, half_both = (
                few_cosine[n : n + 1] for n in range(blocks + 1, blocks + 4)
            )
            plus_real = cy * cx - sy * sx
            plus_imaginary = sy * cx + cy * sx
            minus_real = cy * cx + sy * sx
            minus_imaginary = sy * cx - cy * sx
            minus_real = jnp.where(l0, cy * half_x, jnp.where(r0, cx * half_y, minus_real))
            minus_imaginary = jnp.where(l0, sy * half_x, jnp.where(r0, sx * half_y, minus_imaginary))
            corner = l0 & r0
            turn = (plus_real, plus_imaginary, minus_real, minus_imaginary)
            ends = (1.0, half_x, half_y, half_both)
            for n in range(4):
                turns[t, g, n] = SCALE * jnp.where(corner, ends[n], 2.0 * turn[n])
    pick = chosen_ref[...]
    for axis, values in enumerate(blended):
        base = jnp.zeros(pick.shape, f32)
        for j in range(count):
            base = jnp.where(pick == j, values[j : j + 1, : pick.shape[1]], base)
        base_ref[axis] = base


def peak_kernel(
    inverse_ref,
    inverse_rows_ref,
    mask_ref,
    base_ref,
    turns,
    weights,
    left_rows_ref,
    own_low_ref,
    other_low_ref,
    *refs,
):
    out_ref, image, stacked, lower_ref, high_ref, low_ref = refs[-6:]
    supers = turns.shape[1]
    tails, spectra = refs[:supers], refs[supers : 2 * supers]
    per_row = supers * GROUP
    upper_bands = spectra[0].shape[0]
    bands = upper_bands + lower_ref.shape[0]

    def turn_band(i):
        for g in range(supers):
            lane = g * 2 * LANES
            if i < upper_bands:
                values = quads(spectra[g][i], 0)
            else:
                values = quads(lower_ref[i - upper_bands], g)
            parts = []
            for begin, end, first in ROW_PARTS:
                parts.append(
                    coefficients(
                        [x[begin:end] for x in values],
                        [turns[i % 2, g, n, begin:end] for n in range(4)],
                        first,
                    )
                )
            for n, (a, b) in enumerate(zip(*parts)):
                high, low = split(jnp.concatenate([a, b], axis=0))
                at = slice(i * P_SIZE + n // 2 * HALF, i * P_SIZE + (n // 2 + 1) * HALF)
                lanes = slice(lane + n % 2 * LANES, lane + (n % 2 + 1) * LANES)
                high_ref[at, lanes] = high
                low_ref[at, lanes] = low

    lower_image(own_low_ref, other_low_ref, image)
    for g in range(supers):
        stacked[:, :, : 2 * P_SIZE, g * 2 * LANES : (g + 1) * 2 * LANES] = tails[g][...]
    forward_columns(image, stacked, weights, P_SIZE // STRIDE)
    for i in range(upper_bands // 2):
        turn_band(i)
    forward_rows(stacked, left_rows_ref[...], upper_bands, lower_ref)
    for i in range(upper_bands // 2, bands):
        turn_band(i)
    for g in range(supers):
        at = slice(g * 2 * LANES, (g + 1) * 2 * LANES)
        high, low = split(inverse_columns(high_ref[:, at], low_ref[:, at], inverse_ref))
        high_ref[:, at] = high
        low_ref[:, at] = low
    sums = []
    for i in range(bands):
        rows = slice(i * P_SIZE, (i + 1) * P_SIZE)
        sums.append(column_sums(row_transform(inverse_rows_ref, high_ref[rows], low_ref[rows])))
    found = band_peaks(*(jnp.concatenate(parts, axis=0) for parts in zip(*sums)))
    shape = (per_row, 2 * per_row)
    columns = iota(shape, 1) - 2 * iota(shape, 0)
    mask = mask_ref[...].astype(f32).astype(bf16)
    masks = [
        lax.dot_general(
            (columns == n).astype(bf16),
            mask,
            (((1,), (1,)), ((), ())),
            preferred_element_type=f32,
        )
        for n in range(2)
    ]
    parity = remainder(iota((per_row, bands), 1) + lax.axis_index("gz"), 2)
    chosen = jnp.where(parity == 0, masks[0], masks[1])
    for axis in range(2):
        out_ref[axis, 0] = base_ref[axis] + chosen * found[axis]


def exchanged(value, axis, step):
    return lax.ppermute(value, axis, [(i, i ^ step) for i in range(lax.axis_size(axis))])


def from_next(value, axis):
    count = lax.axis_size(axis)
    got = []
    for odd in range(min(2, count - 1)):
        pairs = [(i, i + 1) for i in range(odd, count - 1, 2)]
        got.append(lax.ppermute(value, axis, pairs + [(j, i) for i, j in pairs]))
    if len(got) < 2:
        return got[0] if got else value
    return jnp.where(lax.axis_index(axis) % 2 == 0, got[0], got[1])


def swapped(value):
    return lax.ppermute(value, "gz", [(0, 1), (1, 0)])


VMEM = pl.BlockSpec(memory_space=pltpu.VMEM)
SMEM = pl.BlockSpec(memory_space=pltpu.SMEM)


def cost(microseconds):
    return pl.CostEstimate(
        flops=0, bytes_accessed=int(microseconds * 3.0e6), transcendentals=0
    )


def params(mebibytes):
    return pltpu.CompilerParams(vmem_limit_bytes=mebibytes * 2**20)


def local(sections, fine_offsets, coarse_offset, tissue_mask):
    own = sections[0]
    rows, width = own.shape
    bands = rows // STRIDE
    per_row = width // P_SIZE
    count = lax.axis_size("gx")
    assert rows == DOWN * P_SIZE and width == DOWN * P_SIZE
    assert count % GROUP == 0 and count & (count - 1) == 0
    wide = width
    supers = width // (2 * LANES)
    own_tile, own_edge, packed = pl.pallas_call(
        prepare_kernel,
        out_shape=(
            jax.ShapeDtypeStruct((rows, width), bf16),
            jax.ShapeDtypeStruct((P_SIZE, width), bf16),
            jax.ShapeDtypeStruct((HALF + rows // 2, LANES), bf16),
        ),
        in_specs=[VMEM],
        out_specs=(VMEM,) * 3,
        compiler_params=params(16),
        cost_estimate=cost(5.0),
    )(own)
    offsets = jnp.concatenate([fine_offsets, coarse_offset])
    tables = pl.pallas_call(
        tables_kernel,
        out_shape=(
            jax.ShapeDtypeStruct((2, 4 * LANES, 2 * LANES), bf16),
            jax.ShapeDtypeStruct((2, 4 * LANES, LANES), bf16),
            jax.ShapeDtypeStruct((2 * P_SIZE, 6 * STRIDE), bf16),
            jax.ShapeDtypeStruct((2, supers, 8, LANES), jnp.int32),
            jax.ShapeDtypeStruct((per_row, bands), jnp.int32),
            jax.ShapeDtypeStruct((P_SIZE, 2 * LANES), bf16),
            jax.ShapeDtypeStruct((6 * LANES, 2 * LANES), bf16),
            jax.ShapeDtypeStruct((P_SIZE, 2 * LANES), bf16),
        ),
        in_specs=[VMEM],
        out_specs=(VMEM,) * 8,
        compiler_params=params(16),
        cost_estimate=cost(0.1),
    )(offsets)
    weights, coarse_weights, left_rows, picks, chosen, forward_rows, inverse, inverse_rows = tables
    low_bands = P_SIZE // STRIDE
    other = swapped(own_tile)
    got_even = exchanged(packed, "gx", 1)
    got_odd = lax.ppermute(packed[HALF:], "gx", [(i + 1, i) for i in range(1, count - 1, 2)])
    got_right = got_even[HALF:]
    other_right = swapped(got_right)
    got_odd, other_right = lax.optimization_barrier((got_odd, other_right))
    even = lax.axis_index("gx") % 2 == 0
    corner = jnp.where(even, got_right[:P_SIZE], got_odd[:P_SIZE])
    own_low = from_next(jnp.concatenate([own_edge, corner], axis=1), "gy")
    other_odd = swapped(got_odd)
    tiles = jnp.concatenate([packed[:HALF], got_even[:HALF]], axis=0)
    step = 2
    while 2 * step < count:
        tiles = jnp.concatenate([tiles, exchanged(tiles, "gx", step)], axis=0)
        step *= 2
    last_tiles = exchanged(tiles, "gx", step)
    def upper(group, *operands):
        return pl.pallas_call(
            functools.partial(upper_kernel, group),
            out_shape=(
                jax.ShapeDtypeStruct((bands - low_bands, P_SIZE, 2 * LANES), f32),
                jax.ShapeDtypeStruct((2, 2, 2 * P_SIZE, 2 * LANES), bf16),
            ),
            in_specs=[VMEM] * (4 + len(operands)),
            out_specs=(VMEM,) * 2,
            scratch_shapes=[
                pltpu.VMEM((2, rows, 3 * LANES), bf16),
                pltpu.VMEM((2, 2, 2 * rows, 2 * LANES), bf16),
            ],
            compiler_params=params(32),
            cost_estimate=cost(0.1),
        )(weights, left_rows, own_tile, other, *operands)

    uppers = [upper(group) for group in range(supers - 1)]
    last_tiles, *uppers = lax.optimization_barrier((last_tiles, *uppers))
    tiles = jnp.concatenate([tiles, last_tiles], axis=0)
    other_tiles = swapped(tiles)
    uppers.append(upper(supers - 1, got_right, got_odd, other_right, other_odd))
    other_tiles, own_low, *uppers = lax.optimization_barrier((other_tiles, own_low, *uppers))
    turns, base = pl.pallas_call(
        turn_kernel,
        out_shape=(
            jax.ShapeDtypeStruct((2, supers, 4, HALF, LANES), f32),
            jax.ShapeDtypeStruct((2, per_row, bands), f32),
        ),
        in_specs=[VMEM] * 8,
        out_specs=(VMEM,) * 2,
        scratch_shapes=[pltpu.VMEM((count, 2, 2 * P_SIZE, LANES), f32)],
        compiler_params=params(32),
        cost_estimate=cost(0.1),
    )(
        forward_rows,
        inverse,
        inverse_rows,
        coarse_weights,
        picks,
        chosen,
        tiles,
        other_tiles,
    )
    other_low = swapped(own_low)
    flow = pl.pallas_call(
        peak_kernel,
        out_shape=jax.ShapeDtypeStruct((2, 1, per_row, bands), f32),
        in_specs=[VMEM] * (9 + 2 * supers),
        out_specs=VMEM,
        scratch_shapes=[
            pltpu.VMEM((2, P_SIZE, width + LANES), bf16),
            pltpu.VMEM((2, 2, 4 * P_SIZE, wide), bf16),
            pltpu.VMEM((low_bands, P_SIZE, wide), f32),
            pltpu.VMEM((bands * P_SIZE, wide), bf16),
            pltpu.VMEM((bands * P_SIZE, wide), bf16),
        ],
        compiler_params=params(40),
        cost_estimate=cost(0.1),
    )(
        inverse,
        inverse_rows,
        tissue_mask,
        base,
        turns,
        weights,
        left_rows,
        own_low,
        other_low,
        *(tail for _, tail in uppers),
        *(spectra for spectra, _ in uppers),
    )
    return jnp.swapaxes(flow, 2, 3)


def solution(mesh):
    placed = (P("gz", ("pairs", "gy"), "gx"), P("pairs"), P("pairs"), P(("pairs", "gy"), "gx"))
    return jax.shard_map(
        local,
        mesh=mesh,
        in_specs=placed,
        out_specs=P(None, "gz", ("pairs", "gy"), "gx"),
        check_vma=False,
    )
```

```python
import functools
import math

import jax
import jax.numpy as jnp
from jax import lax
from jax.experimental import pallas as pl
from jax.experimental.pallas import tpu as pltpu
from jax.sharding import PartitionSpec as P

P_SIZE = 64
HALF = P_SIZE // 2
STRIDE = 32
DOWN = 8
LANES = 128
GROUP = LANES // HALF
SHARPNESS = 12.0
SUBLANES = 8
SCALE = SHARPNESS / float(P_SIZE) ** 4 * math.log2(math.e)

f32 = jnp.float32
bf16 = jnp.bfloat16


def cosine_of_turns(turns):
    square = (turns * (2.0 * math.pi)) ** 2
    total = jnp.full_like(square, 1.0 / math.factorial(20))
    for n in range(9, -1, -1):
        total = total * square + (-1.0) ** n / math.factorial(2 * n)
    return total


def sine_of_turns(turns):
    angle = turns * (2.0 * math.pi)
    square = angle * angle
    total = jnp.full_like(square, -1.0 / math.factorial(19))
    for n in range(8, -1, -1):
        total = total * square + (-1.0) ** n / math.factorial(2 * n + 1)
    return total * angle


def nearest(turns):
    return turns - jnp.round(turns)


def basis_values(frequency, kind, place):
    nyquist = (kind == 1) & (frequency == 0)
    number = jnp.where(nyquist, HALF, frequency)
    quarter = jnp.where((kind == 1) & (frequency != 0), P_SIZE // 4, 0)
    step = (number * place - quarter) & (P_SIZE - 1)
    step = jnp.where(step > HALF, P_SIZE - step, step)
    flip = step > P_SIZE // 4
    step = jnp.where(flip, HALF - step, step)
    square = (step.astype(f32) * (2.0 * math.pi / P_SIZE)) ** 2
    total = jnp.full_like(square, 1.0 / math.factorial(12))
    for n in range(5, -1, -1):
        total = total * square + (-1.0) ** n / math.factorial(2 * n)
    return jnp.where(flip, -total, total)


def quotient(number, divisor):
    return number >> (divisor.bit_length() - 1)


def remainder(number, divisor):
    return number & (divisor - 1)


def iota(shape, axis):
    return lax.broadcasted_iota(jnp.int32, shape, axis)


def split(values):
    high = values.astype(bf16)
    return high, (values - high.astype(f32)).astype(bf16)


def matmul(left, right):
    return jnp.dot(left, right, preferred_element_type=f32)


def add_row_halves(values):
    half = values.shape[0] // 2
    return values[:half] + values[half:]


def first_lane(shape):
    return remainder(iota(shape, 1), HALF) == 0


def half_spectra(cc, cs, sc, ss, first):
    shape = cc.shape
    l0 = first_lane(shape)
    if not first:
        return (
            cc - jnp.where(l0, 0.0, ss),
            sc + jnp.where(l0, 0.0, cs),
            jnp.where(l0, cs, cc + ss),
            jnp.where(l0, ss, sc - cs),
        )
    r0 = iota(shape, 0) == 0
    either = l0 | r0
    return (
        cc - jnp.where(either, 0.0, ss),
        jnp.where(r0, 0.0, sc) + jnp.where(l0, 0.0, cs),
        jnp.where(l0, cs, jnp.where(r0, sc, cc + ss)),
        jnp.where(either, ss, sc - cs),
    )


def cross_spectra(own, other, sign, first):
    a = half_spectra(*own, first)
    b = half_spectra(*other, first)
    out = []
    for r, i in ((0, 1), (2, 3)):
        out.append(b[r] * a[r] + b[i] * a[i])
        out.append(sign * (b[r] * a[i] - b[i] * a[r]))
    if first:
        shape = own[0].shape
        corner = first_lane(shape) & (iota(shape, 0) == 0)
        out = [jnp.where(corner, x * y, o) for x, y, o in zip(own, other, out)]
    return out


def coefficients(g, t, first):
    gpr, gpi, gmr, gmi = g
    tpr, tpi, tmr, tmi = t
    shape = gpr.shape
    l0 = first_lane(shape)
    hpr = gpr * tpr - gpi * tpi
    hpi = gpr * tpi + gpi * tpr
    hmr = gmr * tmr - gmi * tmi
    hmi = gmr * tmi + gmi * tmr
    if not first:
        return (
            hpr + jnp.where(l0, 0.0, hmr),
            jnp.where(l0, hmr, hmi - hpi),
            -hpi - jnp.where(l0, 0.0, hmi),
            jnp.where(l0, -hmi, hmr - hpr),
        )
    r0 = iota(shape, 0) == 0
    either = l0 | r0
    corner = l0 & r0
    out = (
        hpr + jnp.where(either, 0.0, hmr),
        jnp.where(l0, hmr, jnp.where(r0, 0.0, hmi) - hpi),
        jnp.where(r0, hmr, -hpi - jnp.where(l0, 0.0, hmi)),
        jnp.where(either, -hmi, hmr - hpr),
    )
    return [jnp.where(corner, x * y, o) for x, y, o in zip(g, t, out)]


def signed(number):
    return jnp.where(number >= HALF, number - P_SIZE, number).astype(f32)


def column_sums(logits):
    largest = jnp.max(logits, axis=0, keepdims=True)
    weights = jnp.exp2(logits - largest)
    rows = signed(iota((P_SIZE, 1), 0))
    return largest, jnp.sum(weights, axis=0, keepdims=True), jnp.sum(weights * rows, axis=0, keepdims=True)


def band_peaks(largest, total, moment):
    bands, wide = largest.shape
    largest, total, moment = (
        jnp.transpose(x).reshape(wide // P_SIZE, P_SIZE, bands) for x in (largest, total, moment)
    )
    factor = jnp.exp2(largest - jnp.max(largest, axis=1, keepdims=True))
    weight = factor * total
    columns = signed(lax.broadcasted_iota(jnp.int32, (1, P_SIZE, 1), 1))
    bottom = jnp.sum(weight, axis=1)
    return jnp.sum(factor * moment, axis=1) / bottom, jnp.sum(weight * columns, axis=1) / bottom


ROW_PARTS = ((0, 8, True), (8, HALF, False))


def quads(block, group):
    lane = group * 2 * LANES
    top, bottom = block[:HALF], block[HALF:]
    return (
        top[:, lane : lane + LANES],
        top[:, lane + LANES : lane + 2 * LANES],
        bottom[:, lane : lane + LANES],
        bottom[:, lane + LANES : lane + 2 * LANES],
    )


def from_right(refs, rows):
    even = lax.axis_index("gx") % 2 == 0
    return jnp.where(even, refs[0][rows].astype(f32), refs[1][rows].astype(f32))


def unpack(packed):
    wide = packed.astype(f32)
    return jnp.concatenate([wide, pltpu.roll(wide, P_SIZE, axis=1)], axis=0).astype(bf16)


def prepare_kernel(tile_ref, out_ref, low_ref, packed_ref):
    rows, width = tile_ref.shape
    columns = width // DOWN
    pick = quotient(iota((width, LANES), 0), DOWN) == remainder(iota((width, LANES), 1), columns)
    pick = pick.astype(bf16)
    left = iota((columns // 2, LANES), 1) < P_SIZE
    sums = matmul(tile_ref[...], pick)
    coarse = jnp.sum(sums.reshape(rows // DOWN, DOWN, LANES), axis=1) / DOWN
    half = coarse.shape[0] // 2
    packed_ref[:half] = jnp.where(left, coarse[:half], coarse[half:]).astype(bf16)
    low_ref[...] = tile_ref[:P_SIZE]
    edge = tile_ref[:, :LANES].astype(f32)
    half_rows = rows // 2
    left = iota((half_rows, LANES), 1) < P_SIZE
    edge = jnp.where(left, edge[:half_rows], pltpu.roll(edge[half_rows:], P_SIZE, axis=1))
    packed_ref[half:] = edge.astype(bf16)
    out_ref[...] = tile_ref[...]


def beside(high, low):
    left = iota(high.shape, 1) < P_SIZE
    return jnp.concatenate([high, jnp.where(left, low, 0.0)], axis=1).astype(bf16)


def tables_kernel(
    offsets_in,
    weights_ref,
    coarse_weights_ref,
    rows_ref,
    picks_ref,
    chosen_ref,
    forward_rows_ref,
    inverse_ref,
    inverse_rows_ref,
):
    offsets = offsets_in[...].astype(f32).reshape(1, 3)
    row_offset, column_offset, coarse_offset = (
        jnp.max(offsets[:, n : n + 1]).astype(jnp.int32) for n in range(3)
    )
    count = lax.axis_size("gx")
    per_row, bands = chosen_ref.shape
    supers = per_row // GROUP
    side = lax.axis_index("gz")
    gx_place = lax.axis_index("gx")
    shape = (2 * P_SIZE, LANES)
    lane = iota(shape, 1)
    row = iota(shape, 0)
    values = jnp.where(
        quotient(row, P_SIZE) == quotient(remainder(lane, P_SIZE), HALF),
        basis_values(remainder(lane, HALF), quotient(lane, P_SIZE), remainder(row, P_SIZE)),
        0.0,
    )
    padded = jnp.concatenate([values, jnp.zeros((2 * P_SIZE, LANES), f32)], axis=0)
    shape = (P_SIZE, LANES)
    row = iota(shape, 0)
    lane = iota(shape, 1)
    basis = basis_values(remainder(row, HALF), quotient(row, HALF), remainder(lane, P_SIZE))
    high, low = (value.astype(f32) for value in split(basis))
    forward_rows_ref[...] = beside(high, low)
    wide_high = jnp.concatenate([high] * 2, axis=1)
    wide_low = jnp.concatenate([low] * 2, axis=1)
    for kind in range(2):
        rows = slice(kind * HALF, (kind + 1) * HALF)
        for patch in range(GROUP):
            mine = quotient(iota((HALF, GROUP * P_SIZE), 1), P_SIZE) == patch
            at = (kind * GROUP + patch) * HALF
            for part, value in enumerate((wide_high, wide_high, wide_low)):
                begin = at + part * 2 * LANES
                inverse_ref[begin : begin + HALF] = jnp.where(mine, value[rows], 0.0).astype(bf16)
    kind = quotient(remainder(lane, P_SIZE), HALF)
    high, low = split(basis_values(remainder(lane, HALF), kind, row))
    inverse_rows_ref[...] = beside(high.astype(f32), low.astype(f32))
    shifts = [column_offset + STRIDE * ((t + side) % 2) for t in range(2)] + [coarse_offset]
    for t, shift in enumerate(shifts):
        moved = pltpu.roll(padded, shift, axis=0)
        for part, value in enumerate(split(moved)):
            rows = slice(part * 2 * LANES, (part + 1) * 2 * LANES)
            turned = pltpu.roll(value.astype(f32), P_SIZE, axis=1).astype(bf16)
            for order, entry in enumerate((value, turned)):
                if t < 2:
                    weights_ref[order, rows, t * LANES : (t + 1) * LANES] = entry
                else:
                    coarse_weights_ref[order, rows] = entry
    shape = (P_SIZE, 6 * STRIDE)
    number = iota(shape, 0)
    lane = iota(shape, 1)
    place = quotient(lane, P_SIZE) * STRIDE + remainder(lane, STRIDE) - row_offset
    values = jnp.where(
        (place >= 0) & (place < P_SIZE),
        basis_values(remainder(number, HALF), quotient(number, HALF), place),
        0.0,
    )
    high, low = split(values)
    is_low = remainder(lane, P_SIZE) >= STRIDE
    rows_ref[:P_SIZE] = high
    rows_ref[P_SIZE:] = jnp.where(is_low, 0.0, low.astype(f32)).astype(bf16)
    def pick(column):
        centre = (gx_place * (2 * per_row) + column) * STRIDE + column_offset + P_SIZE // 2
        return jnp.clip(quotient(quotient(centre, DOWN) - coarse_offset, P_SIZE), 0, count - 1)

    lane_row = iota((1, LANES), 1)
    for t in range(2):
        for g in range(supers):
            column = 2 * (g * GROUP + quotient(lane_row, HALF)) + remainder(t + side, 2)
            picks_ref[t, g] = jnp.broadcast_to(pick(column), (8, LANES))
    shape = (per_row, bands)
    parity = remainder(iota(shape, 1) + side, 2)
    chosen_ref[...] = pick(2 * iota(shape, 0) + parity)


def column_transform(strips, weights):
    rows = strips[0].shape[0]
    out = []
    for order in range(2):
        part = [x[:, order * LANES : (order + 2) * LANES] for x in strips]
        left = jnp.concatenate([jnp.concatenate([x, x], axis=1) for x in part], axis=0)
        out.append(matmul(left, weights[order]))
    return [[x[n * rows : (n + 1) * rows] for x in out] for n in range(len(strips))]


def pair_up(a, b):
    left = iota(a.shape, 1) < P_SIZE
    return jnp.where(left, a, b), pltpu.roll(jnp.where(left, b, a), P_SIZE, axis=1)


def forward_columns(image, stacked, weights, unread, first_block=0):
    blocks = image.shape[1] // STRIDE
    supers = stacked.shape[3] // (2 * LANES)
    places = [(s, g) for s in range(2) for g in range(supers)]
    strips = [image[s, :, g * 2 * LANES : (2 * g + 3) * LANES] for s, g in places]
    for (s, g), (a, b) in zip(places, column_transform(strips, weights)):
        lane = g * 2 * LANES
        for t in range(2):
            half = slice(t * LANES, (t + 1) * LANES)
            for part, value in enumerate(pair_up(a[:, half], b[:, half])):
                high, low = split(value)
                at = slice(lane + part * LANES, lane + (part + 1) * LANES)
                for n in range(blocks):
                    if (t, n) == unread:
                        continue
                    block = slice(n * STRIDE, (n + 1) * STRIDE)
                    begin = 2 * (first_block + n) * STRIDE
                    stacked[s, t, begin : begin + STRIDE, at] = high[block]
                    stacked[s, t, begin + STRIDE : begin + 2 * STRIDE, at] = low[block]


def forward_rows(stacked, left_rows, first_band, out_ref):
    bands, _, wide = out_ref.shape
    supers = wide // (2 * LANES)
    sign = jnp.where(lax.axis_index("gz") == 0, 1.0, -1.0).astype(f32)
    for i in range(bands):
        spectra = []
        for s in range(2):
            window = stacked[s, (first_band + i) % 2, 2 * STRIDE * i : 2 * STRIDE * (i + 3), :]
            spectra.append(add_row_halves(matmul(left_rows, window)))
        for g in range(supers):
            lane = g * 2 * LANES
            own = quads(spectra[0], g)
            other = quads(spectra[1], g)
            for begin, end, first in ROW_PARTS:
                out = cross_spectra(
                    [x[begin:end] for x in own], [x[begin:end] for x in other], sign, first
                )
                out_ref[i, begin:end, lane : lane + LANES] = out[0]
                out_ref[i, begin:end, lane + LANES : lane + 2 * LANES] = out[1]
                out_ref[i, HALF + begin : HALF + end, lane : lane + LANES] = out[2]
                out_ref[i, HALF + begin : HALF + end, lane + LANES : lane + 2 * LANES] = out[3]


def is_last(axis):
    return lax.axis_index(axis) == lax.axis_size(axis) - 1


def upper_kernel(group, weights, left_rows_ref, own_ref, other_ref, *refs):
    rights, (out_ref, tail_ref, image, stacked) = refs[:-4], refs[-4:]
    lane = group * 2 * LANES
    wide = 2 * LANES if rights else 3 * LANES
    for s, main in enumerate((own_ref, other_ref)):
        image[s, :, :wide] = main[:, lane : lane + wide]
        if rights:
            image[s, :, wide:] = unpack(from_right(rights[2 * s : 2 * s + 2], slice(None)))
    if rights:

        @pl.when(is_last("gx"))
        def _():
            image[:, :, wide:] = jnp.zeros((2, image.shape[1], LANES), bf16)

    forward_columns(image, stacked, weights, (1, 0))
    tail_ref[...] = stacked[:, :, stacked.shape[2] - 2 * P_SIZE :]
    forward_rows(stacked, left_rows_ref[...], 0, out_ref)


def lower_image(own_low_ref, other_low_ref, image):
    shape = own_low_ref.shape
    inside = 1.0 - is_last("gx").astype(f32)
    above = 1.0 - is_last("gy").astype(f32)
    keep = jnp.where(iota(shape, 1) < shape[1] - LANES, above, above * inside)
    for s, low in enumerate((own_low_ref, other_low_ref)):
        image[s] = (low[...].astype(f32) * keep).astype(bf16)


def inverse_columns(high, low, table_ref):
    return matmul(jnp.concatenate([high, low, high], axis=1), table_ref[...])


def row_transform(table_ref, high, low):
    return matmul(table_ref[:, : 3 * P_SIZE], jnp.concatenate([high, low, high], axis=0))


def coarse_peaks(strip, forward_rows_ref, inverse_ref, inverse_rows_ref, weights, sign):
    supers = len(strip) * 2 // GROUP
    strip = strip + [jnp.zeros_like(strip[0])]
    columns = []
    for g in range(supers):
        (pair,) = column_transform([jnp.concatenate(strip[2 * g : 2 * g + 3], axis=1)], weights)
        columns += pair_up(*pair)
    strips = jnp.concatenate(columns, axis=1)
    spectra = []
    for s in range(2):
        spectra.append(
            row_transform(forward_rows_ref, *split(strips[s * P_SIZE : (s + 1) * P_SIZE]))
        )
    peaks = []
    for g in range(supers):
        own = quads(spectra[0], g)
        other = quads(spectra[1], g)
        parts = []
        for begin, end, first in ROW_PARTS:
            shape = (end - begin, LANES)
            values = cross_spectra([x[begin:end] for x in own], [x[begin:end] for x in other], sign, first)
            corner = first_lane(shape) & (iota(shape, 0) == 0) & first
            turn = [
                jnp.where(corner, SCALE, c).astype(f32)
                for c in (2.0 * SCALE, 0.0, 2.0 * SCALE, 0.0)
            ]
            parts.append(coefficients(values, turn, first))
        cc, cs, sc, ss = (jnp.concatenate([a, b], axis=0) for a, b in zip(*parts))
        block = jnp.concatenate(
            [jnp.concatenate([cc, cs], axis=1), jnp.concatenate([sc, ss], axis=1)], axis=0
        )
        found = inverse_columns(*split(block), inverse_ref)
        sums = column_sums(row_transform(inverse_rows_ref, *split(found)))
        wide = [jnp.broadcast_to(x, (LANES, GROUP * P_SIZE)) for x in sums]
        peaks.append(band_peaks(*wide))
    return [jnp.concatenate(parts, axis=0) for parts in zip(*peaks)]


def turn_kernel(
    forward_rows_ref,
    inverse_ref,
    inverse_rows_ref,
    weights,
    picks_ref,
    chosen_ref,
    own_part_ref,
    other_part_ref,
    turns,
    base_ref,
    ordered,
):
    count = ordered.shape[0]
    supers = turns.shape[1]
    side = lax.axis_index("gz")
    place = lax.axis_index("gx")
    sign = jnp.where(side == 0, 1.0, -1.0).astype(f32)
    for step in range(count):
        for part, ref in enumerate((own_part_ref, other_part_ref)):
            tile = ref[step * HALF : (step + 1) * HALF].astype(f32)
            turned = pltpu.roll(tile, P_SIZE, axis=1)
            rows = slice(part * P_SIZE, (part + 1) * P_SIZE)
            ordered[place ^ step, 0, rows] = jnp.concatenate([tile, turned], axis=0)
            ordered[place ^ step, 1, rows] = jnp.concatenate([turned, tile], axis=0)
    left = iota((2 * P_SIZE, LANES), 1) < P_SIZE
    strip = []
    for j in range(0, count, 2):
        strip.append(jnp.where(left, ordered[j, 0], ordered[j + 1, 1]).astype(bf16))
    peaks = coarse_peaks(
        strip, forward_rows_ref, inverse_ref, inverse_rows_ref, weights, sign
    )
    blended = [
        (0.5 * DOWN) * (peak + jnp.sum(peak, axis=0, keepdims=True) / count) for peak in peaks
    ]

    def prior(pick):
        choice = pick == iota((count, LANES), 0)
        return [
            jnp.sum(jnp.where(choice, values, 0.0), axis=0, keepdims=True) for values in blended
        ]

    shape = (HALF, LANES)
    l0 = first_lane(shape)
    r0 = iota(shape, 0) == 0
    row = iota((SUBLANES, LANES), 0)
    steps = row.astype(f32) * (1.0 / P_SIZE)
    frequency_x = remainder(iota((1, LANES), 1), HALF).astype(f32) * (1.0 / P_SIZE)
    blocks = HALF // SUBLANES
    for t in range(2):
        for g in range(supers):
            dy, dx = (
                value - P_SIZE * jnp.round(value * (1.0 / P_SIZE)) for value in prior(picks_ref[t, g, :1])
            )
            few = SUBLANES * steps * dy
            for n, value in enumerate((frequency_x * dx, 0.5 * dy, 0.5 * dx, 0.5 * (dy + dx))):
                few = jnp.where(row == blocks + n, value, few)
            few = nearest(few)
            near = nearest(steps * dy)
            few_cosine, few_sine = cosine_of_turns(few), sine_of_turns(few)
            cosine, sine = cosine_of_turns(near), sine_of_turns(near)
            cy, sy = [], []
            for n in range(blocks):
                c, s = few_cosine[n : n + 1], few_sine[n : n + 1]
                cy.append(cosine * c - sine * s)
                sy.append(sine * c + cosine * s)
            cy, sy = jnp.concatenate(cy, axis=0), jnp.concatenate(sy, axis=0)
            cx, sx = few_cosine[blocks : blocks + 1], few_sine[blocks : blocks + 1]
            half_y, half_x, half_both = (
                few_cosine[n : n + 1] for n in range(blocks + 1, blocks + 4)
            )
            plus_real = cy * cx - sy * sx
            plus_imaginary = sy * cx + cy * sx
            minus_real = cy * cx + sy * sx
            minus_imaginary = sy * cx - cy * sx
            minus_real = jnp.where(l0, cy * half_x, jnp.where(r0, cx * half_y, minus_real))
            minus_imaginary = jnp.where(l0, sy * half_x, jnp.where(r0, sx * half_y, minus_imaginary))
            corner = l0 & r0
            turn = (plus_real, plus_imaginary, minus_real, minus_imaginary)
            ends = (1.0, half_x, half_y, half_both)
            for n in range(4):
                turns[t, g, n] = SCALE * jnp.where(corner, ends[n], 2.0 * turn[n])
    pick = chosen_ref[...]
    for axis, values in enumerate(blended):
        base = jnp.zeros(pick.shape, f32)
        for j in range(count):
            base = jnp.where(pick == j, values[j : j + 1, : pick.shape[1]], base)
        base_ref[axis] = base


def peak_kernel(
    inverse_ref,
    inverse_rows_ref,
    mask_ref,
    base_ref,
    turns,
    weights,
    left_rows_ref,
    own_low_ref,
    other_low_ref,
    *refs,
):
    out_ref, image, stacked, lower_ref, high_ref, low_ref = refs[-6:]
    supers = turns.shape[1]
    tails, spectra = refs[:supers], refs[supers : 2 * supers]
    per_row = supers * GROUP
    upper_bands = spectra[0].shape[0]
    bands = upper_bands + lower_ref.shape[0]

    def turn_band(i):
        for g in range(supers):
            lane = g * 2 * LANES
            if i < upper_bands:
                values = quads(spectra[g][i], 0)
            else:
                values = quads(lower_ref[i - upper_bands], g)
            parts = []
            for begin, end, first in ROW_PARTS:
                parts.append(
                    coefficients(
                        [x[begin:end] for x in values],
                        [turns[i % 2, g, n, begin:end] for n in range(4)],
                        first,
                    )
                )
            for n, (a, b) in enumerate(zip(*parts)):
                high, low = split(jnp.concatenate([a, b], axis=0))
                at = slice(i * P_SIZE + n // 2 * HALF, i * P_SIZE + (n // 2 + 1) * HALF)
                lanes = slice(lane + n % 2 * LANES, lane + (n % 2 + 1) * LANES)
                high_ref[at, lanes] = high
                low_ref[at, lanes] = low

    lower_image(own_low_ref, other_low_ref, image)
    for g in range(supers):
        stacked[:, :, : 2 * P_SIZE, g * 2 * LANES : (g + 1) * 2 * LANES] = tails[g][...]
    forward_columns(image, stacked, weights, (0, P_SIZE // STRIDE - 1), P_SIZE // STRIDE)
    for i in range(upper_bands // 2):
        turn_band(i)
    forward_rows(stacked, left_rows_ref[...], upper_bands, lower_ref)
    for i in range(upper_bands // 2, bands):
        turn_band(i)
    for g in range(supers):
        at = slice(g * 2 * LANES, (g + 1) * 2 * LANES)
        high, low = split(inverse_columns(high_ref[:, at], low_ref[:, at], inverse_ref))
        high_ref[:, at] = high
        low_ref[:, at] = low
    sums = []
    for i in range(bands):
        rows = slice(i * P_SIZE, (i + 1) * P_SIZE)
        sums.append(column_sums(row_transform(inverse_rows_ref, high_ref[rows], low_ref[rows])))
    found = band_peaks(*(jnp.concatenate(parts, axis=0) for parts in zip(*sums)))
    shape = (per_row, 2 * per_row)
    columns = iota(shape, 1) - 2 * iota(shape, 0)
    mask = mask_ref[...].astype(f32).astype(bf16)
    masks = [
        lax.dot_general(
            (columns == n).astype(bf16),
            mask,
            (((1,), (1,)), ((), ())),
            preferred_element_type=f32,
        )
        for n in range(2)
    ]
    parity = remainder(iota((per_row, bands), 1) + lax.axis_index("gz"), 2)
    chosen = jnp.where(parity == 0, masks[0], masks[1])
    for axis in range(2):
        out_ref[axis, 0] = base_ref[axis] + chosen * found[axis]


def exchanged(value, axis, step):
    return lax.ppermute(value, axis, [(i, i ^ step) for i in range(lax.axis_size(axis))])


def from_next(value, axis):
    count = lax.axis_size(axis)
    got = []
    for odd in range(min(2, count - 1)):
        pairs = [(i, i + 1) for i in range(odd, count - 1, 2)]
        got.append(lax.ppermute(value, axis, pairs + [(j, i) for i, j in pairs]))
    if len(got) < 2:
        return got[0] if got else value
    return jnp.where(lax.axis_index(axis) % 2 == 0, got[0], got[1])


def swapped(value):
    return lax.ppermute(value, "gz", [(0, 1), (1, 0)])


VMEM = pl.BlockSpec(memory_space=pltpu.VMEM)
SMEM = pl.BlockSpec(memory_space=pltpu.SMEM)


def cost(microseconds):
    return pl.CostEstimate(
        flops=0, bytes_accessed=int(microseconds * 3.0e6), transcendentals=0
    )


def params(mebibytes):
    return pltpu.CompilerParams(vmem_limit_bytes=mebibytes * 2**20)


def local(sections, fine_offsets, coarse_offset, tissue_mask):
    own = sections[0]
    rows, width = own.shape
    bands = rows // STRIDE
    per_row = width // P_SIZE
    count = lax.axis_size("gx")
    assert rows == DOWN * P_SIZE and width == DOWN * P_SIZE
    assert count % GROUP == 0 and count & (count - 1) == 0
    wide = width
    supers = width // (2 * LANES)
    own_tile, own_edge, packed = pl.pallas_call(
        prepare_kernel,
        out_shape=(
            jax.ShapeDtypeStruct((rows, width), bf16),
            jax.ShapeDtypeStruct((P_SIZE, width), bf16),
            jax.ShapeDtypeStruct((HALF + rows // 2, LANES), bf16),
        ),
        in_specs=[VMEM],
        out_specs=(VMEM,) * 3,
        compiler_params=params(16),
        cost_estimate=cost(5.0),
    )(own)
    offsets = jnp.concatenate([fine_offsets, coarse_offset])
    tables = pl.pallas_call(
        tables_kernel,
        out_shape=(
            jax.ShapeDtypeStruct((2, 4 * LANES, 2 * LANES), bf16),
            jax.ShapeDtypeStruct((2, 4 * LANES, LANES), bf16),
            jax.ShapeDtypeStruct((2 * P_SIZE, 6 * STRIDE), bf16),
            jax.ShapeDtypeStruct((2, supers, 8, LANES), jnp.int32),
            jax.ShapeDtypeStruct((per_row, bands), jnp.int32),
            jax.ShapeDtypeStruct((P_SIZE, 2 * LANES), bf16),
            jax.ShapeDtypeStruct((6 * LANES, 2 * LANES), bf16),
            jax.ShapeDtypeStruct((P_SIZE, 2 * LANES), bf16),
        ),
        in_specs=[VMEM],
        out_specs=(VMEM,) * 8,
        compiler_params=params(16),
        cost_estimate=cost(0.1),
    )(offsets)
    weights, coarse_weights, left_rows, picks, chosen, forward_rows, inverse, inverse_rows = tables
    low_bands = P_SIZE // STRIDE
    other = swapped(own_tile)
    got_even = exchanged(packed, "gx", 1)
    got_odd = lax.ppermute(packed[HALF:], "gx", [(i + 1, i) for i in range(1, count - 1, 2)])
    got_right = got_even[HALF:]
    other_right = swapped(got_right)
    got_odd, other_right = lax.optimization_barrier((got_odd, other_right))
    even = lax.axis_index("gx") % 2 == 0
    corner = jnp.where(even, got_right[:P_SIZE], got_odd[:P_SIZE])
    own_low = from_next(jnp.concatenate([own_edge, corner], axis=1), "gy")
    other_odd = swapped(got_odd)
    tiles = jnp.concatenate([packed[:HALF], got_even[:HALF]], axis=0)
    step = 2
    while 2 * step < count:
        tiles = jnp.concatenate([tiles, exchanged(tiles, "gx", step)], axis=0)
        step *= 2
    last_tiles = exchanged(tiles, "gx", step)
    def upper(group, *operands):
        return pl.pallas_call(
            functools.partial(upper_kernel, group),
            out_shape=(
                jax.ShapeDtypeStruct((bands - low_bands, P_SIZE, 2 * LANES), f32),
                jax.ShapeDtypeStruct((2, 2, 2 * P_SIZE, 2 * LANES), bf16),
            ),
            in_specs=[VMEM] * (4 + len(operands)),
            out_specs=(VMEM,) * 2,
            scratch_shapes=[
                pltpu.VMEM((2, rows, 3 * LANES), bf16),
                pltpu.VMEM((2, 2, 2 * rows, 2 * LANES), bf16),
            ],
            compiler_params=params(32),
            cost_estimate=cost(0.1),
        )(weights, left_rows, own_tile, other, *operands)

    uppers = [upper(group) for group in range(supers - 1)]
    last_tiles, *uppers = lax.optimization_barrier((last_tiles, *uppers))
    tiles = jnp.concatenate([tiles, last_tiles], axis=0)
    other_tiles = swapped(tiles)
    uppers.append(upper(supers - 1, got_right, got_odd, other_right, other_odd))
    other_tiles, own_low, *uppers = lax.optimization_barrier((other_tiles, own_low, *uppers))
    turns, base = pl.pallas_call(
        turn_kernel,
        out_shape=(
            jax.ShapeDtypeStruct((2, supers, 4, HALF, LANES), f32),
            jax.ShapeDtypeStruct((2, per_row, bands), f32),
        ),
        in_specs=[VMEM] * 8,
        out_specs=(VMEM,) * 2,
        scratch_shapes=[pltpu.VMEM((count, 2, 2 * P_SIZE, LANES), f32)],
        compiler_params=params(32),
        cost_estimate=cost(0.1),
    )(
        forward_rows,
        inverse,
        inverse_rows,
        coarse_weights,
        picks,
        chosen,
        tiles,
        other_tiles,
    )
    other_low = swapped(own_low)
    flow = pl.pallas_call(
        peak_kernel,
        out_shape=jax.ShapeDtypeStruct((2, 1, per_row, bands), f32),
        in_specs=[VMEM] * (9 + 2 * supers),
        out_specs=VMEM,
        scratch_shapes=[
            pltpu.VMEM((2, P_SIZE, width + LANES), bf16),
            pltpu.VMEM((2, 2, 4 * P_SIZE, wide), bf16),
            pltpu.VMEM((low_bands, P_SIZE, wide), f32),
            pltpu.VMEM((bands * P_SIZE, wide), bf16),
            pltpu.VMEM((bands * P_SIZE, wide), bf16),
        ],
        compiler_params=params(40),
        cost_estimate=cost(0.1),
    )(
        inverse,
        inverse_rows,
        tissue_mask,
        base,
        turns,
        weights,
        left_rows,
        own_low,
        other_low,
        *(tail for _, tail in uppers),
        *(spectra for spectra, _ in uppers),
    )
    return jnp.swapaxes(flow, 2, 3)


def solution(mesh):
    placed = (P("gz", ("pairs", "gy"), "gx"), P("pairs"), P("pairs"), P(("pairs", "gy"), "gx"))
    return jax.shard_map(
        local,
        mesh=mesh,
        in_specs=placed,
        out_specs=P(None, "gz", ("pairs", "gy"), "gx"),
        check_vma=False,
    )
```

```python
import functools
import math

import jax
import jax.numpy as jnp
from jax import lax
from jax.experimental import pallas as pl
from jax.experimental.pallas import tpu as pltpu
from jax.sharding import PartitionSpec as P

P_SIZE = 64
HALF = P_SIZE // 2
STRIDE = 32
DOWN = 8
LANES = 128
GROUP = LANES // HALF
SHARPNESS = 12.0
SUBLANES = 8
SCALE = SHARPNESS / float(P_SIZE) ** 4 * math.log2(math.e)

f32 = jnp.float32
bf16 = jnp.bfloat16


def cosine_of_turns(turns):
    square = (turns * (2.0 * math.pi)) ** 2
    total = jnp.full_like(square, 1.0 / math.factorial(20))
    for n in range(9, -1, -1):
        total = total * square + (-1.0) ** n / math.factorial(2 * n)
    return total


def sine_of_turns(turns):
    angle = turns * (2.0 * math.pi)
    square = angle * angle
    total = jnp.full_like(square, -1.0 / math.factorial(19))
    for n in range(8, -1, -1):
        total = total * square + (-1.0) ** n / math.factorial(2 * n + 1)
    return total * angle


def nearest(turns):
    return turns - jnp.round(turns)


def basis_values(frequency, kind, place):
    nyquist = (kind == 1) & (frequency == 0)
    number = jnp.where(nyquist, HALF, frequency)
    quarter = jnp.where((kind == 1) & (frequency != 0), P_SIZE // 4, 0)
    step = (number * place - quarter) & (P_SIZE - 1)
    step = jnp.where(step > HALF, P_SIZE - step, step)
    flip = step > P_SIZE // 4
    step = jnp.where(flip, HALF - step, step)
    square = (step.astype(f32) * (2.0 * math.pi / P_SIZE)) ** 2
    total = jnp.full_like(square, 1.0 / math.factorial(12))
    for n in range(5, -1, -1):
        total = total * square + (-1.0) ** n / math.factorial(2 * n)
    return jnp.where(flip, -total, total)


def quotient(number, divisor):
    return number >> (divisor.bit_length() - 1)


def remainder(number, divisor):
    return number & (divisor - 1)


def iota(shape, axis):
    return lax.broadcasted_iota(jnp.int32, shape, axis)


def split(values):
    high = values.astype(bf16)
    return high, (values - high.astype(f32)).astype(bf16)


def matmul(left, right):
    return jnp.dot(left, right, preferred_element_type=f32)


def add_row_halves(values):
    half = values.shape[0] // 2
    return values[:half] + values[half:]


def first_lane(shape):
    return remainder(iota(shape, 1), HALF) == 0


def half_spectra(cc, cs, sc, ss, first):
    shape = cc.shape
    l0 = first_lane(shape)
    if not first:
        return (
            cc - jnp.where(l0, 0.0, ss),
            sc + jnp.where(l0, 0.0, cs),
            jnp.where(l0, cs, cc + ss),
            jnp.where(l0, ss, sc - cs),
        )
    r0 = iota(shape, 0) == 0
    either = l0 | r0
    return (
        cc - jnp.where(either, 0.0, ss),
        jnp.where(r0, 0.0, sc) + jnp.where(l0, 0.0, cs),
        jnp.where(l0, cs, jnp.where(r0, sc, cc + ss)),
        jnp.where(either, ss, sc - cs),
    )


def cross_spectra(own, other, sign, first):
    a = half_spectra(*own, first)
    b = half_spectra(*other, first)
    out = []
    for r, i in ((0, 1), (2, 3)):
        out.append(b[r] * a[r] + b[i] * a[i])
        out.append(sign * (b[r] * a[i] - b[i] * a[r]))
    if first:
        shape = own[0].shape
        corner = first_lane(shape) & (iota(shape, 0) == 0)
        out = [jnp.where(corner, x * y, o) for x, y, o in zip(own, other, out)]
    return out


def coefficients(g, t, first):
    gpr, gpi, gmr, gmi = g
    tpr, tpi, tmr, tmi = t
    shape = gpr.shape
    l0 = first_lane(shape)
    hpr = gpr * tpr - gpi * tpi
    hpi = gpr * tpi + gpi * tpr
    hmr = gmr * tmr - gmi * tmi
    hmi = gmr * tmi + gmi * tmr
    if not first:
        return (
            hpr + jnp.where(l0, 0.0, hmr),
            jnp.where(l0, hmr, hmi - hpi),
            -hpi - jnp.where(l0, 0.0, hmi),
            jnp.where(l0, -hmi, hmr - hpr),
        )
    r0 = iota(shape, 0) == 0
    either = l0 | r0
    corner = l0 & r0
    out = (
        hpr + jnp.where(either, 0.0, hmr),
        jnp.where(l0, hmr, jnp.where(r0, 0.0, hmi) - hpi),
        jnp.where(r0, hmr, -hpi - jnp.where(l0, 0.0, hmi)),
        jnp.where(either, -hmi, hmr - hpr),
    )
    return [jnp.where(corner, x * y, o) for x, y, o in zip(g, t, out)]


def signed(number):
    return jnp.where(number >= HALF, number - P_SIZE, number).astype(f32)


def column_sums(logits):
    largest = jnp.max(logits, axis=0, keepdims=True)
    weights = jnp.exp2(logits - largest)
    rows = signed(iota((P_SIZE, 1), 0))
    return largest, jnp.sum(weights, axis=0, keepdims=True), jnp.sum(weights * rows, axis=0, keepdims=True)


def band_peaks(largest, total, moment):
    bands, wide = largest.shape
    largest, total, moment = (
        jnp.transpose(x).reshape(wide // P_SIZE, P_SIZE, bands) for x in (largest, total, moment)
    )
    factor = jnp.exp2(largest - jnp.max(largest, axis=1, keepdims=True))
    weight = factor * total
    columns = signed(lax.broadcasted_iota(jnp.int32, (1, P_SIZE, 1), 1))
    bottom = jnp.sum(weight, axis=1)
    return jnp.sum(factor * moment, axis=1) / bottom, jnp.sum(weight * columns, axis=1) / bottom


ROW_PARTS = ((0, 8, True), (8, HALF, False))


def quads(block, group):
    lane = group * 2 * LANES
    top, bottom = block[:HALF], block[HALF:]
    return (
        top[:, lane : lane + LANES],
        top[:, lane + LANES : lane + 2 * LANES],
        bottom[:, lane : lane + LANES],
        bottom[:, lane + LANES : lane + 2 * LANES],
    )


def from_right(refs, rows):
    even = lax.axis_index("gx") % 2 == 0
    return jnp.where(even, refs[0][rows].astype(f32), refs[1][rows].astype(f32))


def unpack(packed):
    wide = packed.astype(f32)
    return jnp.concatenate([wide, pltpu.roll(wide, P_SIZE, axis=1)], axis=0).astype(bf16)


def prepare_kernel(tile_ref, out_ref, low_ref, packed_ref):
    rows, width = tile_ref.shape
    columns = width // DOWN
    pick = quotient(iota((width, LANES), 0), DOWN) == remainder(iota((width, LANES), 1), columns)
    pick = pick.astype(bf16)
    left = iota((columns // 2, LANES), 1) < P_SIZE
    sums = matmul(tile_ref[...], pick)
    coarse = jnp.sum(sums.reshape(rows // DOWN, DOWN, LANES), axis=1) / DOWN
    half = coarse.shape[0] // 2
    packed_ref[:half] = jnp.where(left, coarse[:half], coarse[half:]).astype(bf16)
    low_ref[...] = tile_ref[:P_SIZE]
    edge = tile_ref[:, :LANES].astype(f32)
    half_rows = rows // 2
    left = iota((half_rows, LANES), 1) < P_SIZE
    edge = jnp.where(left, edge[:half_rows], pltpu.roll(edge[half_rows:], P_SIZE, axis=1))
    packed_ref[half:] = edge.astype(bf16)
    out_ref[...] = tile_ref[...]


def beside(high, low):
    left = iota(high.shape, 1) < P_SIZE
    return jnp.concatenate([high, jnp.where(left, low, 0.0)], axis=1).astype(bf16)


def tables_kernel(
    offsets_in,
    weights_ref,
    coarse_weights_ref,
    rows_ref,
    picks_ref,
    chosen_ref,
    forward_rows_ref,
    inverse_ref,
    inverse_rows_ref,
):
    offsets = offsets_in[...].astype(f32).reshape(1, 3)
    row_offset, column_offset, coarse_offset = (
        jnp.max(offsets[:, n : n + 1]).astype(jnp.int32) for n in range(3)
    )
    count = lax.axis_size("gx")
    per_row, bands = chosen_ref.shape
    supers = per_row // GROUP
    side = lax.axis_index("gz")
    gx_place = lax.axis_index("gx")
    shape = (2 * P_SIZE, LANES)
    lane = iota(shape, 1)
    row = iota(shape, 0)
    values = jnp.where(
        quotient(row, P_SIZE) == quotient(remainder(lane, P_SIZE), HALF),
        basis_values(remainder(lane, HALF), quotient(lane, P_SIZE), remainder(row, P_SIZE)),
        0.0,
    )
    padded = jnp.concatenate([values, jnp.zeros((2 * P_SIZE, LANES), f32)], axis=0)
    shape = (P_SIZE, LANES)
    row = iota(shape, 0)
    lane = iota(shape, 1)
    basis = basis_values(remainder(row, HALF), quotient(row, HALF), remainder(lane, P_SIZE))
    high, low = (value.astype(f32) for value in split(basis))
    forward_rows_ref[...] = beside(high, low)
    wide_high = jnp.concatenate([high] * 2, axis=1)
    wide_low = jnp.concatenate([low] * 2, axis=1)
    for kind in range(2):
        rows = slice(kind * HALF, (kind + 1) * HALF)
        for patch in range(GROUP):
            mine = quotient(iota((HALF, GROUP * P_SIZE), 1), P_SIZE) == patch
            at = (kind * GROUP + patch) * HALF
            for part, value in enumerate((wide_high, wide_high, wide_low)):
                begin = at + part * 2 * LANES
                inverse_ref[begin : begin + HALF] = jnp.where(mine, value[rows], 0.0).astype(bf16)
    kind = quotient(remainder(lane, P_SIZE), HALF)
    high, low = split(basis_values(remainder(lane, HALF), kind, row))
    inverse_rows_ref[...] = beside(high.astype(f32), low.astype(f32))
    shifts = [column_offset + STRIDE * ((t + side) % 2) for t in range(2)] + [coarse_offset]
    for t, shift in enumerate(shifts):
        moved = pltpu.roll(padded, shift, axis=0)
        for part, value in enumerate(split(moved)):
            rows = slice(part * 2 * LANES, (part + 1) * 2 * LANES)
            turned = pltpu.roll(value.astype(f32), P_SIZE, axis=1).astype(bf16)
            for order, entry in enumerate((value, turned)):
                if t < 2:
                    weights_ref[order, rows, t * LANES : (t + 1) * LANES] = entry
                else:
                    coarse_weights_ref[order, rows] = entry
    shape = (P_SIZE, 6 * STRIDE)
    number = iota(shape, 0)
    lane = iota(shape, 1)
    place = quotient(lane, P_SIZE) * STRIDE + remainder(lane, STRIDE) - row_offset
    values = jnp.where(
        (place >= 0) & (place < P_SIZE),
        basis_values(remainder(number, HALF), quotient(number, HALF), place),
        0.0,
    )
    high, low = split(values)
    is_low = remainder(lane, P_SIZE) >= STRIDE
    rows_ref[:P_SIZE] = high
    rows_ref[P_SIZE:] = jnp.where(is_low, 0.0, low.astype(f32)).astype(bf16)
    def pick(column):
        centre = (gx_place * (2 * per_row) + column) * STRIDE + column_offset + P_SIZE // 2
        return jnp.clip(quotient(quotient(centre, DOWN) - coarse_offset, P_SIZE), 0, count - 1)

    lane_row = iota((1, LANES), 1)
    for t in range(2):
        for g in range(supers):
            column = 2 * (g * GROUP + quotient(lane_row, HALF)) + remainder(t + side, 2)
            picks_ref[t, g] = jnp.broadcast_to(pick(column), (8, LANES))
    shape = (per_row, bands)
    parity = remainder(iota(shape, 1) + side, 2)
    chosen_ref[...] = pick(2 * iota(shape, 0) + parity)


def column_transform(strips, weights):
    rows = strips[0].shape[0]
    out = []
    for order in range(2):
        part = [x[:, order * LANES : (order + 2) * LANES] for x in strips]
        left = jnp.concatenate([jnp.concatenate([x, x], axis=1) for x in part], axis=0)
        out.append(matmul(left, weights[order]))
    return [[x[n * rows : (n + 1) * rows] for x in out] for n in range(len(strips))]


def pair_up(a, b):
    left = iota(a.shape, 1) < P_SIZE
    return jnp.where(left, a, b), pltpu.roll(jnp.where(left, b, a), P_SIZE, axis=1)


def forward_columns(strips, stacked, weights, first_block=0):
    blocks = strips[0].shape[0] // STRIDE
    supers = stacked.shape[3] // (2 * LANES)
    places = [(s, g) for s in range(2) for g in range(supers)]
    for (s, g), (a, b) in zip(places, column_transform(strips, weights)):
        lane = g * 2 * LANES
        for t in range(2):
            half = slice(t * LANES, (t + 1) * LANES)
            for part, value in enumerate(pair_up(a[:, half], b[:, half])):
                high, low = split(value)
                at = slice(lane + part * LANES, lane + (part + 1) * LANES)
                for n in range(blocks):
                    block = slice(n * STRIDE, (n + 1) * STRIDE)
                    begin = 2 * (first_block + n) * STRIDE
                    stacked[s, t, begin : begin + STRIDE, at] = high[block]
                    stacked[s, t, begin + STRIDE : begin + 2 * STRIDE, at] = low[block]


def forward_rows(stacked, left_rows, first_band, out_ref):
    bands, _, wide = out_ref.shape
    supers = wide // (2 * LANES)
    sign = jnp.where(lax.axis_index("gz") == 0, 1.0, -1.0).astype(f32)
    for i in range(bands):
        spectra = []
        for s in range(2):
            window = stacked[s, (first_band + i) % 2, 2 * STRIDE * i : 2 * STRIDE * (i + 3), :]
            spectra.append(add_row_halves(matmul(left_rows, window)))
        for g in range(supers):
            lane = g * 2 * LANES
            own = quads(spectra[0], g)
            other = quads(spectra[1], g)
            for begin, end, first in ROW_PARTS:
                out = cross_spectra(
                    [x[begin:end] for x in own], [x[begin:end] for x in other], sign, first
                )
                out_ref[i, begin:end, lane : lane + LANES] = out[0]
                out_ref[i, begin:end, lane + LANES : lane + 2 * LANES] = out[1]
                out_ref[i, HALF + begin : HALF + end, lane : lane + LANES] = out[2]
                out_ref[i, HALF + begin : HALF + end, lane + LANES : lane + 2 * LANES] = out[3]


def is_last(axis):
    return lax.axis_index(axis) == lax.axis_size(axis) - 1


def upper_kernel(group, weights, left_rows_ref, own_ref, other_ref, *refs):
    rights, (out_ref, tail_ref, stacked) = refs[:-3], refs[-3:]
    lane = group * 2 * LANES
    wide = 2 * LANES if rights else 3 * LANES
    inside = 1.0 - is_last("gx").astype(f32)
    strips = []
    for s, main in enumerate((own_ref, other_ref)):
        strip = main[:, lane : lane + wide]
        if rights:
            halo = unpack(from_right(rights[2 * s : 2 * s + 2], slice(None)) * inside)
            strip = jnp.concatenate([strip, halo], axis=1)
        strips.append(strip)
    forward_columns(strips, stacked, weights)
    tail_ref[...] = stacked[:, :, stacked.shape[2] - 2 * P_SIZE :]
    forward_rows(stacked, left_rows_ref[...], 0, out_ref)


def lower_strips(own_low_ref, other_low_ref, supers):
    shape = own_low_ref.shape
    inside = 1.0 - is_last("gx").astype(f32)
    above = 1.0 - is_last("gy").astype(f32)
    keep = jnp.where(iota(shape, 1) < shape[1] - LANES, above, above * inside)
    rows = [(low[...].astype(f32) * keep).astype(bf16) for low in (own_low_ref, other_low_ref)]
    return [x[:, g * 2 * LANES : (2 * g + 3) * LANES] for x in rows for g in range(supers)]


def inverse_columns(high, low, table_ref):
    return matmul(jnp.concatenate([high, low, high], axis=1), table_ref[...])


def row_transform(table_ref, high, low):
    return matmul(table_ref[:, : 3 * P_SIZE], jnp.concatenate([high, low, high], axis=0))


def coarse_peaks(strip, forward_rows_ref, inverse_ref, inverse_rows_ref, weights, sign):
    supers = len(strip) * 2 // GROUP
    strip = strip + [jnp.zeros_like(strip[0])]
    columns = []
    for g in range(supers):
        (pair,) = column_transform([jnp.concatenate(strip[2 * g : 2 * g + 3], axis=1)], weights)
        columns += pair_up(*pair)
    strips = jnp.concatenate(columns, axis=1)
    spectra = []
    for s in range(2):
        spectra.append(
            row_transform(forward_rows_ref, *split(strips[s * P_SIZE : (s + 1) * P_SIZE]))
        )
    peaks = []
    for g in range(supers):
        own = quads(spectra[0], g)
        other = quads(spectra[1], g)
        parts = []
        for begin, end, first in ROW_PARTS:
            shape = (end - begin, LANES)
            values = cross_spectra([x[begin:end] for x in own], [x[begin:end] for x in other], sign, first)
            corner = first_lane(shape) & (iota(shape, 0) == 0) & first
            turn = [
                jnp.where(corner, SCALE, c).astype(f32)
                for c in (2.0 * SCALE, 0.0, 2.0 * SCALE, 0.0)
            ]
            parts.append(coefficients(values, turn, first))
        cc, cs, sc, ss = (jnp.concatenate([a, b], axis=0) for a, b in zip(*parts))
        block = jnp.concatenate(
            [jnp.concatenate([cc, cs], axis=1), jnp.concatenate([sc, ss], axis=1)], axis=0
        )
        found = inverse_columns(*split(block), inverse_ref)
        sums = column_sums(row_transform(inverse_rows_ref, *split(found)))
        wide = [jnp.broadcast_to(x, (LANES, GROUP * P_SIZE)) for x in sums]
        peaks.append(band_peaks(*wide))
    return [jnp.concatenate(parts, axis=0) for parts in zip(*peaks)]


def turn_kernel(
    forward_rows_ref,
    inverse_ref,
    inverse_rows_ref,
    weights,
    picks_ref,
    chosen_ref,
    own_part_ref,
    other_part_ref,
    turns,
    base_ref,
    ordered,
):
    count = ordered.shape[0]
    supers = turns.shape[1]
    side = lax.axis_index("gz")
    place = lax.axis_index("gx")
    sign = jnp.where(side == 0, 1.0, -1.0).astype(f32)
    for step in range(count):
        for part, ref in enumerate((own_part_ref, other_part_ref)):
            tile = ref[step * HALF : (step + 1) * HALF].astype(f32)
            turned = pltpu.roll(tile, P_SIZE, axis=1)
            rows = slice(part * P_SIZE, (part + 1) * P_SIZE)
            ordered[place ^ step, 0, rows] = jnp.concatenate([tile, turned], axis=0)
            ordered[place ^ step, 1, rows] = jnp.concatenate([turned, tile], axis=0)
    left = iota((2 * P_SIZE, LANES), 1) < P_SIZE
    strip = []
    for j in range(0, count, 2):
        strip.append(jnp.where(left, ordered[j, 0], ordered[j + 1, 1]).astype(bf16))
    peaks = coarse_peaks(
        strip, forward_rows_ref, inverse_ref, inverse_rows_ref, weights, sign
    )
    blended = [
        (0.5 * DOWN) * (peak + jnp.sum(peak, axis=0, keepdims=True) / count) for peak in peaks
    ]

    def prior(pick):
        choice = pick == iota((count, LANES), 0)
        return [
            jnp.sum(jnp.where(choice, values, 0.0), axis=0, keepdims=True) for values in blended
        ]

    shape = (HALF, LANES)
    l0 = first_lane(shape)
    r0 = iota(shape, 0) == 0
    row = iota((SUBLANES, LANES), 0)
    steps = row.astype(f32) * (1.0 / P_SIZE)
    frequency_x = remainder(iota((1, LANES), 1), HALF).astype(f32) * (1.0 / P_SIZE)
    blocks = HALF // SUBLANES
    for t in range(2):
        for g in range(supers):
            dy, dx = (
                value - P_SIZE * jnp.round(value * (1.0 / P_SIZE)) for value in prior(picks_ref[t, g, :1])
            )
            few = SUBLANES * steps * dy
            for n, value in enumerate((frequency_x * dx, 0.5 * dy, 0.5 * dx, 0.5 * (dy + dx))):
                few = jnp.where(row == blocks + n, value, few)
            few = nearest(few)
            near = nearest(steps * dy)
            few_cosine, few_sine = cosine_of_turns(few), sine_of_turns(few)
            cosine, sine = cosine_of_turns(near), sine_of_turns(near)
            cy, sy = [], []
            for n in range(blocks):
                c, s = few_cosine[n : n + 1], few_sine[n : n + 1]
                cy.append(cosine * c - sine * s)
                sy.append(sine * c + cosine * s)
            cy, sy = jnp.concatenate(cy, axis=0), jnp.concatenate(sy, axis=0)
            cx, sx = few_cosine[blocks : blocks + 1], few_sine[blocks : blocks + 1]
            half_y, half_x, half_both = (
                few_cosine[n : n + 1] for n in range(blocks + 1, blocks + 4)
            )
            plus_real = cy * cx - sy * sx
            plus_imaginary = sy * cx + cy * sx
            minus_real = cy * cx + sy * sx
            minus_imaginary = sy * cx - cy * sx
            minus_real = jnp.where(l0, cy * half_x, jnp.where(r0, cx * half_y, minus_real))
            minus_imaginary = jnp.where(l0, sy * half_x, jnp.where(r0, sx * half_y, minus_imaginary))
            corner = l0 & r0
            turn = (plus_real, plus_imaginary, minus_real, minus_imaginary)
            ends = (1.0, half_x, half_y, half_both)
            for n in range(4):
                turns[t, g, n] = SCALE * jnp.where(corner, ends[n], 2.0 * turn[n])
    pick = chosen_ref[...]
    for axis, values in enumerate(blended):
        base = jnp.zeros(pick.shape, f32)
        for j in range(count):
            base = jnp.where(pick == j, values[j : j + 1, : pick.shape[1]], base)
        base_ref[axis] = base


def peak_kernel(
    inverse_ref,
    inverse_rows_ref,
    mask_ref,
    base_ref,
    turns,
    weights,
    left_rows_ref,
    own_low_ref,
    other_low_ref,
    *refs,
):
    out_ref, stacked, lower_ref, high_ref, low_ref = refs[-5:]
    supers = turns.shape[1]
    tails, spectra = refs[:supers], refs[supers : 2 * supers]
    per_row = supers * GROUP
    upper_bands = spectra[0].shape[0]
    bands = upper_bands + lower_ref.shape[0]

    def turn_band(i):
        for g in range(supers):
            lane = g * 2 * LANES
            if i < upper_bands:
                values = quads(spectra[g][i], 0)
            else:
                values = quads(lower_ref[i - upper_bands], g)
            parts = []
            for begin, end, first in ROW_PARTS:
                parts.append(
                    coefficients(
                        [x[begin:end] for x in values],
                        [turns[i % 2, g, n, begin:end] for n in range(4)],
                        first,
                    )
                )
            for n, (a, b) in enumerate(zip(*parts)):
                high, low = split(jnp.concatenate([a, b], axis=0))
                at = slice(i * P_SIZE + n // 2 * HALF, i * P_SIZE + (n // 2 + 1) * HALF)
                lanes = slice(lane + n % 2 * LANES, lane + (n % 2 + 1) * LANES)
                high_ref[at, lanes] = high
                low_ref[at, lanes] = low

    strips = lower_strips(own_low_ref, other_low_ref, supers)
    for g in range(supers):
        stacked[:, :, : 2 * P_SIZE, g * 2 * LANES : (g + 1) * 2 * LANES] = tails[g][...]
    forward_columns(strips, stacked, weights, P_SIZE // STRIDE)
    for i in range(upper_bands // 2):
        turn_band(i)
    forward_rows(stacked, left_rows_ref[...], upper_bands, lower_ref)
    for i in range(upper_bands // 2, bands):
        turn_band(i)
    for g in range(supers):
        at = slice(g * 2 * LANES, (g + 1) * 2 * LANES)
        high, low = split(inverse_columns(high_ref[:, at], low_ref[:, at], inverse_ref))
        high_ref[:, at] = high
        low_ref[:, at] = low
    sums = []
    for i in range(bands):
        rows = slice(i * P_SIZE, (i + 1) * P_SIZE)
        sums.append(column_sums(row_transform(inverse_rows_ref, high_ref[rows], low_ref[rows])))
    found = band_peaks(*(jnp.concatenate(parts, axis=0) for parts in zip(*sums)))
    shape = (per_row, 2 * per_row)
    columns = iota(shape, 1) - 2 * iota(shape, 0)
    mask = mask_ref[...].astype(f32).astype(bf16)
    masks = [
        lax.dot_general(
            (columns == n).astype(bf16),
            mask,
            (((1,), (1,)), ((), ())),
            preferred_element_type=f32,
        )
        for n in range(2)
    ]
    parity = remainder(iota((per_row, bands), 1) + lax.axis_index("gz"), 2)
    chosen = jnp.where(parity == 0, masks[0], masks[1])
    for axis in range(2):
        out_ref[axis, 0] = base_ref[axis] + chosen * found[axis]


def exchanged(value, axis, step):
    return lax.ppermute(value, axis, [(i, i ^ step) for i in range(lax.axis_size(axis))])


def from_next(value, axis):
    count = lax.axis_size(axis)
    got = []
    for odd in range(min(2, count - 1)):
        pairs = [(i, i + 1) for i in range(odd, count - 1, 2)]
        got.append(lax.ppermute(value, axis, pairs + [(j, i) for i, j in pairs]))
    if len(got) < 2:
        return got[0] if got else value
    return jnp.where(lax.axis_index(axis) % 2 == 0, got[0], got[1])


def swapped(value):
    return lax.ppermute(value, "gz", [(0, 1), (1, 0)])


VMEM = pl.BlockSpec(memory_space=pltpu.VMEM)
SMEM = pl.BlockSpec(memory_space=pltpu.SMEM)


def cost(microseconds):
    return pl.CostEstimate(
        flops=0, bytes_accessed=int(microseconds * 3.0e6), transcendentals=0
    )


def params(mebibytes):
    return pltpu.CompilerParams(vmem_limit_bytes=mebibytes * 2**20)


def local(sections, fine_offsets, coarse_offset, tissue_mask):
    own = sections[0]
    rows, width = own.shape
    bands = rows // STRIDE
    per_row = width // P_SIZE
    count = lax.axis_size("gx")
    assert rows == DOWN * P_SIZE and width == DOWN * P_SIZE
    assert count % GROUP == 0 and count & (count - 1) == 0
    wide = width
    supers = width // (2 * LANES)
    own_tile, own_edge, packed = pl.pallas_call(
        prepare_kernel,
        out_shape=(
            jax.ShapeDtypeStruct((rows, width), bf16),
            jax.ShapeDtypeStruct((P_SIZE, width), bf16),
            jax.ShapeDtypeStruct((HALF + rows // 2, LANES), bf16),
        ),
        in_specs=[VMEM],
        out_specs=(VMEM,) * 3,
        compiler_params=params(16),
        cost_estimate=cost(5.0),
    )(own)
    offsets = jnp.concatenate([fine_offsets, coarse_offset])
    tables = pl.pallas_call(
        tables_kernel,
        out_shape=(
            jax.ShapeDtypeStruct((2, 4 * LANES, 2 * LANES), bf16),
            jax.ShapeDtypeStruct((2, 4 * LANES, LANES), bf16),
            jax.ShapeDtypeStruct((2 * P_SIZE, 6 * STRIDE), bf16),
            jax.ShapeDtypeStruct((2, supers, 8, LANES), jnp.int32),
            jax.ShapeDtypeStruct((per_row, bands), jnp.int32),
            jax.ShapeDtypeStruct((P_SIZE, 2 * LANES), bf16),
            jax.ShapeDtypeStruct((6 * LANES, 2 * LANES), bf16),
            jax.ShapeDtypeStruct((P_SIZE, 2 * LANES), bf16),
        ),
        in_specs=[VMEM],
        out_specs=(VMEM,) * 8,
        compiler_params=params(16),
        cost_estimate=cost(0.1),
    )(offsets)
    weights, coarse_weights, left_rows, picks, chosen, forward_rows, inverse, inverse_rows = tables
    low_bands = P_SIZE // STRIDE
    other = swapped(own_tile)
    got_even = exchanged(packed, "gx", 1)
    got_odd = lax.ppermute(packed[HALF:], "gx", [(i + 1, i) for i in range(1, count - 1, 2)])
    got_right = got_even[HALF:]
    other_right = swapped(got_right)
    got_odd, other_right = lax.optimization_barrier((got_odd, other_right))
    even = lax.axis_index("gx") % 2 == 0
    corner = jnp.where(even, got_right[:P_SIZE], got_odd[:P_SIZE])
    own_low = from_next(jnp.concatenate([own_edge, corner], axis=1), "gy")
    other_odd = swapped(got_odd)
    tiles = jnp.concatenate([packed[:HALF], got_even[:HALF]], axis=0)
    step = 2
    while 2 * step < count:
        tiles = jnp.concatenate([tiles, exchanged(tiles, "gx", step)], axis=0)
        step *= 2
    last_tiles = exchanged(tiles, "gx", step)
    def upper(group, *operands):
        return pl.pallas_call(
            functools.partial(upper_kernel, group),
            out_shape=(
                jax.ShapeDtypeStruct((bands - low_bands, P_SIZE, 2 * LANES), f32),
                jax.ShapeDtypeStruct((2, 2, 2 * P_SIZE, 2 * LANES), bf16),
            ),
            in_specs=[VMEM] * (4 + len(operands)),
            out_specs=(VMEM,) * 2,
            scratch_shapes=[
                pltpu.VMEM((2, 2, 2 * rows, 2 * LANES), bf16),
            ],
            compiler_params=params(32),
            cost_estimate=cost(0.1),
        )(weights, left_rows, own_tile, other, *operands)

    uppers = [upper(group) for group in range(supers - 1)]
    last_tiles, *uppers = lax.optimization_barrier((last_tiles, *uppers))
    tiles = jnp.concatenate([tiles, last_tiles], axis=0)
    other_tiles = swapped(tiles)
    uppers.append(upper(supers - 1, got_right, got_odd, other_right, other_odd))
    other_tiles, own_low, *uppers = lax.optimization_barrier((other_tiles, own_low, *uppers))
    turns, base = pl.pallas_call(
        turn_kernel,
        out_shape=(
            jax.ShapeDtypeStruct((2, supers, 4, HALF, LANES), f32),
            jax.ShapeDtypeStruct((2, per_row, bands), f32),
        ),
        in_specs=[VMEM] * 8,
        out_specs=(VMEM,) * 2,
        scratch_shapes=[pltpu.VMEM((count, 2, 2 * P_SIZE, LANES), f32)],
        compiler_params=params(32),
        cost_estimate=cost(0.1),
    )(
        forward_rows,
        inverse,
        inverse_rows,
        coarse_weights,
        picks,
        chosen,
        tiles,
        other_tiles,
    )
    other_low = swapped(own_low)
    flow = pl.pallas_call(
        peak_kernel,
        out_shape=jax.ShapeDtypeStruct((2, 1, per_row, bands), f32),
        in_specs=[VMEM] * (9 + 2 * supers),
        out_specs=VMEM,
        scratch_shapes=[
            pltpu.VMEM((2, 2, 4 * P_SIZE, wide), bf16),
            pltpu.VMEM((low_bands, P_SIZE, wide), f32),
            pltpu.VMEM((bands * P_SIZE, wide), bf16),
            pltpu.VMEM((bands * P_SIZE, wide), bf16),
        ],
        compiler_params=params(40),
        cost_estimate=cost(0.1),
    )(
        inverse,
        inverse_rows,
        tissue_mask,
        base,
        turns,
        weights,
        left_rows,
        own_low,
        other_low,
        *(tail for _, tail in uppers),
        *(spectra for spectra, _ in uppers),
    )
    return jnp.swapaxes(flow, 2, 3)


def solution(mesh):
    placed = (P("gz", ("pairs", "gy"), "gx"), P("pairs"), P("pairs"), P(("pairs", "gy"), "gx"))
    return jax.shard_map(
        local,
        mesh=mesh,
        in_specs=placed,
        out_specs=P(None, "gz", ("pairs", "gy"), "gx"),
        check_vma=False,
    )
```
